128 devices in a mesh: gx: 8 (over x_lo, y), gy: 16 (over z, x_hi, core).
Axes of the slice: x: 4 (x_hi: 2, x_lo: 2; x = x_hi * 2 + x_lo), y: 4, z: 4, core: 2. Of those that a mesh axis runs over, the one named last changes fastest.
Arguments:
- log_dens: float32 [8, 256, 32768], P(None, 'gx', 'gy'), may hold values from -5 to 5
- theta: float32 [8], replicated, may hold values from -4 to 4
- cotangent: float32 [256, 32768], P('gx', 'gy'), may hold values from -6 to 6
Outputs:
- barycenter: float32 [256, 32768], P('gx', 'gy')
- grad_dens: float32 [8, 256, 32768], P(None, 'gx', 'gy')
- grad_theta: float32 [8], replicated
The draws below stay inside these ranges and needn't reach their ends.
All inputs are finite; a program needn't handle non-finite values.
Results may differ from the reference program's by a relative error of at most 0.0003.
Values sent between devices are 32-bit elements; how exact they have to be, the bound alone decides.
No kernel may reach another device: no remote copies, remote signals or barrier semaphores. Data moves between devices by JAX's collectives and lax.ppermute only.
A program may use at most 192 MiB of HBM per device.

```python
import math
import jax
import jax.numpy as jnp
from jax import lax

DENSITIES = 8
ITERS = 2
NZ = 64
NX = 256
NY = 512


def draw_log_dens(key, part):
    key = jax.random.fold_in(key, 7)
    ramp = math.log(3.0) * jnp.arange(NX, dtype=jnp.float32) / NX
    rough = 0.7 * jax.random.normal(key, (DENSITIES, NX, NY * NZ), jnp.float32)
    return jnp.clip(rough + ramp[None, :, None], -5.0, 5.0)


def block_scale(stream_key, extent, pieces, least, largest):
    def one(dim, shards_of):
        heights = jax.random.uniform(jax.random.fold_in(jax.random.fold_in(stream_key, 6), dim), (shards_of,), jnp.float32, least / len(pieces), largest / len(pieces))
        return jnp.repeat(jnp.exp(heights), extent[dim] // shards_of).reshape((-1,) + (1,) * (len(extent) - dim - 1))

    factor_of = one(*pieces[0])
    for cut in pieces[1:]:
        factor_of = factor_of * one(*cut)
    return factor_of


def normal_values(rng, extent, scale, bound, split=(), held_as=jnp.bfloat16):
    values = scale * jax.random.normal(rng, extent, jnp.float32)
    if split:
        values = values * block_scale(rng, extent, split, -0.22, 0.18)
    return jnp.clip(values, -bound, bound).astype(held_as)


def setup_inputs(seed: int = 0) -> dict:
    seeds = jax.random.split(jax.random.key(seed), 4)
    return {
        "log_dens": draw_log_dens(jax.random.fold_in(seeds[3], 71), 0),
        "theta": normal_values(seeds[1], (DENSITIES,), 1.0, 4.0, (), jnp.float32),
        "cotangent": normal_values(seeds[2], (NX, NY * NZ), 1.0, 6.0, ((0, 8), (1, 16)), jnp.float32),
    }


def tap_list():
    raw_taps = [math.exp(-(offset * offset) / 8.0) for offset in range(-4, 5)]
    tap_total = 0.0
    for value in raw_taps:
        tap_total = tap_total + value
    return [value / tap_total for value in raw_taps]


def band_matrix(depth):
    row_index = jnp.arange(depth, dtype=jnp.int32)[:, None]
    col_index = jnp.arange(depth, dtype=jnp.int32)[None, :]
    offsets = row_index - col_index
    result = jnp.zeros((depth, depth), jnp.float32)
    for position, weight in enumerate(tap_list()):
        result = result + weight * (offsets == position - 4).astype(jnp.float32)
    return result


def smooth_field(values, matrix):
    taps = tap_list()
    width_x = values.shape[1]
    width_y = values.shape[2]
    padded = jnp.pad(values, ((0, 0), (4, 4), (0, 0), (0, 0)))
    along_x = taps[0] * padded[:, 0:width_x]
    for position in range(1, 9):
        along_x = along_x + taps[position] * padded[:, position:position + width_x]
    padded = jnp.pad(along_x, ((0, 0), (0, 0), (4, 4), (0, 0)))
    along_y = taps[0] * padded[:, :, 0:width_y]
    for position in range(1, 9):
        along_y = along_y + taps[position] * padded[:, :, position:position + width_y]
    return jnp.einsum("abcz,zw->abcw", along_y, matrix, precision=lax.Precision.HIGHEST)


def reference(log_dens, theta, cotangent):
    matrix = band_matrix(NZ)
    source = log_dens.reshape(DENSITIES, NX, NY, NZ)
    total_mass = jnp.sum(jnp.exp(source), axis=(1, 2, 3))
    log_p = source - jnp.log(total_mass)[:, None, None, None] + jnp.log(jnp.float32(NX * NY * NZ))
    weights = jax.nn.softmax(theta)
    potential = jnp.zeros_like(log_p)
    saved = []
    for iteration in range(ITERS):
        smooth = jnp.log(smooth_field(jnp.exp(potential), matrix))
        log_u = log_p - smooth
        spread = jnp.log(smooth_field(jnp.exp(log_u), matrix))
        log_q = jnp.sum(weights[:, None, None, None] * spread, axis=0)
        saved.append((potential, smooth, log_u, spread))
        potential = log_q[None] - spread
    barycenter = jnp.exp(log_q)
    back_q = cotangent.reshape(NX, NY, NZ) * barycenter
    back_v = jnp.zeros_like(log_p)
    grad_p = jnp.zeros_like(log_p)
    weight_grad = jnp.zeros((DENSITIES,), jnp.float32)
    for iteration in reversed(range(ITERS)):
        potential, smooth, log_u, spread = saved[iteration]
        combined = jnp.sum(back_v, axis=0)
        if iteration == ITERS - 1:
            combined = combined + back_q
        back_r = weights[:, None, None, None] * combined[None] - back_v
        weight_grad = weight_grad + jnp.sum(combined[None] * spread, axis=(1, 2, 3))
        back_u = jnp.exp(log_u) * smooth_field(back_r * jnp.exp(-spread), matrix)
        grad_p = grad_p + back_u
        if iteration > 0:
            back_v = -(jnp.exp(potential) * smooth_field(back_u * jnp.exp(-smooth), matrix))
    grad_sums = jnp.sum(grad_p, axis=(1, 2, 3))
    grad_dens = grad_p - jnp.exp(source) / total_mass[:, None, None, None] * grad_sums[:, None, None, None]
    grad_theta = weights * (weight_grad - jnp.sum(weights * weight_grad))
    return (barycenter.reshape(NX, NY * NZ), grad_dens.reshape(DENSITIES, NX, NY * NZ), grad_theta)
```

```python
import math

import jax
import jax.numpy as jnp
import numpy as np
from jax import lax
from jax.experimental import pallas as pl
from jax.experimental.pallas import tpu as pltpu
from jax.sharding import PartitionSpec as P

NZ = 64
K = 8
L = 128
HALO = 8
HT = HALO * NZ // L
VMEM = 56 * 1024 * 1024
F32 = jnp.float32
BF16 = jnp.bfloat16


def tap_list():
    raw_taps = [math.exp(-(offset * offset) / 8.0) for offset in range(-4, 5)]
    tap_total = 0.0
    for value in raw_taps:
        tap_total = tap_total + value
    return [value / tap_total for value in raw_taps]


G4, G3, G2, G1, G0 = tap_list()[:5]


def depth_weights():
    taps = tap_list()
    band = np.zeros((L, L), np.float32)
    for i in range(L):
        for j in range(L):
            if i // NZ == j // NZ and abs(i - j) <= 4:
                band[i, j] = taps[i - j + 4]
    high = band.astype(BF16)
    low = (band - high.astype(np.float32)).astype(BF16)
    half = np.concatenate([high, low], axis=1)
    return np.concatenate([half, half], axis=0)


def nine(at):
    return (G0 * at(4) + G1 * (at(3) + at(5))) + (G2 * (at(2) + at(6)) + G3 * (at(1) + at(7))) + G4 * (at(0) + at(8))


def conv_x(src, dst):
    rows, tiles = dst.shape[0], dst.shape[1]

    def column(t, carry):
        for first in range(0, rows, 8):
            block = src[first : first + 16, t]
            dst[first : first + 8, t] = nine(lambda j: block[j : j + 8])
        return carry

    lax.fori_loop(0, tiles, column, 0)


def conv_yz(src, first, rows, w_ref):
    value = src[pl.ds(first, rows)]
    tiles = value.shape[1]
    n = tiles - 4
    flat = (rows * (tiles - 1) * K, L)
    lane = lax.broadcasted_iota(jnp.int32, flat, 1)
    mixed = jnp.where(lane < NZ, value[:, 1:].reshape(flat), value[:, :-1].reshape(flat))
    odd = pltpu.roll(mixed, NZ, axis=1).reshape(rows, tiles - 1, K, L)
    along = (G0 * value[:, 2 : n + 2] + G1 * (odd[:, 1 : n + 1] + odd[:, 2 : n + 2])) + (
        G2 * (value[:, 1 : n + 1] + value[:, 3 : n + 3]) + G3 * (odd[:, 0:n] + odd[:, 3 : n + 3])
    ) + G4 * (value[:, 0:n] + value[:, 4 : n + 4])
    along = along.reshape(rows * n * K, L)
    high = along.astype(BF16)
    low = (along - high.astype(F32)).astype(BF16)
    both = jnp.dot(jnp.concatenate([high, low], axis=1), w_ref[...], preferred_element_type=F32)
    return (both[:, :L] + both[:, L:]).reshape(rows, n, K, L)


def parities():
    return lax.rem(lax.axis_index("gx"), 2), lax.rem(lax.axis_index("gy"), 2)


def assemble(big, own, xa, xb, ya, yb, ca, cb):
    rows, tiles = own.shape[0], own.shape[1]
    px, py = parities()
    row_a, row_b = (1 - px) * (rows + HALO), px * (rows + HALO)
    col_a, col_b = (1 - py) * (tiles + HT), py * (tiles + HT)
    big[pl.ds(HALO, rows), pl.ds(HT, tiles)] = own[...]
    big[pl.ds(row_a, HALO), pl.ds(HT, tiles)] = xa[0:HALO]
    big[pl.ds(row_b, HALO), pl.ds(HT, tiles)] = xb[0:HALO]
    slabs = xa.shape[0]
    for col, y, c in ((col_a, ya, ca), (col_b, yb, cb)):
        big[pl.ds(HALO, rows), pl.ds(col, HT)] = y[0:rows]
        big[pl.ds(row_a, HALO), pl.ds(col, HT)] = c[0:HALO]
        big[pl.ds(row_b, HALO), pl.ds(col, HT)] = c[slabs : slabs + HALO]


def give_edges(own, xa, xb, ya, yb):
    rows, tiles = own.shape[0], own.shape[1]
    px, py = parities()
    xa[0:HALO] = own[pl.ds((1 - px) * (rows - HALO), HALO)]
    xb[0:HALO] = own[pl.ds(px * (rows - HALO), HALO)]
    ya[0:rows] = own[:, pl.ds((1 - py) * (tiles - HT), HT)]
    yb[0:rows] = own[:, pl.ds(py * (tiles - HT), HT)]


def clear_outside(*fields):
    rows, tiles = fields[0].shape[0], fields[0].shape[1]
    gx, gy = lax.axis_index("gx"), lax.axis_index("gy")

    def zero(rs, ts):
        def write():
            for f in fields:
                f[rs, ts] = jnp.zeros_like(f[rs, ts])

        return write

    pl.when(gx == 0)(zero(slice(0, 4), slice(0, tiles)))
    pl.when(gx == lax.axis_size("gx") - 1)(zero(slice(rows - 4, rows), slice(0, tiles)))
    pl.when(gy == 0)(zero(slice(0, rows), slice(0, 2)))
    pl.when(gy == lax.axis_size("gy") - 1)(zero(slice(0, rows), slice(tiles - 2, tiles)))


def start_kernel(log_ref, rx_ref, ryz_ref, dens, e, mass, xa, xb, ya, yb, turn):
    rows, tiles = dens.shape[0], dens.shape[1]
    for t in range(tiles):
        turn[t] = log_ref[:, t * L : (t + 1) * L]

    def row(i, acc):
        for t in range(tiles):
            d = jnp.exp(turn[t, pl.ds(i, K, stride=rows), :])
            dens[i, t] = d
            e[i, t] = d * (ryz_ref[:, t * L : (t + 1) * L] * rx_ref[pl.ds(i, 1), :])
            acc = acc + d
        return acc

    mass[...] = lax.fori_loop(0, rows, row, jnp.zeros((K, L), F32))
    give_edges(e, xa, xb, ya, yb)


def first_kernel(w_ref, wb, dens, cot, own, rxa, rxb, rya, ryb, rca, rcb, inv_a, v, u, inv_s, xa, xb, ya, yb, big, tmp, tmp2):
    rows, tiles = own.shape[0], own.shape[1]
    assemble(big, own, rxa, rxb, rya, ryb, rca, rcb)
    conv_x(big, tmp)

    def ring(c, carry):
        spread = jnp.log(conv_yz(tmp, c * 4, 4, w_ref))
        log_q = jnp.sum(wb[...] * spread, axis=2, keepdims=True)
        v[pl.ds(c * 4, 4)] = jnp.exp(log_q - spread)
        inv_a[pl.ds(c * 4, 4)] = jnp.exp(-spread)
        return carry

    lax.fori_loop(0, (rows + 8) // 4, ring, 0)
    clear_outside(v, inv_a)
    conv_x(v, tmp2)

    def inner(c, carry):
        inv = 1.0 / conv_yz(tmp2, c * 4, 4, w_ref)
        inv_s[pl.ds(c * 4, 4)] = inv
        u[pl.ds(c * 4, 4)] = dens[pl.ds(c * 4, 4)] * inv
        return carry

    lax.fori_loop(0, rows // 4, inner, 0)
    give_edges(u, xa, xb, ya, yb)
    px, py = parities()
    for t in range(tiles):
        xa[HALO, t] = cot[pl.ds(pl.multiple_of((1 - px) * (rows - 8), 8), 8), t * L : (t + 1) * L]
        xb[HALO, t] = cot[pl.ds(pl.multiple_of(px * (rows - 8), 8), 8), t * L : (t + 1) * L]
    for out, side in ((ya, 1 - py), (yb, py)):
        for t in range(HT):
            lanes = pl.ds(pl.multiple_of((side * (tiles - HT) + t) * L, L), L)
            for b in range(rows // 8):
                out[rows + b, t] = cot[b * 8 : b * 8 + 8, lanes]


def second_kernel(w_ref, wb, cot, inv_s, own, rxa, rxb, rya, ryb, rca, rcb, bu, z, q, sums, xa, xb, ya, yb, big, tmp, r, tmp2, cots):
    rows, tiles = own.shape[0], own.shape[1]
    assemble(big, own, rxa, rxb, rya, ryb, rca, rcb)
    px, py = parities()
    row_a, row_b = (1 - px) * (rows + HALO), px * (rows + HALO)
    col_a, col_b = (1 - py) * (tiles + HT), py * (tiles + HT)
    row_a, row_b = pl.multiple_of(row_a, 8), pl.multiple_of(row_b, 8)
    for t in range(tiles):
        cots[HT + t, HALO : HALO + rows] = cot[:, t * L : (t + 1) * L]
        cots[HT + t, pl.ds(row_a, 8)] = rxa[HALO, t]
        cots[HT + t, pl.ds(row_b, 8)] = rxb[HALO, t]
    for col, y, c in ((col_a, rya, rca), (col_b, ryb, rcb)):
        for t in range(HT):
            for b in range(rows // 8):
                cots[col + t, HALO + b * 8 : HALO + b * 8 + 8] = y[rows + b, t]
            cots[col + t, pl.ds(row_a, 8)] = c[HALO, t]
            cots[col + t, pl.ds(row_b, 8)] = c[2 * HALO + 1, t]
    conv_x(big, tmp)

    def ring(c, mine):
        spread = jnp.log(conv_yz(tmp, c * 4, 4, w_ref))
        log_q = jnp.sum(wb[...] * spread, axis=2, keepdims=True)
        ratio = wb[...] * jnp.exp(log_q - spread)
        acc_k = jnp.zeros((K, L), F32)
        acc_s = jnp.zeros((1, L), F32)
        for i in range(4):
            for t in range(tiles + 4):
                cell = cots[t + 2, pl.ds(c * 4 + i + 4, 1), :]
                r[c * 4 + i, t] = ratio[i, t] * cell
                if mine and 2 <= t < tiles + 2:
                    row_q = jnp.exp(log_q[i, t])
                    q[t - 2, pl.ds(c * 4 + i - 4, 1), :] = row_q[0:1]
                    combined = cell * row_q[0:1]
                    acc_s = acc_s + combined
                    acc_k = acc_k + combined * spread[i, t]
        if mine:
            sums[0] += acc_k
            sums[1, 0:1] += acc_s

    sums[...] = jnp.zeros_like(sums)
    ring(0, False)
    ring((rows + 4) // 4, False)

    def middle(c, carry):
        ring(c, True)
        return carry

    lax.fori_loop(1, (rows + 4) // 4, middle, 0)
    clear_outside(r)
    conv_x(r, tmp2)

    def inner(c, carry):
        s = pl.ds(c * 4, 4)
        back = own[s] * conv_yz(tmp2, c * 4, 4, w_ref)
        bu[s] = back
        z[s] = back * inv_s[s]
        return carry

    lax.fori_loop(0, rows // 4, inner, 0)
    give_edges(z, xa, xb, ya, yb)


def third_kernel(w_ref, wb, inv_a, v, e, bu, own, rxa, rxb, rya, ryb, rca, rcb, gp, sums, big, tmp, r, tmp2):
    rows, tiles = own.shape[0], own.shape[1]
    assemble(big, own, rxa, rxb, rya, ryb, rca, rcb)
    conv_x(big, tmp)

    def ring(c, mine):
        s = pl.ds(c * 4, 4)
        back_v = -(v[s] * conv_yz(tmp, c * 4, 4, w_ref))
        combined = jnp.sum(back_v, axis=2, keepdims=True)
        inv = inv_a[s]
        r[s] = (wb[...] * combined - back_v) * inv
        if mine:
            part = combined[:, 2 : tiles + 2]
            sums[0] += jnp.sum(part * -jnp.log(inv[:, 2 : tiles + 2]), axis=(0, 1))
            sums[1, 0:1] += jnp.sum(part, axis=(0, 1))

    sums[...] = jnp.zeros_like(sums)
    ring(0, False)
    ring((rows + 4) // 4, False)

    def middle(c, carry):
        ring(c, True)
        return carry

    lax.fori_loop(1, (rows + 4) // 4, middle, 0)
    conv_x(r, tmp2)

    def inner(c, carry):
        s = pl.ds(c * 4, 4)
        gp[s] = bu[s] + e[s] * conv_yz(tmp2, c * 4, 4, w_ref)
        return carry

    lax.fori_loop(0, rows // 4, inner, 0)


def last_kernel(scale, coef, gp, dens, q, out, bary, turn):
    rows, tiles = gp.shape[0], gp.shape[1]

    def row(i, carry):
        for t in range(tiles):
            turn[t, pl.ds(i, K, stride=rows), :] = gp[i, t] * scale[...] - dens[i, t] * coef[...]
        return carry

    lax.fori_loop(0, rows, row, 0)
    for t in range(tiles):
        out[:, t * L : (t + 1) * L] = turn[t]
        bary[:, t * L : (t + 1) * L] = q[t] * scale[0:1, :]


def call(kernel, outs, scratch, *args):
    vmem = pl.BlockSpec(memory_space=pltpu.VMEM)
    return pl.pallas_call(
        kernel,
        out_shape=[jax.ShapeDtypeStruct(s, F32) for s in outs],
        in_specs=[vmem] * len(args),
        out_specs=[vmem] * len(outs),
        scratch_shapes=[pltpu.VMEM(s, F32) for s in scratch],
        compiler_params=pltpu.CompilerParams(vmem_limit_bytes=VMEM),
    )(*args)


def swap(value, axis, parity):
    count = lax.axis_size(axis)
    pairs = []
    for i in range(count):
        j = i + 1 if i % 2 == parity else i - 1
        if 0 <= j < count:
            pairs.append((i, j))
    return lax.ppermute(value, axis, pairs)


def exchange(xa, xb, ya, yb, tiles):
    rxa, rxb = swap(xa, "gx", 0), swap(xb, "gx", 1)
    rya, ryb = swap(ya, "gy", 0), swap(yb, "gy", 1)
    py = lax.rem(lax.axis_index("gy"), 2)

    def corner(side):
        first = side * (tiles - HT)
        return jnp.concatenate([lax.dynamic_slice_in_dim(r, first, HT, axis=1) for r in (rxa, rxb)], axis=0)

    rca, rcb = swap(corner(1 - py), "gy", 0), swap(corner(py), "gy", 1)
    return rxa, rxb, rya, ryb, rca, rcb


def inside_sum(axis, length):
    count = lax.axis_size(axis) * length
    at = lax.axis_index(axis) * length + jnp.arange(length)
    total = jnp.zeros((length,), F32)
    for offset, tap in zip(range(-4, 5), tap_list()):
        total = total + tap * ((at + offset >= 0) & (at + offset < count)).astype(F32)
    return total


def depth_sum():
    at = jnp.arange(NZ)
    total = jnp.zeros((NZ,), F32)
    for offset, tap in zip(range(-4, 5), tap_list()):
        total = total + tap * ((at + offset >= 0) & (at + offset < NZ)).astype(F32)
    return total


def shards(log_dens, theta, cotangent):
    _, rows, merged = log_dens.shape
    tiles = merged // L
    devices = lax.axis_size("gx") * lax.axis_size("gy")
    cells = devices * rows * merged
    weights = jax.nn.softmax(theta)
    wb = jnp.broadcast_to(weights[:, None], (K, L))
    w = jnp.asarray(depth_weights())
    rx = jnp.broadcast_to((1.0 / inside_sum("gx", rows))[:, None], (rows, L))
    ryz = (1.0 / (inside_sum("gy", merged // NZ)[:, None] * depth_sum()[None, :])).reshape(1, merged)

    field, ringed, full = (rows, tiles, K, L), (rows + 8, tiles + 4, K, L), (rows + 16, tiles + 8, K, L)
    tmp, tmp2 = (rows + 8, tiles + 8, K, L), (rows, tiles + 4, K, L)
    acc = (2, K, L)

    def edges(x_extra, y_extra):
        return [(HALO + x_extra, tiles, K, L)] * 2 + [(rows + y_extra, HT, K, L)] * 2

    dens, e, mass, *sent = call(start_kernel, [field, field, (K, L)] + edges(0, 0), [(tiles, K * rows, L)], log_dens.reshape(K * rows, merged), rx, ryz)
    got = exchange(*sent, tiles)
    inv_a, v, u, inv_s, *sent = call(
        first_kernel, [ringed, ringed, field, field] + edges(1, rows // 8), [full, tmp, tmp2], w, wb, dens, cotangent, e, *got
    )
    got = exchange(*sent, tiles)
    bu, z, q, sums1, *sent = call(
        second_kernel,
        [field, field, (tiles, rows, L), acc] + edges(0, 0),
        [full, tmp, ringed, tmp2, (tiles + 8, rows + 16, L)],
        w, wb, cotangent, inv_s, u, *got,
    )
    got = exchange(*sent, tiles)
    gp, sums0 = call(third_kernel, [field, acc], [full, tmp, ringed, tmp2], w, wb, inv_a, v, e, bu, z, *got)

    local = jnp.concatenate([mass[None], sums1, sums0], axis=0).sum(axis=2).reshape(1, 5 * K)
    local = jnp.broadcast_to(jnp.pad(local, ((0, 0), (0, L - 5 * K))), (devices, L))
    total = lax.all_to_all(local, ("gx", "gy"), 0, 0, tiled=True).sum(axis=0)
    total_mass, wg1, s1, wg0, s0 = total[:K], total[K : 2 * K], total[2 * K], total[3 * K : 4 * K], total[4 * K]

    shift_k = jnp.log(F32(cells)) - jnp.log(total_mass)
    shift = jnp.sum(weights * shift_k)
    scale = jnp.exp(shift)
    weight_grad = scale * (wg1 + (2.0 * shift_k - shift) * s1 + wg0 + shift_k * s0)
    grad_theta = weights * (weight_grad - jnp.sum(weights * weight_grad))
    late = weights * (scale * s1)
    grad_sums = late + (late - weights * jnp.sum(late))
    coef = jnp.broadcast_to((grad_sums / total_mass)[:, None], (K, L))
    grad, bary = call(last_kernel, [(K * rows, merged), (rows, merged)], [(tiles, K * rows, L)], jnp.broadcast_to(scale, (K, L)), coef, gp, dens, q)
    return bary, grad.reshape(K, rows, merged), grad_theta


def solution(mesh):
    placed = (P(None, "gx", "gy"), P(), P("gx", "gy"))
    return jax.shard_map(
        shards,
        mesh=mesh,
        in_specs=placed,
        out_specs=(P("gx", "gy"), P(None, "gx", "gy"), P()),
        check_vma=False,
    )
```

```python
import functools
import math

import jax
import jax.numpy as jnp
import numpy as np
from jax import lax
from jax.experimental import pallas as pl
from jax.experimental.pallas import tpu as pltpu
from jax.sharding import PartitionSpec as P

NZ = 64
K = 8
L = 128
HALO = 8
HT = HALO * NZ // L
VMEM = 24 * 1024 * 1024
F32 = jnp.float32
BF16 = jnp.bfloat16


def tap_list():
    raw_taps = [math.exp(-(offset * offset) / 8.0) for offset in range(-4, 5)]
    tap_total = 0.0
    for value in raw_taps:
        tap_total = tap_total + value
    return [value / tap_total for value in raw_taps]


G4, G3, G2, G1, G0 = tap_list()[:5]


def depth_weights():
    taps = tap_list()
    band = np.zeros((L, L), np.float32)
    for i in range(L):
        for j in range(L):
            if i // NZ == j // NZ and abs(i - j) <= 4:
                band[i, j] = taps[i - j + 4]
    high = band.astype(BF16)
    low = (band - high.astype(np.float32)).astype(BF16)
    half = np.concatenate([high, low], axis=1)
    return np.concatenate([half, half], axis=0)


def nine(at):
    return (G0 * at(4) + G1 * (at(3) + at(5))) + (G2 * (at(2) + at(6)) + G3 * (at(1) + at(7))) + G4 * (at(0) + at(8))


def conv_x(src, dst):
    rows, tiles = dst.shape[0], dst.shape[1]

    def column(t, carry):
        for first in range(0, rows, 8):
            block = src[first : first + 16, t]
            dst[first : first + 8, t] = nine(lambda j: block[j : j + 8])
        return carry

    lax.fori_loop(0, tiles, column, 0)


def conv_yz(src, first, rows, w_ref):
    value = src[pl.ds(first, rows)]
    tiles = value.shape[1]
    n = tiles - 4
    flat = (rows * (tiles - 1) * K, L)
    lane = lax.broadcasted_iota(jnp.int32, flat, 1)
    mixed = jnp.where(lane < NZ, value[:, 1:].reshape(flat), value[:, :-1].reshape(flat))
    odd = pltpu.roll(mixed, NZ, axis=1).reshape(rows, tiles - 1, K, L)
    along = (G0 * value[:, 2 : n + 2] + G1 * (odd[:, 1 : n + 1] + odd[:, 2 : n + 2])) + (
        G2 * (value[:, 1 : n + 1] + value[:, 3 : n + 3]) + G3 * (odd[:, 0:n] + odd[:, 3 : n + 3])
    ) + G4 * (value[:, 0:n] + value[:, 4 : n + 4])
    along = along.reshape(rows * n * K, L)
    high = along.astype(BF16)
    low = (along - high.astype(F32)).astype(BF16)
    both = jnp.dot(jnp.concatenate([high, low], axis=1), w_ref[...], preferred_element_type=F32)
    return (both[:, :L] + both[:, L:]).reshape(rows, n, K, L)


def parities():
    return lax.rem(lax.axis_index("gx"), 2), lax.rem(lax.axis_index("gy"), 2)


def sides(rows, tiles):
    px, py = parities()
    return ((1 - px) * (rows + HALO), px * (rows + HALO)), ((1 - py) * (tiles + HT), py * (tiles + HT))


def assemble(big, own, got):
    rows, tiles = own.shape[0], own.shape[1]
    xa, xb, ya, yb, ca, cb = got
    (row_a, row_b), (col_a, col_b) = sides(rows, tiles)
    middle, slabs = pl.ds(HALO, rows), xa.shape[0]
    big[middle, pl.ds(HT, tiles)] = own[...]
    big[pl.ds(row_a, HALO), pl.ds(HT, tiles)] = xa[0:HALO]
    big[pl.ds(row_b, HALO), pl.ds(HT, tiles)] = xb[0:HALO]
    for col, y, c in ((col_a, ya, ca), (col_b, yb, cb)):
        big[middle, pl.ds(col, HT)] = y[0:rows]
        big[pl.ds(row_a, HALO), pl.ds(col, HT)] = c[0:HALO]
        big[pl.ds(row_b, HALO), pl.ds(col, HT)] = c[slabs : slabs + HALO]


def give_edges(own, outs):
    xa, xb, ya, yb = outs
    rows, tiles = own.shape[0], own.shape[1]
    px, py = parities()
    xa[0:HALO] = own[pl.ds((1 - px) * (rows - HALO), HALO)]
    xb[0:HALO] = own[pl.ds(px * (rows - HALO), HALO)]
    ya[0:rows] = own[:, pl.ds((1 - py) * (tiles - HT), HT)]
    yb[0:rows] = own[:, pl.ds(py * (tiles - HT), HT)]


def clear_outside(*fields):
    rows, tiles = fields[0].shape[0], fields[0].shape[1]
    gx, gy = lax.axis_index("gx"), lax.axis_index("gy")

    def zero(rs, ts):
        def write():
            for f in fields:
                f[rs, ts] = jnp.zeros_like(f[rs, ts])

        return write

    pl.when(gx == 0)(zero(slice(0, 4), slice(0, tiles)))
    pl.when(gx == lax.axis_size("gx") - 1)(zero(slice(rows - 4, rows), slice(0, tiles)))
    pl.when(gy == 0)(zero(slice(0, rows), slice(0, 2)))
    pl.when(gy == lax.axis_size("gy") - 1)(zero(slice(0, rows), slice(tiles - 2, tiles)))


def inside(at, count):
    total = jnp.zeros(at.shape, F32)
    for offset, tap in zip(range(-4, 5), tap_list()):
        total = total + jnp.where((at + offset >= 0) & (at + offset < count), F32(tap), F32(0.0))
    return total


def in_lanes(*columns):
    lane = lax.broadcasted_iota(jnp.int32, (K, L), 1)
    out = jnp.zeros((K, L), F32)
    for i, c in enumerate(columns):
        out = jnp.where(lane == i, c, out)
    return out


def over_lanes(value):
    return jnp.sum(value, axis=1, keepdims=True)


def centre(field):
    return jnp.log(over_lanes(field[field.shape[0] // 2, field.shape[1] // 2]) * (1.0 / L))


def start_kernel(log_ref, dens, e, mass, *rest):
    edges, (turn, around, sem) = rest[:4], rest[4:]
    rows, tiles = dens.shape[0], dens.shape[1]
    loads = [pltpu.make_async_copy(log_ref.at[:, pl.ds(t * L, L)], turn.at[t], sem.at[t]) for t in range(tiles)]
    for c in loads:
        c.start()
    lane = lax.broadcasted_iota(jnp.int32, (K, L), 1)
    depth = inside(lane % NZ, NZ)
    first = lax.axis_index("gy") * (tiles * L // NZ)
    for t in range(tiles):
        along = inside(first + t * (L // NZ) + lane // NZ, lax.axis_size("gy") * (tiles * L // NZ))
        around[t] = 1.0 / (along * depth)
    for c in loads:
        c.wait()

    def row(x, acc):
        across = 1.0 / inside(jnp.full((K, L), lax.axis_index("gx") * rows + x), lax.axis_size("gx") * rows)
        for t in range(tiles):
            d = jnp.exp(turn[t, pl.ds(x, K, stride=rows), :])
            dens[x, t] = d
            e[x, t] = d * (around[t] * across)
            acc = acc + d
        return acc

    mass[...] = lax.fori_loop(0, rows, row, jnp.zeros((K, L), F32))
    give_edges(e, edges)


def first_kernel(w_ref, wb, cot, dens, own, *rest):
    got, (inv_a, v, u, inv_s), edges, (big, tmp) = rest[:6], rest[6:10], rest[10:14], rest[14:]
    rows, tiles = own.shape[0], own.shape[1]
    assemble(big, own, got)
    conv_x(big, tmp)

    def ring(c, carry):
        s = pl.ds(c * 4, 4)
        spread = jnp.log(conv_yz(tmp, c * 4, 4, w_ref))
        log_q = jnp.sum(wb[...] * spread, axis=2, keepdims=True)
        v[s] = jnp.exp(log_q - spread)
        inv_a[s] = jnp.exp(-spread)
        return carry

    lax.fori_loop(0, (rows + 8) // 4, ring, 0)
    clear_outside(v, inv_a)
    tmp2 = tmp.at[pl.ds(0, rows), pl.ds(0, tiles + 4)]
    conv_x(v, tmp2)

    def inner(c, carry):
        s = pl.ds(c * 4, 4)
        inv = 1.0 / conv_yz(tmp2, c * 4, 4, w_ref)
        inv_s[s] = inv
        u[s] = dens[s] * inv
        return carry

    lax.fori_loop(0, rows // 4, inner, 0)
    give_edges(u, edges)
    xa, xb, ya, yb = edges
    px, py = parities()
    row_a = pl.ds(pl.multiple_of((1 - px) * (rows - 8), 8), 8)
    row_b = pl.ds(pl.multiple_of(px * (rows - 8), 8), 8)
    for t in range(tiles):
        xa[HALO, t] = cot[row_a, t * L : (t + 1) * L]
        xb[HALO, t] = cot[row_b, t * L : (t + 1) * L]
    for out, side in ((ya, 1 - py), (yb, py)):
        for t in range(HT):
            lanes = pl.ds(pl.multiple_of((side * (tiles - HT) + t) * L, L), L)
            for b in range(rows // 8):
                out[rows + b, t] = cot[b * 8 : b * 8 + 8, lanes]


def second_kernel(w_ref, wb, mass, cot, inv_s, own, *rest):
    got, (bu, z, q, told), edges, (big, tmp, r, cots, sums) = rest[:6], rest[6:10], rest[10:14], rest[14:]
    rows, tiles = own.shape[0], own.shape[1]
    assemble(big, own, got)
    (row_a, row_b), (col_a, col_b) = sides(rows, tiles)
    rxa, rxb, rya, ryb, rca, rcb = got
    slab = rxa.shape[0]
    ra, rb = pl.ds(pl.multiple_of(row_a, 8), 8), pl.ds(pl.multiple_of(row_b, 8), 8)
    for t in range(tiles):
        cots[HT + t, HALO : HALO + rows] = cot[:, t * L : (t + 1) * L]
        cots[HT + t, ra] = rxa[HALO, t]
        cots[HT + t, rb] = rxb[HALO, t]
    for col, y, c in ((col_a, rya, rca), (col_b, ryb, rcb)):
        for t in range(HT):
            for b in range(rows // 8):
                cots[col + t, HALO + b * 8 : HALO + b * 8 + 8] = y[rows + b, t]
            cots[col + t, ra] = c[HALO, t]
            cots[col + t, rb] = c[slab + HALO, t]
    conv_x(big, tmp)
    mean = centre(own)

    def ring(c, mine):
        spread = jnp.log(conv_yz(tmp, c * 4, 4, w_ref))
        log_q = jnp.sum(wb[...] * spread, axis=2, keepdims=True)
        ratio = wb[...] * jnp.exp(log_q - spread)
        acc_k = jnp.zeros((K, L), F32)
        acc_s = jnp.zeros((1, L), F32)
        for i in range(4):
            for t in range(tiles + 4):
                cell = cots[t + 2, pl.ds(c * 4 + i + 4, 1), :]
                r[c * 4 + i, t] = ratio[i, t] * cell
                if mine and 2 <= t < tiles + 2:
                    row_q = jnp.exp(log_q[i, t])
                    q[t - 2, pl.ds(c * 4 + i - 4, 1), :] = row_q[0:1]
                    combined = cell * row_q[0:1]
                    acc_s = acc_s + combined
                    acc_k = acc_k + combined * (spread[i, t] - mean)
        if mine:
            sums[0] += acc_k
            sums[1, 0:1] += acc_s

    sums[...] = jnp.zeros_like(sums)
    ring(0, False)
    ring((rows + 4) // 4, False)

    def middle(c, carry):
        ring(c, True)
        return carry

    lax.fori_loop(1, (rows + 4) // 4, middle, 0)
    clear_outside(r)
    told[...] = in_lanes(over_lanes(mass[...]), over_lanes(sums[0]), over_lanes(sums[1, 0:1]), mean)
    tmp2 = tmp.at[pl.ds(0, rows), pl.ds(0, tiles + 4)]
    conv_x(r, tmp2)

    def inner(c, carry):
        s = pl.ds(c * 4, 4)
        back = own[s] * conv_yz(tmp2, c * 4, 4, w_ref)
        bu[s] = back
        z[s] = back * inv_s[s]
        return carry

    lax.fori_loop(0, rows // 4, inner, 0)
    give_edges(z, edges)


def third_kernel(w_ref, wb, before, inv_a, v, e, own, *rest):
    got, (r, told), (big, tmp, sums) = rest[:6], rest[6:8], rest[8:]
    rows, tiles = own.shape[0], own.shape[1]
    assemble(big, own, got)
    conv_x(big, tmp)
    mean = centre(e)

    def ring(c, mine):
        s = pl.ds(c * 4, 4)
        back_v = -(v[s] * conv_yz(tmp, c * 4, 4, w_ref))
        combined = jnp.sum(back_v, axis=2, keepdims=True)
        inv = inv_a[s]
        r[s] = (wb[...] * combined - back_v) * inv
        if mine:
            part = combined[:, 2 : tiles + 2]
            sums[0] += jnp.sum(part * (-jnp.log(inv[:, 2 : tiles + 2]) - mean), axis=(0, 1))
            sums[1, 0:1] += jnp.sum(part, axis=(0, 1))

    sums[...] = jnp.zeros_like(sums)
    ring(0, False)
    ring((rows + 4) // 4, False)

    def middle(c, carry):
        ring(c, True)
        return carry

    lax.fori_loop(1, (rows + 4) // 4, middle, 0)
    early = before[...]
    told[...] = in_lanes(*[early[:, i : i + 1] for i in range(4)], over_lanes(sums[0]), over_lanes(sums[1, 0:1]), mean)


def fourth_kernel(w_ref, r, bu, e, gp, tmp2):
    conv_x(r, tmp2)

    def inner(c, carry):
        s = pl.ds(c * 4, 4)
        gp[s] = bu[s] + e[s] * conv_yz(tmp2, c * 4, 4, w_ref)
        return carry

    lax.fori_loop(0, gp.shape[0] // 4, inner, 0)


def last_kernel(cells, wb, heard, gp, dens, q, out, bary, theta_out, turn, sem):
    rows, tiles = gp.shape[0], gp.shape[1]
    weights = wb[:, 0:1]
    everyone = heard[...]
    total = jnp.sum(everyone, axis=0)
    mass, late = total[:, 0:1], total[:, 2:3]
    shift_k = jnp.log(F32(cells)) - jnp.log(mass)
    shift = jnp.sum(weights * shift_k, axis=0, keepdims=True)
    scale = jnp.exp(shift)
    last = weights * (scale * late)
    grad_sums = last + (last - weights * jnp.sum(last, axis=0, keepdims=True))
    coef = jnp.broadcast_to(grad_sums / mass, (K, L))
    scale_all = jnp.broadcast_to(scale, (K, L))
    copies = []
    for t in range(tiles):

        def rows_of(c, carry):
            for i in range(8):
                x = c * 8 + i
                turn[t, pl.ds(x, K, stride=rows), :] = gp[x, t] * scale_all - dens[x, t] * coef
            return carry

        lax.fori_loop(0, rows // 8, rows_of, 0)
        copies.append(pltpu.make_async_copy(turn.at[t], out.at[:, pl.ds(t * L, L)], sem.at[t]))
        copies[-1].start()
        bary[:, t * L : (t + 1) * L] = q[t] * scale
    second = everyone[:, :, 1:2] + (everyone[:, :, 3:4] + (2.0 * shift_k - shift)) * everyone[:, :, 2:3]
    first = everyone[:, :, 4:5] + (everyone[:, :, 6:7] + shift_k) * everyone[:, :, 5:6]
    weight_grad = scale * jnp.sum(first + second, axis=0)
    grad = weights * (weight_grad - jnp.sum(weights * weight_grad, axis=0, keepdims=True))
    theta_out[...] = jnp.broadcast_to(grad, (K, L))
    for c in copies:
        c.wait()


def call(kernel, outs, scratch, semaphores, args, kept=True, far_in=0, far_out=0):
    vmem, far = pl.BlockSpec(memory_space=pltpu.VMEM), pl.BlockSpec(memory_space=pl.ANY)
    near = len(args) - far_in
    args = [pltpu.with_memory_space_constraint(a, pltpu.VMEM) if kept and a.size > L * L * 4 else a for a in args[:near]] + args[near:]
    return pl.pallas_call(
        kernel,
        out_shape=[pltpu.VMEM(s, F32) if kept else jax.ShapeDtypeStruct(s, F32) for s in outs],
        in_specs=[vmem] * near + [far] * far_in,
        out_specs=[far] * far_out + [vmem] * (len(outs) - far_out),
        scratch_shapes=[pltpu.VMEM(s, F32) for s in scratch] + [pltpu.SemaphoreType.DMA((n,)) for n in semaphores],
        compiler_params=pltpu.CompilerParams(vmem_limit_bytes=VMEM),
    )(*args)


def partners(axis, parity):
    count = lax.axis_size(axis)
    found = {}
    for i in range(count):
        j = i + 1 if i % 2 == parity else i - 1
        if 0 <= j < count:
            found[i] = j
    return found


def swap(value, axis, parity):
    return lax.ppermute(value, axis, list(partners(axis, parity).items()))


def exchange(xa, xb, ya, yb, tiles):
    rxa, rxb = swap(xa, "gx", 0), swap(xb, "gx", 1)
    rya, ryb = swap(ya, "gy", 0), swap(yb, "gy", 1)
    py = lax.rem(lax.axis_index("gy"), 2)

    def corner(side):
        first = side * (tiles - HT)
        return jnp.concatenate([lax.dynamic_slice_in_dim(r, first, HT, axis=1) for r in (rxa, rxb)], axis=0)

    rca, rcb = swap(corner(1 - py), "gy", 0), swap(corner(py), "gy", 1)
    return rxa, rxb, rya, ryb, rca, rcb


def over_all(told):
    devices = lax.axis_size("gx") * lax.axis_size("gy")
    return lax.all_to_all(jnp.broadcast_to(told[None], (devices, K, L)), ("gx", "gy"), 0, 0, tiled=True)


def shards(log_dens, theta, cotangent):
    _, rows, merged = log_dens.shape
    tiles = merged // L
    cells = lax.axis_size("gx") * lax.axis_size("gy") * rows * merged
    wb = jnp.broadcast_to(jax.nn.softmax(theta)[:, None], (K, L))
    w = jnp.asarray(depth_weights())

    field, ringed, full = (rows, tiles, K, L), (rows + 8, tiles + 4, K, L), (rows + 16, tiles + 8, K, L)
    tmp, tmp2 = (rows + 8, tiles + 8, K, L), (rows, tiles + 4, K, L)
    acc, turn = (2, K, L), (tiles, K * rows, L)

    def edges(more, more_y):
        return [(HALO + more, tiles, K, L)] * 2 + [(rows + more_y, HT, K, L)] * 2

    logs = log_dens.reshape(K * rows, merged)
    dens, e, mass, *sent = call(start_kernel, [field, field, (K, L)] + edges(0, 0), [turn, (tiles, K, L)], [tiles], [logs], far_in=1)
    got = exchange(*sent, tiles)
    inv_a, v, u, inv_s, *sent = call(
        first_kernel, [ringed, ringed, field, field] + edges(1, rows // 8), [full, tmp], [], [w, wb, cotangent, dens, e, *got]
    )
    got = exchange(*sent, tiles)
    bu, z, q, told, *sent = call(
        second_kernel, [field, field, (tiles, rows, L), (K, L)] + edges(0, 0),
        [full, tmp, ringed, (tiles + 8, rows + 16, L), acc], [], [w, wb, mass, cotangent, inv_s, u, *got],
    )
    got = exchange(*sent, tiles)
    r, told = call(third_kernel, [ringed, (K, L)], [full, tmp, acc], [], [w, wb, told, inv_a, v, e, z, *got])
    heard = over_all(told)
    (gp,) = call(fourth_kernel, [field], [tmp2], [], [w, r, bu, e])
    grad, bary, grad_theta = call(
        functools.partial(last_kernel, cells), [(K * rows, merged), (rows, merged), (K, L)], [turn], [tiles],
        [wb, heard, gp, dens, q], False, 0, 1,
    )
    return bary, grad.reshape(K, rows, merged), grad_theta[:, 0]


def solution(mesh):
    placed = (P(None, "gx", "gy"), P(), P("gx", "gy"))
    return jax.shard_map(
        shards,
        mesh=mesh,
        in_specs=placed,
        out_specs=(P("gx", "gy"), P(None, "gx", "gy"), P()),
        check_vma=False,
    )
```

```python
import functools
import math

import jax
import jax.numpy as jnp
import numpy as np
from jax import lax
from jax.experimental import pallas as pl
from jax.experimental.pallas import tpu as pltpu
from jax.sharding import PartitionSpec as P

NZ = 64
K = 8
L = 128
HALO = 8
HT = HALO * NZ // L
VMEM = 24 * 1024 * 1024
F32 = jnp.float32
BF16 = jnp.bfloat16


def tap_list():
    raw_taps = [math.exp(-(offset * offset) / 8.0) for offset in range(-4, 5)]
    tap_total = 0.0
    for value in raw_taps:
        tap_total = tap_total + value
    return [value / tap_total for value in raw_taps]


G4, G3, G2, G1, G0 = tap_list()[:5]


def depth_weights():
    taps = tap_list()
    band = np.zeros((L, L), np.float32)
    for i in range(L):
        for j in range(L):
            if i // NZ == j // NZ and abs(i - j) <= 4:
                band[i, j] = taps[i - j + 4]
    high = band.astype(BF16)
    low = (band - high.astype(np.float32)).astype(BF16)
    half = np.concatenate([high, low], axis=1)
    return np.concatenate([half, half], axis=0)


def nine(at):
    return (G0 * at(4) + G1 * (at(3) + at(5))) + (G2 * (at(2) + at(6)) + G3 * (at(1) + at(7))) + G4 * (at(0) + at(8))


def conv_xz(src, dst, w_ref, shift, ranges):
    rows = dst.shape[0]

    def pair(i, first):
        t = first + 2 * i
        two = pl.ds(t, 2)
        for x in range(0, rows, 8):
            block = src[x : x + 16, pl.ds(t - shift, 2)]
            dst[x : x + 8, two] = nine(lambda j: block[j : j + 8])
        value = dst[:, two].reshape(rows * 2 * K, L)
        high = value.astype(BF16)
        low = (value - high.astype(F32)).astype(BF16)
        both = jnp.dot(jnp.concatenate([high, low], axis=1), w_ref[...], preferred_element_type=F32)
        dst[:, two] = (both[:, :L] + both[:, L:]).reshape(rows, 2, K, L)
        return first

    for first, end in ranges:
        lax.fori_loop(0, (end - first) // 2, pair, first)


def conv_y(src, first, rows, tile, n):
    value = src[pl.ds(first, rows), tile : tile + n + 4]
    flat = (rows * (n + 3) * K, L)
    lane = lax.broadcasted_iota(jnp.int32, flat, 1)
    mixed = jnp.where(lane < NZ, value[:, 1:].reshape(flat), value[:, :-1].reshape(flat))
    odd = pltpu.roll(mixed, NZ, axis=1).reshape(rows, n + 3, K, L)
    return (G0 * value[:, 2 : n + 2] + G1 * (odd[:, 1 : n + 1] + odd[:, 2 : n + 2])) + (
        G2 * (value[:, 1 : n + 1] + value[:, 3 : n + 3]) + G3 * (odd[:, 0:n] + odd[:, 3 : n + 3])
    ) + G4 * (value[:, 0:n] + value[:, 4 : n + 4])


def parities():
    return lax.rem(lax.axis_index("gx"), 2), lax.rem(lax.axis_index("gy"), 2)


def sides(rows, tiles):
    px, py = parities()
    return ((1 - px) * (rows + HALO), px * (rows + HALO)), ((1 - py) * (tiles + HT), py * (tiles + HT))


def join_rows(big, own, xa, xb):
    rows = own.shape[0]
    (row_a, row_b), _ = sides(rows, own.shape[1])
    big[HALO : HALO + rows] = own[...]
    big[pl.ds(row_a, HALO)] = xa[0:HALO]
    big[pl.ds(row_b, HALO)] = xb[0:HALO]


def join_ends(ends, rows, slabs, ya, yb, ca, cb):
    (row_a, row_b), _ = sides(rows, 0)
    _, py = parities()
    for col, y, c in (((1 - py) * HT, ya, ca), (py * HT, yb, cb)):
        lanes = pl.ds(col, HT)
        ends[pl.ds(HALO, rows), lanes] = y[0:rows]
        ends[pl.ds(row_a, HALO), lanes] = c[0:HALO]
        ends[pl.ds(row_b, HALO), lanes] = c[slabs : slabs + HALO]


def give_edges(own, outs):
    xa, xb, ya, yb = outs
    rows, tiles = own.shape[0], own.shape[1]
    px, py = parities()
    xa[0:HALO] = own[pl.ds((1 - px) * (rows - HALO), HALO)]
    xb[0:HALO] = own[pl.ds(px * (rows - HALO), HALO)]
    ya[0:rows] = own[:, pl.ds((1 - py) * (tiles - HT), HT)]
    yb[0:rows] = own[:, pl.ds(py * (tiles - HT), HT)]


def clear_outside(fields, ranges, ends):
    rows, tiles = fields[0].shape[0], fields[0].shape[1]
    gx, gy = lax.axis_index("gx"), lax.axis_index("gy")

    def zero(first, count, ts):
        def write():
            for f in fields:
                for start, end in ts:
                    f[first : first + count, start:end] = jnp.zeros((count, end - start, K, L), F32)

        return write

    pl.when(gx == 0)(zero(0, 4, ranges))
    pl.when(gx == lax.axis_size("gx") - 1)(zero(rows - 4, 4, ranges))
    if ends:
        pl.when(gy == 0)(zero(0, rows, [(0, 2)]))
        pl.when(gy == lax.axis_size("gy") - 1)(zero(0, rows, [(tiles - 2, tiles)]))


def parts(tiles, inner):
    if inner:
        return [(HT, tiles + HT)], [(HT, tiles)], [(HT, tiles)], [(HT, tiles - HT)]
    return (
        [(0, HT), (tiles + HT, tiles + 2 * HT)],
        [(0, HT), (tiles, tiles + HT)],
        [(0, HT), (tiles, tiles + HT)],
        [(0, HT), (tiles - HT, tiles)],
    )


def first_conv(inner, src, tmp, w_ref, tiles):
    whole = parts(tiles, inner)[0]
    if inner:
        conv_xz(src, tmp, w_ref, HT, whole)
    else:
        conv_xz(src, tmp, w_ref, 0, whole[:1])
        conv_xz(src, tmp, w_ref, tiles, whole[1:])


def inside(at, count):
    total = jnp.zeros(at.shape, F32)
    for offset, tap in zip(range(-4, 5), tap_list()):
        total = total + jnp.where((at + offset >= 0) & (at + offset < count), F32(tap), F32(0.0))
    return total


def in_lanes(*columns):
    lane = lax.broadcasted_iota(jnp.int32, (K, L), 1)
    out = jnp.zeros((K, L), F32)
    for i, c in enumerate(columns):
        out = jnp.where(lane == i, c, out)
    return out


def over_lanes(value):
    return jnp.sum(value, axis=1, keepdims=True)


def centre(field):
    return jnp.log(over_lanes(field[field.shape[0] // 2, field.shape[1] // 2]) * (1.0 / L))


def start_kernel(log_ref, dens, e, mass, *rest):
    edges, (turn, around, sem) = rest[:4], rest[4:]
    rows, tiles = dens.shape[0], dens.shape[1]
    loads = [pltpu.make_async_copy(log_ref.at[:, pl.ds(t * L, L)], turn.at[t], sem.at[t]) for t in range(tiles)]
    for c in loads:
        c.start()
    lane = lax.broadcasted_iota(jnp.int32, (K, L), 1)
    depth = inside(lane % NZ, NZ)
    first = lax.axis_index("gy") * (tiles * L // NZ)
    for t in range(tiles):
        along = inside(first + t * (L // NZ) + lane // NZ, lax.axis_size("gy") * (tiles * L // NZ))
        around[t] = 1.0 / (along * depth)
    for c in loads:
        c.wait()

    def row(x, acc):
        across = 1.0 / inside(jnp.full((K, L), lax.axis_index("gx") * rows + x), lax.axis_size("gx") * rows)
        for t in range(tiles):
            d = jnp.exp(turn[t, pl.ds(x, K, stride=rows), :])
            dens[x, t] = d
            e[x, t] = d * (around[t] * across)
            acc = acc + d
        return acc

    mass[...] = lax.fori_loop(0, rows, row, jnp.zeros((K, L), F32))
    give_edges(e, edges)


def first_fields(inner, wb, w_ref, dens, src, tmp, v, inv_a, tmp2, u, inv_s):
    rows, tiles = dens.shape[0], dens.shape[1]
    _, outs, again, last = parts(tiles, inner)
    first_conv(inner, src, tmp, w_ref, tiles)

    def ring(c, carry):
        s = pl.ds(c * 4, 4)
        for start, end in outs:
            spread = jnp.log(conv_y(tmp, c * 4, 4, start, end - start))
            log_q = jnp.sum(wb[...] * spread, axis=2, keepdims=True)
            v[s, start:end] = jnp.exp(log_q - spread)
            inv_a[s, start:end] = jnp.exp(-spread)
        return carry

    lax.fori_loop(0, (rows + 8) // 4, ring, 0)
    clear_outside((v, inv_a), outs, not inner)
    conv_xz(v, tmp2, w_ref, 0, again)

    def second(c, carry):
        s = pl.ds(c * 4, 4)
        for start, end in last:
            inv = 1.0 / conv_y(tmp2, c * 4, 4, start, end - start)
            inv_s[s, start:end] = inv
            u[s, start:end] = dens[s, start:end] * inv
        return carry

    lax.fori_loop(0, rows // 4, second, 0)


def first_inner(w_ref, wb, dens, own, xa, xb, tmp, v, inv_a, tmp2, u, inv_s, big):
    join_rows(big, own, xa, xb)
    first_fields(True, wb, w_ref, dens, big, tmp, v, inv_a, tmp2, u, inv_s)


def first_outer(w_ref, wb, cot, dens, e, ya, yb, ca, cb, *rest):
    fields, dens_out, mean = rest[6:12], rest[12], rest[13]
    edges, (ends, sem) = rest[14:18], rest[18:]
    rows, tiles = dens.shape[0], dens.shape[1]
    kept = pltpu.make_async_copy(dens, dens_out, sem.at[0])
    kept.start()
    mean[...] = jnp.broadcast_to(centre(e), (K, L))
    join_ends(ends, rows, HALO, ya, yb, ca, cb)
    first_fields(False, wb, w_ref, dens, ends, *fields)
    give_edges(fields[4], edges)
    xa, xb, ya, yb = edges
    px, py = parities()
    row_a = pl.ds(pl.multiple_of((1 - px) * (rows - 8), 8), 8)
    row_b = pl.ds(pl.multiple_of(px * (rows - 8), 8), 8)
    for t in range(tiles):
        xa[HALO, t] = cot[row_a, t * L : (t + 1) * L]
        xb[HALO, t] = cot[row_b, t * L : (t + 1) * L]
    for out, side in ((ya, 1 - py), (yb, py)):
        for t in range(HT):
            lanes = pl.ds(pl.multiple_of((side * (tiles - HT) + t) * L, L), L)
            for b in range(rows // 8):
                out[rows + b, t] = cot[b * 8 : b * 8 + 8, lanes]
    kept.wait()


def second_fields(inner, wb, w_ref, mean, cots, own, inv_s, src, tmp, r, tmp2, bu, z, q, sums):
    rows, tiles = own.shape[0], own.shape[1]
    _, outs, again, last = parts(tiles, inner)
    first_conv(inner, src, tmp, w_ref, tiles)

    def ring(c, mine):
        acc_k = jnp.zeros((K, L), F32)
        acc_s = jnp.zeros((1, L), F32)
        for start, end in outs:
            spread = jnp.log(conv_y(tmp, c * 4, 4, start, end - start))
            log_q = jnp.sum(wb[...] * spread, axis=2, keepdims=True)
            ratio = wb[...] * jnp.exp(log_q - spread)
            for i in range(4):
                for t in range(start, end):
                    cell = cots[t + 2, pl.ds(c * 4 + i + 4, 1), :]
                    r[c * 4 + i, t] = ratio[i, t - start] * cell
                    if mine and 2 <= t < tiles + 2:
                        row_q = jnp.exp(log_q[i, t - start])
                        q[t - 2, pl.ds(c * 4 + i - 4, 1), :] = row_q[0:1]
                        combined = cell * row_q[0:1]
                        acc_s = acc_s + combined
                        acc_k = acc_k + combined * (spread[i, t - start] - mean)
        if mine:
            sums[0] += acc_k
            sums[1, 0:1] += acc_s

    ring(0, False)
    ring((rows + 4) // 4, False)

    def middle(c, carry):
        ring(c, True)
        return carry

    lax.fori_loop(1, (rows + 4) // 4, middle, 0)
    clear_outside((r,), outs, not inner)
    conv_xz(r, tmp2, w_ref, 0, again)

    def second(c, carry):
        s = pl.ds(c * 4, 4)
        for start, end in last:
            back = own[s, start:end] * conv_y(tmp2, c * 4, 4, start, end - start)
            bu[s, start:end] = back
            z[s, start:end] = back * inv_s[s, start:end]
        return carry

    lax.fori_loop(0, rows // 4, second, 0)


def second_inner(w_ref, wb, cot, inv_s, own, xa, xb, tmp, r, tmp2, bu, z, q, sums, big, cots):
    rows, tiles = own.shape[0], own.shape[1]
    join_rows(big, own, xa, xb)
    (row_a, row_b), _ = sides(rows, tiles)
    for t in range(tiles):
        cots[HT + t, HALO : HALO + rows] = cot[:, t * L : (t + 1) * L]
        cots[HT + t, pl.ds(pl.multiple_of(row_a, 8), 8)] = xa[HALO, t]
        cots[HT + t, pl.ds(pl.multiple_of(row_b, 8), 8)] = xb[HALO, t]
    sums[...] = jnp.zeros_like(sums)
    second_fields(True, wb, w_ref, centre(own), cots, own, inv_s, big, tmp, r, tmp2, bu, z, q, sums)


def second_outer(w_ref, wb, mass, cot, inv_s, own, xa, xb, ya, yb, ca, cb, *rest):
    tmp, r, tmp2, bu, z, q, sums = rest[7:14]
    told, edges, (ends, cots) = rest[14], rest[15:19], rest[19:]
    rows, tiles = own.shape[0], own.shape[1]
    slabs = xa.shape[0]
    join_ends(ends, rows, slabs, ya, yb, ca, cb)
    (row_a, row_b), (col_a, col_b) = sides(rows, tiles)
    row_a, row_b = pl.ds(pl.multiple_of(row_a, 8), 8), pl.ds(pl.multiple_of(row_b, 8), 8)
    for t in (0, 1, tiles - 2, tiles - 1):
        cots[HT + t, HALO : HALO + rows] = cot[:, t * L : (t + 1) * L]
        cots[HT + t, row_a] = xa[HALO, t]
        cots[HT + t, row_b] = xb[HALO, t]
    for col, y, c in ((col_a, ya, ca), (col_b, yb, cb)):
        for t in range(HT):
            for b in range(rows // 8):
                cots[col + t, HALO + b * 8 : HALO + b * 8 + 8] = y[rows + b, t]
            cots[col + t, row_a] = c[HALO, t]
            cots[col + t, row_b] = c[slabs + HALO, t]
    mean = centre(own)
    second_fields(False, wb, w_ref, mean, cots, own, inv_s, ends, tmp, r, tmp2, bu, z, q, sums)
    told[...] = in_lanes(over_lanes(mass[...]), over_lanes(sums[0]), over_lanes(sums[1, 0:1]), mean)
    give_edges(z, edges)


def third_fields(inner, wb, w_ref, mean, inv_a, v, e, bu, src, tmp, r, tmp2, gp, sums):
    rows, tiles = e.shape[0], e.shape[1]
    _, outs, again, last = parts(tiles, inner)
    first_conv(inner, src, tmp, w_ref, tiles)

    def ring(c, mine):
        s = pl.ds(c * 4, 4)
        for start, end in outs:
            back_v = -(v[s, start:end] * conv_y(tmp, c * 4, 4, start, end - start))
            combined = jnp.sum(back_v, axis=2, keepdims=True)
            inv = inv_a[s, start:end]
            r[s, start:end] = (wb[...] * combined - back_v) * inv
            if mine:
                low, high = max(start, 2) - start, min(end, tiles + 2) - start
                part = combined[:, low:high]
                sums[0] += jnp.sum(part * (-jnp.log(inv[:, low:high]) - mean), axis=(0, 1))
                sums[1, 0:1] += jnp.sum(part, axis=(0, 1))

    ring(0, False)
    ring((rows + 4) // 4, False)

    def middle(c, carry):
        ring(c, True)
        return carry

    lax.fori_loop(1, (rows + 4) // 4, middle, 0)
    conv_xz(r, tmp2, w_ref, 0, again)

    def second(c, carry):
        s = pl.ds(c * 4, 4)
        for start, end in last:
            gp[s, start:end] = bu[s, start:end] + e[s, start:end] * conv_y(tmp2, c * 4, 4, start, end - start)
        return carry

    lax.fori_loop(0, rows // 4, second, 0)


def third_inner(w_ref, wb, mean, inv_a, v, e, bu, own, xa, xb, tmp, r, tmp2, gp, sums, big):
    join_rows(big, own, xa, xb)
    sums[...] = jnp.zeros_like(sums)
    third_fields(True, wb, w_ref, mean[...], inv_a, v, e, bu, big, tmp, r, tmp2, gp, sums)


def third_outer(w_ref, wb, mean, before, inv_a, v, e, bu, q, ya, yb, ca, cb, *rest):
    tmp, r, tmp2, gp, sums = rest[5:10]
    gp_out, q_out, told, ends, sem = rest[10:]
    rows, tiles = e.shape[0], e.shape[1]
    middle = pl.ds(HT, tiles - 2 * HT)
    copies = [pltpu.make_async_copy(q, q_out, sem.at[0]), pltpu.make_async_copy(gp.at[:, middle], gp_out.at[:, middle], sem.at[1])]
    for c in copies:
        c.start()
    join_ends(ends, rows, HALO, ya, yb, ca, cb)
    third_fields(False, wb, w_ref, mean[...], inv_a, v, e, bu, ends, tmp, r, tmp2, gp, sums)
    for i, first in enumerate((0, tiles - HT)):
        lanes = pl.ds(first, HT)
        copies.append(pltpu.make_async_copy(gp.at[:, lanes], gp_out.at[:, lanes], sem.at[i + 2]))
        copies[-1].start()
    early = before[...]
    told[...] = in_lanes(
        *[early[:, i : i + 1] for i in range(4)], over_lanes(sums[0]), over_lanes(sums[1, 0:1]), mean[:, 0:1]
    )
    for c in copies:
        c.wait()


def last_kernel(cells, wb, heard, q, gp_far, dens_far, out, bary, theta_out, turn, gp, dens, sem):
    rows, tiles = gp.shape[0], gp.shape[1]
    loads = []
    for i, first in enumerate(range(0, tiles, 4)):
        lanes = pl.ds(first, 4)
        for j, (src, dst) in enumerate(((gp_far, gp), (dens_far, dens))):
            loads.append(pltpu.make_async_copy(src.at[:, lanes], dst.at[:, lanes], sem.at[tiles + 2 * i + j]))
            loads[-1].start()
    weights = wb[:, 0:1]
    everyone = heard[...]
    total = jnp.sum(everyone, axis=0)
    mass, late = total[:, 0:1], total[:, 2:3]
    shift_k = jnp.log(F32(cells)) - jnp.log(mass)
    shift = jnp.sum(weights * shift_k, axis=0, keepdims=True)
    scale = jnp.exp(shift)
    last = weights * (scale * late)
    grad_sums = last + (last - weights * jnp.sum(last, axis=0, keepdims=True))
    coef = jnp.broadcast_to(grad_sums / mass, (K, L))
    scale_all = jnp.broadcast_to(scale, (K, L))
    copies = []
    for t in range(tiles):

        def rows_of(c, carry):
            for i in range(8):
                x = c * 8 + i
                turn[t, pl.ds(x, K, stride=rows), :] = gp[x, t] * scale_all - dens[x, t] * coef
            return carry

        if t % 4 == 0:
            loads[t // 2].wait()
            loads[t // 2 + 1].wait()
        lax.fori_loop(0, rows // 8, rows_of, 0)
        copies.append(pltpu.make_async_copy(turn.at[t], out.at[:, pl.ds(t * L, L)], sem.at[t]))
        copies[-1].start()
        bary[:, t * L : (t + 1) * L] = q[t] * scale
    second = everyone[:, :, 1:2] + (everyone[:, :, 3:4] + (2.0 * shift_k - shift)) * everyone[:, :, 2:3]
    first = everyone[:, :, 4:5] + (everyone[:, :, 6:7] + shift_k) * everyone[:, :, 5:6]
    weight_grad = scale * jnp.sum(first + second, axis=0)
    grad = weights * (weight_grad - jnp.sum(weights * weight_grad, axis=0, keepdims=True))
    theta_out[...] = jnp.broadcast_to(grad, (K, L))
    for c in copies:
        c.wait()


def call(kernel, outs, scratch, semaphores, args, near_out=(), far_in=0, same=None):
    vmem, far = pl.BlockSpec(memory_space=pltpu.VMEM), pl.BlockSpec(memory_space=pl.ANY)
    near = len(args) - far_in
    args = [pltpu.with_memory_space_constraint(a, pltpu.VMEM if i < near else pltpu.HBM) for i, a in enumerate(args)]
    return pl.pallas_call(
        kernel,
        out_shape=outs,
        in_specs=[vmem] * near + [far] * far_in,
        out_specs=[far if i in near_out else vmem for i in range(len(outs))],
        scratch_shapes=[pltpu.VMEM(s, F32) for s in scratch] + [pltpu.SemaphoreType.DMA((n,)) for n in semaphores],
        input_output_aliases=same or {},
        compiler_params=pltpu.CompilerParams(vmem_limit_bytes=VMEM),
    )(*args)


def partners(axis, parity):
    count = lax.axis_size(axis)
    found = {}
    for i in range(count):
        j = i + 1 if i % 2 == parity else i - 1
        if 0 <= j < count:
            found[i] = j
    return found


def swap(value, axis, parity):
    return lax.ppermute(value, axis, list(partners(axis, parity).items()))


def exchange(xa, xb, ya, yb, tiles):
    rxa, rxb = swap(xa, "gx", 0), swap(xb, "gx", 1)
    rya, ryb = swap(ya, "gy", 0), swap(yb, "gy", 1)
    py = lax.rem(lax.axis_index("gy"), 2)

    def corner(side):
        first = side * (tiles - HT)
        return jnp.concatenate([lax.dynamic_slice_in_dim(r, first, HT, axis=1) for r in (rxa, rxb)], axis=0)

    rca, rcb = swap(corner(1 - py), "gy", 0), swap(corner(py), "gy", 1)
    return rxa, rxb, rya, ryb, rca, rcb


def over_all(told):
    devices = lax.axis_size("gx") * lax.axis_size("gy")
    return lax.all_to_all(jnp.broadcast_to(told[None], (devices, K, L)), ("gx", "gy"), 0, 0, tiled=True)


def shards(log_dens, theta, cotangent):
    _, rows, merged = log_dens.shape
    tiles = merged // L
    cells = lax.axis_size("gx") * lax.axis_size("gy") * rows * merged
    wb = jnp.broadcast_to(jax.nn.softmax(theta)[:, None], (K, L))
    w = jnp.asarray(depth_weights())

    field, ringed, big = (rows, tiles, K, L), (rows + 8, tiles + 4, K, L), (rows + 16, tiles, K, L)
    tmp, tmp2, ends = (rows + 8, tiles + 8, K, L), (rows, tiles + 4, K, L), (rows + 16, 2 * HT, K, L)
    acc, turn, small, cots, q_shape = (2, K, L), (tiles, K * rows, L), (K, L), (tiles + 8, rows + 16, L), (tiles, rows, L)

    def near(*shapes):
        return [pltpu.VMEM(s, F32) for s in shapes]

    def edges(more, more_y):
        return near(*[(HALO + more, tiles, K, L)] * 2, *[(rows + more_y, HT, K, L)] * 2)

    logs = log_dens.reshape(K * rows, merged)
    dens, e, mass, *sent = call(start_kernel, near(field, field, small) + edges(0, 0), [turn, (tiles, K, L)], [tiles], [logs], far_in=1)
    xa, xb, *others = exchange(*sent, tiles)
    held = [tmp, ringed, ringed, tmp2, field, field]
    held_now = call(first_inner, near(*held), [big], [], [w, wb, dens, e, xa, xb])
    _, v, inv_a, _, u, inv_s, dens_far, mean, *sent = call(
        first_outer, near(*held) + [pltpu.HBM(field, F32)] + near(small) + edges(1, rows // 8), [ends], [1],
        [w, wb, cotangent, dens, e, *others, *held_now], (6,), same={9 + i: i for i in range(6)},
    )
    xa, xb, *others = exchange(*sent, tiles)
    held = [tmp, ringed, tmp2, field, field, q_shape, acc]
    held_now = call(second_inner, near(*held), [big, cots], [], [w, wb, cotangent, inv_s, u, xa, xb])
    _, _, _, bu, z, q, _, told, *sent = call(
        second_outer, near(*held, small) + edges(0, 0), [ends, cots], [],
        [w, wb, mass, cotangent, inv_s, u, xa, xb, *others, *held_now], same={12 + i: i for i in range(7)},
    )
    xa, xb, *others = exchange(*sent, tiles)
    held = [tmp, ringed, tmp2, field, acc]
    held_now = call(third_inner, near(*held), [big], [], [w, wb, mean, inv_a, v, e, bu, z, xa, xb])
    *_, gp_far, q_far, told = call(
        third_outer, near(*held) + [pltpu.HBM(field, F32), pltpu.HBM(q_shape, F32)] + near(small), [ends], [4],
        [w, wb, mean, told, inv_a, v, e, bu, q, *others, *held_now], (5, 6), same={13 + i: i for i in range(5)},
    )
    plain = [jax.ShapeDtypeStruct(s, F32) for s in ((K * rows, merged), (rows, merged), small)]
    grad, bary, grad_theta = call(
        functools.partial(last_kernel, cells), plain, [turn, field, field], [tiles + tiles // 2],
        [wb, over_all(told), q_far, gp_far, dens_far], (0,), 2,
    )
    return bary, grad.reshape(K, rows, merged), grad_theta[:, 0]


def solution(mesh):
    placed = (P(None, "gx", "gy"), P(), P("gx", "gy"))
    return jax.shard_map(
        shards,
        mesh=mesh,
        in_specs=placed,
        out_specs=(P("gx", "gy"), P(None, "gx", "gy"), P()),
        check_vma=False,
    )
```

```python
import functools
import math

import jax
import jax.numpy as jnp
import numpy as np
from jax import lax
from jax.experimental import pallas as pl
from jax.experimental.pallas import tpu as pltpu
from jax.sharding import PartitionSpec as P

NZ = 64
K = 8
L = 128
HALO = 8
HT = HALO * NZ // L
VMEM = 14 * 1024 * 1024
F32 = jnp.float32
BF16 = jnp.bfloat16


def tap_list():
    raw_taps = [math.exp(-(offset * offset) / 8.0) for offset in range(-4, 5)]
    tap_total = 0.0
    for value in raw_taps:
        tap_total = tap_total + value
    return [value / tap_total for value in raw_taps]


G4, G3, G2, G1, G0 = tap_list()[:5]


def depth_weights():
    taps = tap_list()
    band = np.zeros((L, L), np.float32)
    for i in range(L):
        for j in range(L):
            if i // NZ == j // NZ and abs(i - j) <= 4:
                band[i, j] = taps[i - j + 4]
    high = band.astype(BF16)
    low = (band - high.astype(np.float32)).astype(BF16)
    half = np.concatenate([high, low], axis=1)
    return np.concatenate([half, half], axis=0)


def nine(at):
    return (G0 * at(4) + G1 * (at(3) + at(5))) + (G2 * (at(2) + at(6)) + G3 * (at(1) + at(7))) + G4 * (at(0) + at(8))


def conv_xz(src, dst, w_ref, shift, ranges):
    rows = dst.shape[0]

    def pair(i, first):
        t = first + 2 * i
        two = pl.ds(t, 2)
        for x in range(0, rows, 8):
            block = src[x : x + 16, pl.ds(t - shift, 2)]
            dst[x : x + 8, two] = nine(lambda j: block[j : j + 8])
        value = dst[:, two].reshape(rows * 2 * K, L)
        high = value.astype(BF16)
        low = (value - high.astype(F32)).astype(BF16)
        both = jnp.dot(jnp.concatenate([high, low], axis=1), w_ref[...], preferred_element_type=F32)
        dst[:, two] = (both[:, :L] + both[:, L:]).reshape(rows, 2, K, L)
        return first

    for first, end in ranges:
        lax.fori_loop(0, (end - first) // 2, pair, first)


def conv_y(src, first, rows, tile, n):
    value = src[pl.ds(first, rows), tile : tile + n + 4]
    flat = (rows * (n + 3) * K, L)
    lane = lax.broadcasted_iota(jnp.int32, flat, 1)
    mixed = jnp.where(lane < NZ, value[:, 1:].reshape(flat), value[:, :-1].reshape(flat))
    odd = pltpu.roll(mixed, NZ, axis=1).reshape(rows, n + 3, K, L)
    return (G0 * value[:, 2 : n + 2] + G1 * (odd[:, 1 : n + 1] + odd[:, 2 : n + 2])) + (
        G2 * (value[:, 1 : n + 1] + value[:, 3 : n + 3]) + G3 * (odd[:, 0:n] + odd[:, 3 : n + 3])
    ) + G4 * (value[:, 0:n] + value[:, 4 : n + 4])


def parities():
    return lax.rem(lax.axis_index("gx"), 2), lax.rem(lax.axis_index("gy"), 2)


def sides(rows, tiles):
    px, py = parities()
    return ((1 - px) * (rows + HALO), px * (rows + HALO)), ((1 - py) * (tiles + HT), py * (tiles + HT))


def join_rows(big, own, xa, xb):
    rows = own.shape[0]
    (row_a, row_b), _ = sides(rows, own.shape[1])
    big[HALO : HALO + rows] = own[...]
    big[pl.ds(row_a, HALO)] = xa[0:HALO]
    big[pl.ds(row_b, HALO)] = xb[0:HALO]


def join_ends(ends, rows, slabs, ya, yb, ca, cb):
    (row_a, row_b), _ = sides(rows, 0)
    _, py = parities()
    for col, y, c in (((1 - py) * HT, ya, ca), (py * HT, yb, cb)):
        lanes = pl.ds(col, HT)
        ends[pl.ds(HALO, rows), lanes] = y[0:rows]
        ends[pl.ds(row_b, HALO), lanes] = c[0:HALO]
        ends[pl.ds(row_a, HALO), lanes] = c[slabs : slabs + HALO]


def give_edges(own, outs):
    xa, xb, ya, yb = outs
    rows, tiles = own.shape[0], own.shape[1]
    px, py = parities()
    xa[0:HALO] = own[pl.ds((1 - px) * (rows - HALO), HALO)]
    xb[0:HALO] = own[pl.ds(px * (rows - HALO), HALO)]
    ya[0:rows] = own[:, pl.ds((1 - py) * (tiles - HT), HT)]
    yb[0:rows] = own[:, pl.ds(py * (tiles - HT), HT)]


def clear_outside(fields, ranges, ends):
    rows, tiles = fields[0].shape[0], fields[0].shape[1]
    gx, gy = lax.axis_index("gx"), lax.axis_index("gy")

    def zero(first, count, ts):
        def write():
            for f in fields:
                for start, end in ts:
                    f[first : first + count, start:end] = jnp.zeros((count, end - start, K, L), F32)

        return write

    pl.when(gx == 0)(zero(0, 4, ranges))
    pl.when(gx == lax.axis_size("gx") - 1)(zero(rows - 4, 4, ranges))
    if ends:
        pl.when(gy == 0)(zero(0, rows, [(0, 2)]))
        pl.when(gy == lax.axis_size("gy") - 1)(zero(0, rows, [(tiles - 2, tiles)]))


def parts(tiles, inner):
    if inner:
        return [(HT, tiles + HT)], [(HT, tiles)], [(HT, tiles)], [(HT, tiles - HT)]
    return (
        [(0, HT), (tiles + HT, tiles + 2 * HT)],
        [(0, HT), (tiles, tiles + HT)],
        [(0, HT), (tiles, tiles + HT)],
        [(0, HT), (tiles - HT, tiles)],
    )


def first_conv(inner, src, tmp, w_ref, tiles):
    whole = parts(tiles, inner)[0]
    if inner:
        conv_xz(src, tmp, w_ref, HT, whole)
    else:
        conv_xz(src, tmp, w_ref, 0, whole[:1])
        conv_xz(src, tmp, w_ref, tiles, whole[1:])


def inside(at, count):
    total = jnp.zeros(at.shape, F32)
    for offset, tap in zip(range(-4, 5), tap_list()):
        total = total + jnp.where((at + offset >= 0) & (at + offset < count), F32(tap), F32(0.0))
    return total


def in_lanes(*columns):
    lane = lax.broadcasted_iota(jnp.int32, (K, L), 1)
    out = jnp.zeros((K, L), F32)
    for i, c in enumerate(columns):
        out = jnp.where(lane == i, c, out)
    return out


def over_lanes(value):
    return jnp.sum(value, axis=1, keepdims=True)


def centre(field):
    return jnp.log(over_lanes(field[field.shape[0] // 2, field.shape[1] // 2]) * (1.0 / L))


def start_kernel(theta, log_ref, dens, e, mass, wb, *rest):
    edges, (turn, across, sem) = rest[:4], rest[4:]
    rows, tiles = dens.shape[0], dens.shape[1]
    loads = [pltpu.make_async_copy(log_ref.at[:, pl.ds(t * L, L)], turn.at[t], sem.at[t]) for t in range(tiles)]
    for c in loads:
        c.start()
    density = lax.broadcasted_iota(jnp.int32, (K, L), 0)
    lane = lax.broadcasted_iota(jnp.int32, (K, L), 1)
    logits = jnp.zeros((K, L), F32)
    for k in range(K):
        logits = jnp.where(density == k, theta[k], logits)
    powers = jnp.exp(logits - jnp.max(logits, axis=0, keepdims=True))
    wb[...] = powers / jnp.sum(powers, axis=0, keepdims=True)
    depth = inside(lane % NZ, NZ)
    first = lax.axis_index("gy") * (tiles * L // NZ)

    def factor(x, carry):
        across[x] = 1.0 / inside(jnp.full((K, L), lax.axis_index("gx") * rows + x), lax.axis_size("gx") * rows)
        return carry

    lax.fori_loop(0, rows, factor, 0)
    mass[...] = jnp.zeros((K, L), F32)
    for t in range(tiles):
        along = inside(first + t * (L // NZ) + lane // NZ, lax.axis_size("gy") * (tiles * L // NZ))
        around = 1.0 / (along * depth)
        loads[t].wait()

        def some(c, acc):
            for i in range(8):
                x = c * 8 + i
                d = jnp.exp(turn[t, pl.ds(x, K, stride=rows), :])
                dens[x, t] = d
                e[x, t] = d * (around * across[x])
                acc = acc + d
            return acc

        mass[...] += lax.fori_loop(0, rows // 8, some, jnp.zeros((K, L), F32))
    give_edges(e, edges)


def first_fields(inner, wb, w_ref, dens, src, tmp, v, inv_a, tmp2, u, inv_s):
    rows, tiles = dens.shape[0], dens.shape[1]
    _, outs, again, last = parts(tiles, inner)
    first_conv(inner, src, tmp, w_ref, tiles)

    def ring(c, carry):
        s = pl.ds(c * 4, 4)
        for start, end in outs:
            spread = jnp.log(conv_y(tmp, c * 4, 4, start, end - start))
            log_q = jnp.sum(wb[...] * spread, axis=2, keepdims=True)
            v[s, start:end] = jnp.exp(log_q - spread)
            inv_a[s, start:end] = jnp.exp(-spread)
        return carry

    lax.fori_loop(0, (rows + 8) // 4, ring, 0)
    clear_outside((v, inv_a), outs, not inner)
    conv_xz(v, tmp2, w_ref, 0, again)

    def second(c, carry):
        s = pl.ds(c * 4, 4)
        for start, end in last:
            inv = 1.0 / conv_y(tmp2, c * 4, 4, start, end - start)
            inv_s[s, start:end] = inv
            u[s, start:end] = dens[s, start:end] * inv
        return carry

    lax.fori_loop(0, rows // 4, second, 0)


def first_inner(w_ref, wb, dens, own, xb, xa, tmp, v, inv_a, tmp2, u, inv_s, big):
    join_rows(big, own, xa, xb)
    first_fields(True, wb, w_ref, dens, big, tmp, v, inv_a, tmp2, u, inv_s)


def first_outer(w_ref, wb, cot, dens, e, yb, ya, cb, ca, *rest):
    fields, dens_out, mean = rest[6:12], rest[12], rest[13]
    edges, (ends, sem) = rest[14:18], rest[18:]
    rows, tiles = dens.shape[0], dens.shape[1]
    kept = pltpu.make_async_copy(dens, dens_out, sem.at[0])
    kept.start()
    mean[...] = jnp.broadcast_to(centre(e), (K, L))
    join_ends(ends, rows, HALO, ya, yb, ca, cb)
    first_fields(False, wb, w_ref, dens, ends, *fields)
    give_edges(fields[4], edges)
    xa, xb, ya, yb = edges
    px, py = parities()
    row_a = pl.ds(pl.multiple_of((1 - px) * (rows - 8), 8), 8)
    row_b = pl.ds(pl.multiple_of(px * (rows - 8), 8), 8)
    for t in range(tiles):
        xa[HALO, t] = cot[row_a, t * L : (t + 1) * L]
        xb[HALO, t] = cot[row_b, t * L : (t + 1) * L]
    for out, side in ((ya, 1 - py), (yb, py)):
        for t in range(HT):
            lanes = pl.ds(pl.multiple_of((side * (tiles - HT) + t) * L, L), L)
            for b in range(rows // 8):
                out[rows + b, t] = cot[b * 8 : b * 8 + 8, lanes]
    kept.wait()


def second_fields(inner, wb, w_ref, mean, cots, own, inv_s, src, tmp, r, tmp2, bu, z, q, sums):
    rows, tiles = own.shape[0], own.shape[1]
    _, outs, again, last = parts(tiles, inner)
    first_conv(inner, src, tmp, w_ref, tiles)

    def ring(c, mine):
        acc_k = jnp.zeros((K, L), F32)
        acc_s = jnp.zeros((1, L), F32)
        for start, end in outs:
            spread = jnp.log(conv_y(tmp, c * 4, 4, start, end - start))
            log_q = jnp.sum(wb[...] * spread, axis=2, keepdims=True)
            ratio = wb[...] * jnp.exp(log_q - spread)
            for i in range(4):
                for t in range(start, end):
                    cell = cots[t + 2, pl.ds(c * 4 + i + 4, 1), :]
                    r[c * 4 + i, t] = ratio[i, t - start] * cell
                    if mine and 2 <= t < tiles + 2:
                        row_q = jnp.exp(log_q[i, t - start])
                        q[t - 2, pl.ds(c * 4 + i - 4, 1), :] = row_q[0:1]
                        combined = cell * row_q[0:1]
                        acc_s = acc_s + combined
                        acc_k = acc_k + combined * (spread[i, t - start] - mean)
        if mine:
            sums[0] += acc_k
            sums[1, 0:1] += acc_s

    ring(0, False)
    ring((rows + 4) // 4, False)

    def middle(c, carry):
        ring(c, True)
        return carry

    lax.fori_loop(1, (rows + 4) // 4, middle, 0)
    clear_outside((r,), outs, not inner)
    conv_xz(r, tmp2, w_ref, 0, again)

    def second(c, carry):
        s = pl.ds(c * 4, 4)
        for start, end in last:
            back = own[s, start:end] * conv_y(tmp2, c * 4, 4, start, end - start)
            bu[s, start:end] = back
            z[s, start:end] = back * inv_s[s, start:end]
        return carry

    lax.fori_loop(0, rows // 4, second, 0)


def second_inner(w_ref, wb, cot, inv_s, own, xb, xa, tmp, r, tmp2, bu, z, q, sums, big, cots):
    rows, tiles = own.shape[0], own.shape[1]
    join_rows(big, own, xa, xb)
    (row_a, row_b), _ = sides(rows, tiles)
    for t in range(tiles):
        cots[HT + t, HALO : HALO + rows] = cot[:, t * L : (t + 1) * L]
        cots[HT + t, pl.ds(pl.multiple_of(row_a, 8), 8)] = xa[HALO, t]
        cots[HT + t, pl.ds(pl.multiple_of(row_b, 8), 8)] = xb[HALO, t]
    sums[...] = jnp.zeros_like(sums)
    second_fields(True, wb, w_ref, centre(own), cots, own, inv_s, big, tmp, r, tmp2, bu, z, q, sums)


def second_outer(w_ref, wb, mass, cot, inv_s, own, xb, xa, yb, ya, cb, ca, *rest):
    tmp, r, tmp2, bu, z, q, sums = rest[7:14]
    told, edges, (ends, cots) = rest[14], rest[15:19], rest[19:]
    rows, tiles = own.shape[0], own.shape[1]
    slabs = xa.shape[0]
    join_ends(ends, rows, slabs, ya, yb, ca, cb)
    (row_a, row_b), (col_a, col_b) = sides(rows, tiles)
    row_a, row_b = pl.ds(pl.multiple_of(row_a, 8), 8), pl.ds(pl.multiple_of(row_b, 8), 8)
    for t in (0, 1, tiles - 2, tiles - 1):
        cots[HT + t, HALO : HALO + rows] = cot[:, t * L : (t + 1) * L]
        cots[HT + t, row_a] = xa[HALO, t]
        cots[HT + t, row_b] = xb[HALO, t]
    for col, y, c in ((col_a, ya, ca), (col_b, yb, cb)):
        for t in range(HT):
            for b in range(rows // 8):
                cots[col + t, HALO + b * 8 : HALO + b * 8 + 8] = y[rows + b, t]
            cots[col + t, row_b] = c[HALO, t]
            cots[col + t, row_a] = c[slabs + HALO, t]
    mean = centre(own)
    second_fields(False, wb, w_ref, mean, cots, own, inv_s, ends, tmp, r, tmp2, bu, z, q, sums)
    told[...] = in_lanes(over_lanes(mass[...]), over_lanes(sums[0]), over_lanes(sums[1, 0:1]), mean)
    give_edges(z, edges)


def third_fields(inner, wb, w_ref, mean, inv_a, v, e, bu, src, tmp, r, tmp2, gp, sums):
    rows, tiles = e.shape[0], e.shape[1]
    _, outs, again, last = parts(tiles, inner)
    first_conv(inner, src, tmp, w_ref, tiles)

    def ring(c, mine):
        s = pl.ds(c * 4, 4)
        for start, end in outs:
            back_v = -(v[s, start:end] * conv_y(tmp, c * 4, 4, start, end - start))
            combined = jnp.sum(back_v, axis=2, keepdims=True)
            inv = inv_a[s, start:end]
            r[s, start:end] = (wb[...] * combined - back_v) * inv
            if mine:
                low, high = max(start, 2) - start, min(end, tiles + 2) - start
                part = combined[:, low:high]
                sums[0] += jnp.sum(part * (-jnp.log(inv[:, low:high]) - mean), axis=(0, 1))
                sums[1, 0:1] += jnp.sum(part, axis=(0, 1))

    ring(0, False)
    ring((rows + 4) // 4, False)

    def middle(c, carry):
        ring(c, True)
        return carry

    lax.fori_loop(1, (rows + 4) // 4, middle, 0)
    conv_xz(r, tmp2, w_ref, 0, again)

    def second(c, carry):
        s = pl.ds(c * 4, 4)
        for start, end in last:
            gp[s, start:end] = bu[s, start:end] + e[s, start:end] * conv_y(tmp2, c * 4, 4, start, end - start)
        return carry

    lax.fori_loop(0, rows // 4, second, 0)


def third_inner(w_ref, wb, mean, inv_a, v, e, bu, own, xb, xa, tmp, r, tmp2, gp, sums, big):
    join_rows(big, own, xa, xb)
    sums[...] = jnp.zeros_like(sums)
    third_fields(True, wb, w_ref, mean[...], inv_a, v, e, bu, big, tmp, r, tmp2, gp, sums)


def third_outer(w_ref, wb, mean, before, inv_a, v, e, bu, q, yb, ya, cb, ca, *rest):
    tmp, r, tmp2, gp, sums = rest[5:10]
    gp_out, q_out, told, ends, sem = rest[10:]
    rows, tiles = e.shape[0], e.shape[1]
    middle = pl.ds(HT, tiles - 2 * HT)
    copies = [pltpu.make_async_copy(q, q_out, sem.at[0]), pltpu.make_async_copy(gp.at[:, middle], gp_out.at[:, middle], sem.at[1])]
    for c in copies:
        c.start()
    join_ends(ends, rows, HALO, ya, yb, ca, cb)
    third_fields(False, wb, w_ref, mean[...], inv_a, v, e, bu, ends, tmp, r, tmp2, gp, sums)
    for i, first in enumerate((0, tiles - HT)):
        lanes = pl.ds(first, HT)
        copies.append(pltpu.make_async_copy(gp.at[:, lanes], gp_out.at[:, lanes], sem.at[i + 2]))
        copies[-1].start()
    early = before[...]
    told[...] = in_lanes(
        *[early[:, i : i + 1] for i in range(4)], over_lanes(sums[0]), over_lanes(sums[1, 0:1]), mean[:, 0:1]
    )
    for c in copies:
        c.wait()


def last_kernel(cells, wb, heard, q, gp_far, dens_far, out, bary, theta_out, turn, gp, dens, sem):
    rows, tiles = gp.shape[0], gp.shape[1]
    loads = []
    for i, first in enumerate(range(0, tiles, 4)):
        lanes = pl.ds(first, 4)
        for j, (src, dst) in enumerate(((gp_far, gp), (dens_far, dens))):
            loads.append(pltpu.make_async_copy(src.at[:, lanes], dst.at[:, lanes], sem.at[tiles + 2 * i + j]))
            loads[-1].start()
    weights = wb[:, 0:1]
    everyone = heard[...]
    total = jnp.sum(everyone, axis=0)
    mass, late = total[:, 0:1], total[:, 2:3]
    shift_k = jnp.log(F32(cells)) - jnp.log(mass)
    shift = jnp.sum(weights * shift_k, axis=0, keepdims=True)
    scale = jnp.exp(shift)
    last = weights * (scale * late)
    grad_sums = last + (last - weights * jnp.sum(last, axis=0, keepdims=True))
    coef = jnp.broadcast_to(grad_sums / mass, (K, L))
    scale_all = jnp.broadcast_to(scale, (K, L))
    copies = []
    for t in range(tiles):

        def rows_of(c, carry):
            for i in range(8):
                x = c * 8 + i
                turn[t, pl.ds(x, K, stride=rows), :] = gp[x, t] * scale_all - dens[x, t] * coef
            return carry

        if t % 4 == 0:
            loads[t // 2].wait()
            loads[t // 2 + 1].wait()
        lax.fori_loop(0, rows // 8, rows_of, 0)
        copies.append(pltpu.make_async_copy(turn.at[t], out.at[:, pl.ds(t * L, L)], sem.at[t]))
        copies[-1].start()
        bary[:, t * L : (t + 1) * L] = q[t] * scale
    second = everyone[:, :, 1:2] + (everyone[:, :, 3:4] + (2.0 * shift_k - shift)) * everyone[:, :, 2:3]
    first = everyone[:, :, 4:5] + (everyone[:, :, 6:7] + shift_k) * everyone[:, :, 5:6]
    weight_grad = scale * jnp.sum(first + second, axis=0)
    grad = weights * (weight_grad - jnp.sum(weights * weight_grad, axis=0, keepdims=True))
    theta_out[...] = jnp.broadcast_to(grad, (K, L))
    for c in copies:
        c.wait()


def call(kernel, outs, scratch, semaphores, args, near_out=(), far_in=0, same=None, numbers=()):
    vmem, far = pl.BlockSpec(memory_space=pltpu.VMEM), pl.BlockSpec(memory_space=pl.ANY)
    near = len(args) - far_in
    args = [pltpu.with_memory_space_constraint(a, pltpu.VMEM if i < near else pltpu.HBM) for i, a in enumerate(args)]
    return pl.pallas_call(
        kernel,
        out_shape=outs,
        in_specs=[pl.BlockSpec(memory_space=pltpu.SMEM)] * len(numbers) + [vmem] * near + [far] * far_in,
        out_specs=[far if i in near_out else vmem for i in range(len(outs))],
        scratch_shapes=[pltpu.VMEM(s, F32) for s in scratch] + [pltpu.SemaphoreType.DMA((n,)) for n in semaphores],
        input_output_aliases=same or {},
        compiler_params=pltpu.CompilerParams(vmem_limit_bytes=VMEM),
    )(*numbers, *args)


def partners(axis, parity):
    count = lax.axis_size(axis)
    found = {}
    for i in range(count):
        j = i + 1 if i % 2 == parity else i - 1
        if 0 <= j < count:
            found[i] = j
    return found


def swap(value, axis, parity):
    return lax.ppermute(value, axis, list(partners(axis, parity).items()))


def exchange(xa, xb, ya, yb, tiles):
    rxb, ryb = swap(xb, "gx", 1), swap(yb, "gy", 1)
    rxa, rya = swap(xa, "gx", 0), swap(ya, "gy", 0)
    py = lax.rem(lax.axis_index("gy"), 2)

    def corner(side):
        first = side * (tiles - HT)
        return jnp.concatenate([lax.dynamic_slice_in_dim(r, first, HT, axis=1) for r in (rxb, rxa)], axis=0)

    rcb = swap(corner(py), "gy", 1)
    rca = swap(corner(1 - py), "gy", 0)
    return rxa, rxb, ryb, rya, rcb, rca


def over_all(told):
    devices = lax.axis_size("gx") * lax.axis_size("gy")
    return lax.all_to_all(jnp.broadcast_to(told[None], (devices, K, L)), ("gx", "gy"), 0, 0, tiled=True)


def shards(log_dens, theta, cotangent):
    _, rows, merged = log_dens.shape
    tiles = merged // L
    cells = lax.axis_size("gx") * lax.axis_size("gy") * rows * merged
    w = jnp.asarray(depth_weights())

    field, ringed, big = (rows, tiles, K, L), (rows + 8, tiles + 4, K, L), (rows + 16, tiles, K, L)
    tmp, tmp2, ends = (rows + 8, tiles + 8, K, L), (rows, tiles + 4, K, L), (rows + 16, 2 * HT, K, L)
    acc, turn, small, cots, q_shape = (2, K, L), (tiles, K * rows, L), (K, L), (tiles + 8, rows + 16, L), (tiles, rows, L)

    def near(*shapes):
        return [pltpu.VMEM(s, F32) for s in shapes]

    def edges(more, more_y):
        return near(*[(HALO + more, tiles, K, L)] * 2, *[(rows + more_y, HT, K, L)] * 2)

    logs = log_dens.reshape(K * rows, merged)
    dens, e, mass, wb, *sent = call(
        start_kernel, near(field, field, small, small) + edges(0, 0), [turn, (rows, K, L)], [tiles], [logs], far_in=1, numbers=(theta,)
    )
    xa, xb, *others = exchange(*sent, tiles)
    held = [tmp, ringed, ringed, tmp2, field, field]
    held_now = call(first_inner, near(*held), [big], [], [w, wb, dens, e, xb, xa])
    _, v, inv_a, _, u, inv_s, dens_far, mean, *sent = call(
        first_outer, near(*held) + [pltpu.HBM(field, F32)] + near(small) + edges(1, rows // 8), [ends], [1],
        [w, wb, cotangent, dens, e, *others, *held_now], (6,), same={9 + i: i for i in range(6)},
    )
    xa, xb, *others = exchange(*sent, tiles)
    held = [tmp, ringed, tmp2, field, field, q_shape, acc]
    held_now = call(second_inner, near(*held), [big, cots], [], [w, wb, cotangent, inv_s, u, xb, xa])
    _, _, _, bu, z, q, _, told, *sent = call(
        second_outer, near(*held, small) + edges(0, 0), [ends, cots], [],
        [w, wb, mass, cotangent, inv_s, u, xb, xa, *others, *held_now], same={12 + i: i for i in range(7)},
    )
    xa, xb, *others = exchange(*sent, tiles)
    held = [tmp, ringed, tmp2, field, acc]
    held_now = call(third_inner, near(*held), [big], [], [w, wb, mean, inv_a, v, e, bu, z, xb, xa])
    *_, gp_far, q_far, told = call(
        third_outer, near(*held) + [pltpu.HBM(field, F32), pltpu.HBM(q_shape, F32)] + near(small), [ends], [4],
        [w, wb, mean, told, inv_a, v, e, bu, q, *others, *held_now], (5, 6), same={13 + i: i for i in range(5)},
    )
    plain = [jax.ShapeDtypeStruct(s, F32) for s in ((K * rows, merged), (rows, merged), small)]
    grad, bary, grad_theta = call(
        functools.partial(last_kernel, cells), plain, [turn, field, field], [tiles + tiles // 2],
        [wb, over_all(told), q_far, gp_far, dens_far], (0,), 2,
    )
    return bary, grad.reshape(K, rows, merged), grad_theta[:, 0]


def solution(mesh):
    placed = (P(None, "gx", "gy"), P(), P("gx", "gy"))
    return jax.shard_map(
        shards,
        mesh=mesh,
        in_specs=placed,
        out_specs=(P("gx", "gy"), P(None, "gx", "gy"), P()),
        check_vma=False,
    )
```

```python
import functools
import math

import jax
import jax.numpy as jnp
import numpy as np
from jax import lax
from jax.experimental import pallas as pl
from jax.experimental.pallas import tpu as pltpu
from jax.sharding import PartitionSpec as P

NZ = 64
K = 8
L = 128
HALO = 8
HT = HALO * NZ // L
VMEM = 14 * 1024 * 1024
F32 = jnp.float32
BF16 = jnp.bfloat16


def tap_list():
    raw_taps = [math.exp(-(offset * offset) / 8.0) for offset in range(-4, 5)]
    tap_total = 0.0
    for value in raw_taps:
        tap_total = tap_total + value
    return [value / tap_total for value in raw_taps]


G4, G3, G2, G1, G0 = tap_list()[:5]


def depth_weights():
    taps = tap_list()
    band = np.zeros((L, L), np.float32)
    for i in range(L):
        for j in range(L):
            if i // NZ == j // NZ and abs(i - j) <= 4:
                band[i, j] = taps[i - j + 4]
    high = band.astype(BF16)
    low = (band - high.astype(np.float32)).astype(BF16)
    half = np.concatenate([high, low], axis=1)
    return np.concatenate([half, half], axis=0)


def nine(at):
    return (G0 * at(4) + G1 * (at(3) + at(5))) + (G2 * (at(2) + at(6)) + G3 * (at(1) + at(7))) + G4 * (at(0) + at(8))


def conv_xz(src, dst, w_ref, pieces):
    rows = dst.shape[0]

    def some(now):
        for t, u in now:
            along = []
            for i in range(4):
                for x in range(0, rows, 8):
                    block = src[x : x + 16, u + i]
                    along.append(nine(lambda j: block[j : j + 8]).reshape(8 * K, L))
            value = jnp.concatenate(along, axis=0)
            high = value.astype(BF16)
            low = (value - high.astype(F32)).astype(BF16)
            both = jnp.dot(jnp.concatenate([high, low], axis=1), w_ref[...], preferred_element_type=F32)
            out = both[:, :L] + both[:, L:]
            for i in range(4):
                dst[:, t + i] = out[i * rows * K : (i + 1) * rows * K].reshape(rows, K, L)

    if len(pieces) < 4:
        some(pieces)
    else:

        def two(i, carry):
            some([(t + 8 * i, u + 8 * i) for t, u in pieces[:2]])
            return carry

        lax.fori_loop(0, len(pieces) // 2, two, 0)


def conv_y(src, first, rows, tile, n):
    value = src[pl.ds(first, rows), tile : tile + n + 4]
    flat = (rows * (n + 3) * K, L)
    lane = lax.broadcasted_iota(jnp.int32, flat, 1)
    mixed = jnp.where(lane < NZ, value[:, 1:].reshape(flat), value[:, :-1].reshape(flat))
    odd = pltpu.roll(mixed, NZ, axis=1).reshape(rows, n + 3, K, L)
    return (G0 * value[:, 2 : n + 2] + G1 * (odd[:, 1 : n + 1] + odd[:, 2 : n + 2])) + (
        G2 * (value[:, 1 : n + 1] + value[:, 3 : n + 3]) + G3 * (odd[:, 0:n] + odd[:, 3 : n + 3])
    ) + G4 * (value[:, 0:n] + value[:, 4 : n + 4])


def parities():
    return lax.rem(lax.axis_index("gx"), 2), lax.rem(lax.axis_index("gy"), 2)


def sides(rows, tiles):
    px, py = parities()
    return ((1 - px) * (rows + HALO), px * (rows + HALO)), ((1 - py) * (tiles + HT), py * (tiles + HT))


def join_rows(big, own, xa, xb):
    rows = own.shape[0]
    (row_a, row_b), _ = sides(rows, own.shape[1])
    big[HALO : HALO + rows] = own[...]
    big[pl.ds(row_a, HALO)] = xa[0:HALO]
    big[pl.ds(row_b, HALO)] = xb[0:HALO]


def join_ends(ends, rows, slabs, ya, yb, ca, cb):
    (row_a, row_b), _ = sides(rows, 0)
    _, py = parities()
    for col, y, c in (((1 - py) * HT, ya, ca), (py * HT, yb, cb)):
        lanes = pl.ds(col, HT)
        ends[pl.ds(HALO, rows), lanes] = y[0:rows]
        ends[pl.ds(row_b, HALO), lanes] = c[0:HALO]
        ends[pl.ds(row_a, HALO), lanes] = c[slabs : slabs + HALO]


def give_edges(own, outs):
    xa, xb, ya, yb = outs
    rows, tiles = own.shape[0], own.shape[1]
    px, py = parities()
    xa[0:HALO] = own[pl.ds((1 - px) * (rows - HALO), HALO)]
    xb[0:HALO] = own[pl.ds(px * (rows - HALO), HALO)]
    ya[0:rows] = own[:, pl.ds((1 - py) * (tiles - HT), HT)]
    yb[0:rows] = own[:, pl.ds(py * (tiles - HT), HT)]


def clear_outside(fields, ranges, ends):
    rows, tiles = fields[0].shape[0], fields[0].shape[1]
    gx, gy = lax.axis_index("gx"), lax.axis_index("gy")

    def zero(first, count, ts):
        def write():
            for f in fields:
                for start, end in ts:
                    f[first : first + count, start:end] = jnp.zeros((count, end - start, K, L), F32)

        return write

    pl.when(gx == 0)(zero(0, 4, ranges))
    pl.when(gx == lax.axis_size("gx") - 1)(zero(rows - 4, 4, ranges))
    if ends:
        pl.when(gy == 0)(zero(0, rows, [(0, 2)]))
        pl.when(gy == lax.axis_size("gy") - 1)(zero(0, rows, [(tiles - 2, tiles)]))


def parts(tiles, inner):
    if inner:
        starts, outs, last = range(HT, tiles + HT, 4), [(HT, tiles)], [(HT, tiles - HT)]
        again = range(HT, tiles, 4)
        return [(t, t - HT) for t in starts], outs, [(t, t) for t in again], last
    outs, last = [(0, HT), (tiles, tiles + HT)], [(0, HT), (tiles - HT, tiles)]
    return [(0, 0), (tiles + HT, HT)], outs, [(0, 0), (tiles, tiles)], last


def inside(at, count):
    total = jnp.zeros(at.shape, F32)
    for offset, tap in zip(range(-4, 5), tap_list()):
        total = total + jnp.where((at + offset >= 0) & (at + offset < count), F32(tap), F32(0.0))
    return total


def in_lanes(*columns):
    lane = lax.broadcasted_iota(jnp.int32, (K, L), 1)
    out = jnp.zeros((K, L), F32)
    for i, c in enumerate(columns):
        out = jnp.where(lane == i, c, out)
    return out


def over_lanes(value):
    return jnp.sum(value, axis=1, keepdims=True)


def centre(field):
    return jnp.log(over_lanes(field[field.shape[0] // 2, field.shape[1] // 2]) * (1.0 / L))


def start_kernel(theta, log_ref, dens_out, e, mass, wb, *rest):
    edges, (turn, across, dens, sem) = rest[:4], rest[4:]
    rows, tiles = dens.shape[0], dens.shape[1]
    loads = [pltpu.make_async_copy(log_ref.at[:, pl.ds(t * L, L)], turn.at[t], sem.at[t]) for t in range(tiles)]
    for c in loads:
        c.start()
    density = lax.broadcasted_iota(jnp.int32, (K, L), 0)
    lane = lax.broadcasted_iota(jnp.int32, (K, L), 1)
    logits = jnp.zeros((K, L), F32)
    for k in range(K):
        logits = jnp.where(density == k, theta[k], logits)
    powers = jnp.exp(logits - jnp.max(logits, axis=0, keepdims=True))
    wb[...] = powers / jnp.sum(powers, axis=0, keepdims=True)
    depth = inside(lane % NZ, NZ)
    first = lax.axis_index("gy") * (tiles * L // NZ)

    def factor(x, carry):
        across[x] = 1.0 / inside(jnp.full((K, L), lax.axis_index("gx") * rows + x), lax.axis_size("gx") * rows)
        return carry

    lax.fori_loop(0, rows, factor, 0)
    mass[...] = jnp.zeros((K, L), F32)
    for t in range(tiles):
        along = inside(first + t * (L // NZ) + lane // NZ, lax.axis_size("gy") * (tiles * L // NZ))
        around = 1.0 / (along * depth)
        loads[t].wait()

        def some(c, acc):
            for i in range(8):
                x = c * 8 + i
                d = jnp.exp(turn[t, pl.ds(x, K, stride=rows), :])
                dens[x, t] = d
                e[x, t] = d * (around * across[x])
                acc = acc + d
            return acc

        mass[...] += lax.fori_loop(0, rows // 8, some, jnp.zeros((K, L), F32))
        pltpu.make_async_copy(dens.at[:, t], dens_out.at[:, t], sem.at[tiles]).start()
    give_edges(e, edges)
    pltpu.make_async_copy(dens, dens_out, sem.at[tiles]).wait()


def first_fields(inner, wb, w_ref, dens, src, tmp, v, inv_a, tmp2, u, inv_s):
    rows, tiles = dens.shape[0], dens.shape[1]
    first, outs, again, last = parts(tiles, inner)
    conv_xz(src, tmp, w_ref, first)

    def ring(c, carry):
        s = pl.ds(c * 8, 8)
        for start, end in outs:
            spread = jnp.log(conv_y(tmp, c * 8, 8, start, end - start))
            log_q = jnp.sum(wb[...] * spread, axis=2, keepdims=True)
            v[s, start:end] = jnp.exp(log_q - spread)
            inv_a[s, start:end] = jnp.exp(-spread)
        return carry

    lax.fori_loop(0, (rows + 8) // 8, ring, 0)
    clear_outside((v, inv_a), outs, not inner)
    conv_xz(v, tmp2, w_ref, again)

    def second(c, carry):
        s = pl.ds(c * 8, 8)
        for start, end in last:
            inv = 1.0 / conv_y(tmp2, c * 8, 8, start, end - start)
            inv_s[s, start:end] = inv
            u[s, start:end] = dens[s, start:end] * inv
        return carry

    lax.fori_loop(0, rows // 8, second, 0)


def first_inner(w_ref, wb, dens, own, xb, xa, tmp, v, inv_a, tmp2, u, inv_s, big):
    join_rows(big, own, xa, xb)
    first_fields(True, wb, w_ref, dens, big, tmp, v, inv_a, tmp2, u, inv_s)


def first_outer(w_ref, wb, cot, dens, e, yb, ya, cb, ca, *rest):
    fields, mean, edges, ends = rest[6:12], rest[12], rest[13:17], rest[17]
    rows, tiles = dens.shape[0], dens.shape[1]
    mean[...] = jnp.broadcast_to(centre(e), (K, L))
    join_ends(ends, rows, HALO, ya, yb, ca, cb)
    first_fields(False, wb, w_ref, dens, ends, *fields)
    give_edges(fields[4], edges)
    xa, xb, ya, yb = edges
    px, py = parities()
    row_a = pl.ds(pl.multiple_of((1 - px) * (rows - 8), 8), 8)
    row_b = pl.ds(pl.multiple_of(px * (rows - 8), 8), 8)
    for t in range(tiles):
        xa[HALO, t] = cot[row_a, t * L : (t + 1) * L]
        xb[HALO, t] = cot[row_b, t * L : (t + 1) * L]
    for out, side in ((ya, 1 - py), (yb, py)):
        for t in range(HT):
            lanes = pl.ds(pl.multiple_of((side * (tiles - HT) + t) * L, L), L)
            for b in range(rows // 8):
                out[rows + b, t] = cot[b * 8 : b * 8 + 8, lanes]


def second_fields(inner, wb, w_ref, mean, cots, own, inv_s, src, tmp, r, tmp2, bu, z, q, sums):
    rows, tiles = own.shape[0], own.shape[1]
    first, outs, again, last = parts(tiles, inner)
    conv_xz(src, tmp, w_ref, first)

    def ring(x, count, mine):
        acc_k = jnp.zeros((K, L), F32)
        acc_s = jnp.zeros((1, L), F32)
        for start, end in outs:
            spread = jnp.log(conv_y(tmp, x, count, start, end - start))
            log_q = jnp.sum(wb[...] * spread, axis=2, keepdims=True)
            ratio = wb[...] * jnp.exp(log_q - spread)
            for i in range(count):
                for t in range(start, end):
                    cell = cots[t + 2, pl.ds(x + i + 4, 1), :]
                    r[x + i, t] = ratio[i, t - start] * cell
                    if mine and 2 <= t < tiles + 2:
                        row_q = jnp.exp(log_q[i, t - start])
                        q[t - 2, pl.ds(x + i - 4, 1), :] = row_q[0:1]
                        combined = cell * row_q[0:1]
                        acc_s = acc_s + combined
                        acc_k = acc_k + combined * (spread[i, t - start] - mean)
        if mine:
            sums[0] += acc_k
            sums[1, 0:1] += acc_s

    ring(0, 4, False)
    ring(rows + 4, 4, False)

    def middle(c, carry):
        ring(c * 8 + 4, 8, True)
        return carry

    lax.fori_loop(0, rows // 8, middle, 0)
    clear_outside((r,), outs, not inner)
    conv_xz(r, tmp2, w_ref, again)

    def second(c, carry):
        s = pl.ds(c * 8, 8)
        for start, end in last:
            back = own[s, start:end] * conv_y(tmp2, c * 8, 8, start, end - start)
            bu[s, start:end] = back
            z[s, start:end] = back * inv_s[s, start:end]
        return carry

    lax.fori_loop(0, rows // 8, second, 0)


def second_inner(w_ref, wb, cot, inv_s, own, xb, xa, tmp, r, tmp2, bu, z, q, sums, big, cots):
    rows, tiles = own.shape[0], own.shape[1]
    join_rows(big, own, xa, xb)
    (row_a, row_b), _ = sides(rows, tiles)
    for t in range(tiles):
        cots[HT + t, HALO : HALO + rows] = cot[:, t * L : (t + 1) * L]
        cots[HT + t, pl.ds(pl.multiple_of(row_a, 8), 8)] = xa[HALO, t]
        cots[HT + t, pl.ds(pl.multiple_of(row_b, 8), 8)] = xb[HALO, t]
    sums[...] = jnp.zeros_like(sums)
    second_fields(True, wb, w_ref, centre(own), cots, own, inv_s, big, tmp, r, tmp2, bu, z, q, sums)


def second_outer(w_ref, wb, mass, cot, inv_s, own, xb, xa, yb, ya, cb, ca, *rest):
    tmp, r, tmp2, bu, z, q, sums = rest[7:14]
    told, edges, (ends, cots) = rest[14], rest[15:19], rest[19:]
    rows, tiles = own.shape[0], own.shape[1]
    slabs = xa.shape[0]
    join_ends(ends, rows, slabs, ya, yb, ca, cb)
    (row_a, row_b), (col_a, col_b) = sides(rows, tiles)
    row_a, row_b = pl.ds(pl.multiple_of(row_a, 8), 8), pl.ds(pl.multiple_of(row_b, 8), 8)
    for t in (0, 1, tiles - 2, tiles - 1):
        cots[HT + t, HALO : HALO + rows] = cot[:, t * L : (t + 1) * L]
        cots[HT + t, row_a] = xa[HALO, t]
        cots[HT + t, row_b] = xb[HALO, t]
    for col, y, c in ((col_a, ya, ca), (col_b, yb, cb)):
        for t in range(HT):
            for b in range(rows // 8):
                cots[col + t, HALO + b * 8 : HALO + b * 8 + 8] = y[rows + b, t]
            cots[col + t, row_b] = c[HALO, t]
            cots[col + t, row_a] = c[slabs + HALO, t]
    mean = centre(own)
    second_fields(False, wb, w_ref, mean, cots, own, inv_s, ends, tmp, r, tmp2, bu, z, q, sums)
    told[...] = in_lanes(over_lanes(mass[...]), over_lanes(sums[0]), over_lanes(sums[1, 0:1]), mean)
    give_edges(z, edges)


def third_fields(inner, wb, w_ref, mean, inv_a, v, e, bu, src, tmp, r, tmp2, gp, sums):
    rows, tiles = e.shape[0], e.shape[1]
    first, outs, again, last = parts(tiles, inner)
    conv_xz(src, tmp, w_ref, first)

    def ring(x, count, mine):
        s = pl.ds(x, count)
        for start, end in outs:
            back_v = -(v[s, start:end] * conv_y(tmp, x, count, start, end - start))
            combined = jnp.sum(back_v, axis=2, keepdims=True)
            inv = inv_a[s, start:end]
            r[s, start:end] = (wb[...] * combined - back_v) * inv
            if mine:
                low, high = max(start, 2) - start, min(end, tiles + 2) - start
                part = combined[:, low:high]
                sums[0] += jnp.sum(part * (-jnp.log(inv[:, low:high]) - mean), axis=(0, 1))
                sums[1, 0:1] += jnp.sum(part, axis=(0, 1))

    ring(0, 4, False)
    ring(rows + 4, 4, False)

    def middle(c, carry):
        ring(c * 8 + 4, 8, True)
        return carry

    lax.fori_loop(0, rows // 8, middle, 0)
    conv_xz(r, tmp2, w_ref, again)

    def second(c, carry):
        s = pl.ds(c * 8, 8)
        for start, end in last:
            gp[s, start:end] = bu[s, start:end] + e[s, start:end] * conv_y(tmp2, c * 8, 8, start, end - start)
        return carry

    lax.fori_loop(0, rows // 8, second, 0)


def third_inner(w_ref, wb, mean, inv_a, v, e, bu, own, xb, xa, tmp, r, tmp2, gp, sums, big):
    join_rows(big, own, xa, xb)
    sums[...] = jnp.zeros_like(sums)
    third_fields(True, wb, w_ref, mean[...], inv_a, v, e, bu, big, tmp, r, tmp2, gp, sums)


def third_outer(w_ref, wb, mean, before, inv_a, v, e, bu, q, yb, ya, cb, ca, *rest):
    tmp, r, tmp2, gp, sums = rest[5:10]
    gp_out, q_out, told, ends, sem = rest[10:]
    rows, tiles = e.shape[0], e.shape[1]
    middle = pl.ds(HT, tiles - 2 * HT)
    copies = [pltpu.make_async_copy(q, q_out, sem.at[0]), pltpu.make_async_copy(gp.at[:, middle], gp_out.at[:, middle], sem.at[1])]
    for c in copies:
        c.start()
    join_ends(ends, rows, HALO, ya, yb, ca, cb)
    third_fields(False, wb, w_ref, mean[...], inv_a, v, e, bu, ends, tmp, r, tmp2, gp, sums)
    for i, first in enumerate((0, tiles - HT)):
        lanes = pl.ds(first, HT)
        copies.append(pltpu.make_async_copy(gp.at[:, lanes], gp_out.at[:, lanes], sem.at[i + 2]))
        copies[-1].start()
    early = before[...]
    told[...] = in_lanes(
        *[early[:, i : i + 1] for i in range(4)], over_lanes(sums[0]), over_lanes(sums[1, 0:1]), mean[:, 0:1]
    )
    for c in copies:
        c.wait()


def last_kernel(cells, wb, heard, q_far, gp_far, dens_far, out, bary, theta_out, turn, gp, dens, q, sem):
    rows, tiles = gp.shape[0], gp.shape[1]
    loads = []
    for i, first in enumerate(range(0, tiles, 4)):
        lanes = pl.ds(first, 4)
        for j, (src, dst) in enumerate(((gp_far, gp), (dens_far, dens))):
            loads.append(pltpu.make_async_copy(src.at[:, lanes], dst.at[:, lanes], sem.at[tiles + 2 * i + j]))
            loads[-1].start()
    loads.append(pltpu.make_async_copy(q_far, q, sem.at[tiles + tiles // 2]))
    loads[-1].start()
    weights = wb[:, 0:1]
    everyone = heard[...]
    total = jnp.sum(everyone, axis=0)
    mass, late = total[:, 0:1], total[:, 2:3]
    shift_k = jnp.log(F32(cells)) - jnp.log(mass)
    shift = jnp.sum(weights * shift_k, axis=0, keepdims=True)
    scale = jnp.exp(shift)
    last = weights * (scale * late)
    grad_sums = last + (last - weights * jnp.sum(last, axis=0, keepdims=True))
    coef = jnp.broadcast_to(grad_sums / mass, (K, L))
    scale_all = jnp.broadcast_to(scale, (K, L))
    copies = []
    for t in range(tiles):

        def rows_of(c, carry):
            for i in range(8):
                x = c * 8 + i
                turn[t, pl.ds(x, K, stride=rows), :] = gp[x, t] * scale_all - dens[x, t] * coef
            return carry

        if t % 4 == 0:
            loads[t // 2].wait()
            loads[t // 2 + 1].wait()
        if t == 0:
            loads[-1].wait()
        lax.fori_loop(0, rows // 8, rows_of, 0)
        copies.append(pltpu.make_async_copy(turn.at[t], out.at[:, pl.ds(t * L, L)], sem.at[t]))
        copies[-1].start()
        bary[:, t * L : (t + 1) * L] = q[t] * scale
    second = everyone[:, :, 1:2] + (everyone[:, :, 3:4] + (2.0 * shift_k - shift)) * everyone[:, :, 2:3]
    first = everyone[:, :, 4:5] + (everyone[:, :, 6:7] + shift_k) * everyone[:, :, 5:6]
    weight_grad = scale * jnp.sum(first + second, axis=0)
    grad = weights * (weight_grad - jnp.sum(weights * weight_grad, axis=0, keepdims=True))
    theta_out[...] = jnp.broadcast_to(grad, (K, L))
    for c in copies:
        c.wait()


def call(kernel, outs, scratch, semaphores, args, near_out=(), far_in=0, same=None, numbers=()):
    vmem, far = pl.BlockSpec(memory_space=pltpu.VMEM), pl.BlockSpec(memory_space=pl.ANY)
    near = len(args) - far_in
    args = [pltpu.with_memory_space_constraint(a, pltpu.VMEM if i < near else pltpu.HBM) for i, a in enumerate(args)]
    return pl.pallas_call(
        kernel,
        out_shape=outs,
        in_specs=[pl.BlockSpec(memory_space=pltpu.SMEM)] * len(numbers) + [vmem] * near + [far] * far_in,
        out_specs=[far if i in near_out else vmem for i in range(len(outs))],
        scratch_shapes=[pltpu.VMEM(s, F32) for s in scratch] + [pltpu.SemaphoreType.DMA((n,)) for n in semaphores],
        input_output_aliases=same or {},
        compiler_params=pltpu.CompilerParams(vmem_limit_bytes=VMEM),
    )(*numbers, *args)


def partners(axis, parity):
    count = lax.axis_size(axis)
    found = {}
    for i in range(count):
        j = i + 1 if i % 2 == parity else i - 1
        if 0 <= j < count:
            found[i] = j
    return found


def swap(value, axis, parity):
    return lax.ppermute(value, axis, list(partners(axis, parity).items()))


def exchange(xa, xb, ya, yb, tiles):
    rxb, ryb = swap(xb, "gx", 1), swap(yb, "gy", 1)
    rxa, rya = swap(xa, "gx", 0), swap(ya, "gy", 0)
    py = lax.rem(lax.axis_index("gy"), 2)

    def corner(side):
        first = side * (tiles - HT)
        return jnp.concatenate([lax.dynamic_slice_in_dim(r, first, HT, axis=1) for r in (rxb, rxa)], axis=0)

    rcb = swap(corner(py), "gy", 1)
    rca = swap(corner(1 - py), "gy", 0)
    return rxa, rxb, ryb, rya, rcb, rca


def over_all(told):
    devices = lax.axis_size("gx") * lax.axis_size("gy")
    return lax.all_to_all(jnp.broadcast_to(told[None], (devices, K, L)), ("gx", "gy"), 0, 0, tiled=True)


def shards(log_dens, theta, cotangent):
    _, rows, merged = log_dens.shape
    tiles = merged // L
    cells = lax.axis_size("gx") * lax.axis_size("gy") * rows * merged
    w = jnp.asarray(depth_weights())

    field, ringed, big = (rows, tiles, K, L), (rows + 8, tiles + 4, K, L), (rows + 16, tiles, K, L)
    tmp, tmp2, ends = (rows + 8, tiles + 8, K, L), (rows, tiles + 4, K, L), (rows + 16, 2 * HT, K, L)
    acc, turn, small, cots, q_shape = (2, K, L), (tiles, K * rows, L), (K, L), (tiles + 8, rows + 16, L), (tiles, rows, L)

    def near(*shapes):
        return [pltpu.VMEM(s, F32) for s in shapes]

    def edges(more, more_y):
        return near(*[(HALO + more, tiles, K, L)] * 2, *[(rows + more_y, HT, K, L)] * 2)

    logs = log_dens.reshape(K * rows, merged)
    dens, e, mass, wb, *sent = call(
        start_kernel, [pltpu.HBM(field, F32)] + near(field, small, small) + edges(0, 0), [turn, (rows, K, L), field], [tiles + 1],
        [logs], (0,), 1, numbers=(theta,),
    )
    xa, xb, *others = exchange(*sent, tiles)
    held = [tmp, ringed, ringed, tmp2, field, field]
    held_now = call(first_inner, near(*held), [big], [], [w, wb, dens, e, xb, xa])
    _, v, inv_a, _, u, inv_s, mean, *sent = call(
        first_outer, near(*held, small) + edges(1, rows // 8), [ends], [],
        [w, wb, cotangent, dens, e, *others, *held_now], same={9 + i: i for i in range(6)},
    )
    xa, xb, *others = exchange(*sent, tiles)
    held = [tmp, ringed, tmp2, field, field, q_shape, acc]
    held_now = call(second_inner, near(*held), [big, cots], [], [w, wb, cotangent, inv_s, u, xb, xa])
    _, _, _, bu, z, q, _, told, *sent = call(
        second_outer, near(*held, small) + edges(0, 0), [ends, cots], [],
        [w, wb, mass, cotangent, inv_s, u, xb, xa, *others, *held_now], same={12 + i: i for i in range(7)},
    )
    xa, xb, *others = exchange(*sent, tiles)
    held = [tmp, ringed, tmp2, field, acc]
    held_now = call(third_inner, near(*held), [big], [], [w, wb, mean, inv_a, v, e, bu, z, xb, xa])
    *_, gp_far, q_far, told = call(
        third_outer, near(*held) + [pltpu.HBM(field, F32), pltpu.HBM(q_shape, F32)] + near(small), [ends], [4],
        [w, wb, mean, told, inv_a, v, e, bu, q, *others, *held_now], (5, 6), same={13 + i: i for i in range(5)},
    )
    plain = [jax.ShapeDtypeStruct(s, F32) for s in ((K * rows, merged), (rows, merged), small)]
    grad, bary, grad_theta = call(
        functools.partial(last_kernel, cells), plain, [turn, field, field, q_shape], [tiles + tiles // 2 + 1],
        [wb, over_all(told), q_far, gp_far, dens], (0,), 3,
    )
    return bary, grad.reshape(K, rows, merged), grad_theta[:, 0]


def solution(mesh):
    placed = (P(None, "gx", "gy"), P(), P("gx", "gy"))
    return jax.shard_map(
        shards,
        mesh=mesh,
        in_specs=placed,
        out_specs=(P("gx", "gy"), P(None, "gx", "gy"), P()),
        check_vma=False,
    )
```

```python
import functools
import math

import jax
import jax.numpy as jnp
import numpy as np
from jax import lax
from jax.experimental import pallas as pl
from jax.experimental.pallas import tpu as pltpu
from jax.sharding import PartitionSpec as P

NZ = 64
K = 8
L = 128
HALO = 8
HT = HALO * NZ // L
VMEM = 14 * 1024 * 1024
F32 = jnp.float32
BF16 = jnp.bfloat16


def tap_list():
    raw_taps = [math.exp(-(offset * offset) / 8.0) for offset in range(-4, 5)]
    tap_total = 0.0
    for value in raw_taps:
        tap_total = tap_total + value
    return [value / tap_total for value in raw_taps]


G4, G3, G2, G1, G0 = tap_list()[:5]


def depth_weights():
    taps = tap_list()
    band = np.zeros((L, L), np.float32)
    for i in range(L):
        for j in range(L):
            if i // NZ == j // NZ and abs(i - j) <= 4:
                band[i, j] = taps[i - j + 4]
    high = band.astype(BF16)
    low = (band - high.astype(np.float32)).astype(BF16)
    half = np.concatenate([high, low], axis=1)
    return np.concatenate([half, half], axis=0)


def nine(at):
    return (G0 * at(4) + G1 * (at(3) + at(5))) + (G2 * (at(2) + at(6)) + G3 * (at(1) + at(7))) + G4 * (at(0) + at(8))


def conv_xz(src, dst, w_ref, pieces):
    rows = dst.shape[0]

    def some(now):
        for t, u in now:
            along = []
            for i in range(4):
                for x in range(0, rows, 8):
                    block = src[x : x + 16, u + i]
                    along.append(nine(lambda j: block[j : j + 8]).reshape(8 * K, L))
            value = jnp.concatenate(along, axis=0)
            high = value.astype(BF16)
            low = (value - high.astype(F32)).astype(BF16)
            both = jnp.dot(jnp.concatenate([high, low], axis=1), w_ref[...], preferred_element_type=F32)
            out = both[:, :L] + both[:, L:]
            for i in range(4):
                dst[:, t + i] = out[i * rows * K : (i + 1) * rows * K].reshape(rows, K, L)

    if len(pieces) < 4:
        some(pieces)
    else:

        def two(i, carry):
            some([(t + 8 * i, u + 8 * i) for t, u in pieces[:2]])
            return carry

        lax.fori_loop(0, len(pieces) // 2, two, 0)


def conv_y(src, first, rows, tile, n):
    value = src[pl.ds(first, rows), tile : tile + n + 4]
    flat = (rows * (n + 3) * K, L)
    lane = lax.broadcasted_iota(jnp.int32, flat, 1)
    mixed = jnp.where(lane < NZ, value[:, 1:].reshape(flat), value[:, :-1].reshape(flat))
    odd = pltpu.roll(mixed, NZ, axis=1).reshape(rows, n + 3, K, L)
    return (G0 * value[:, 2 : n + 2] + G1 * (odd[:, 1 : n + 1] + odd[:, 2 : n + 2])) + (
        G2 * (value[:, 1 : n + 1] + value[:, 3 : n + 3]) + G3 * (odd[:, 0:n] + odd[:, 3 : n + 3])
    ) + G4 * (value[:, 0:n] + value[:, 4 : n + 4])


def parities():
    return lax.rem(lax.axis_index("gx"), 2), lax.rem(lax.axis_index("gy"), 2)


def sides(rows, tiles):
    px, py = parities()
    return ((1 - px) * (rows + HALO), px * (rows + HALO)), ((1 - py) * (tiles + HT), py * (tiles + HT))


def join_rows(big, own, xa, xb):
    rows = own.shape[0]
    (row_a, row_b), _ = sides(rows, own.shape[1])
    big[HALO : HALO + rows] = own[...]
    big[pl.ds(row_a, HALO)] = xa[0:HALO]
    big[pl.ds(row_b, HALO)] = xb[0:HALO]


def join_ends(ends, rows, slabs, ya, yb, ca, da, db):
    (row_a, row_b), _ = sides(rows, 0)
    _, py = parities()
    row_a, row_b, middle = pl.ds(row_a, HALO), pl.ds(row_b, HALO), pl.ds(HALO, rows)
    col_a, col_b = pl.ds((1 - py) * HT, HT), pl.ds(py * HT, HT)
    ends[middle, col_a] = ya[0:rows]
    ends[row_b, col_a] = ca[0:HALO]
    ends[row_a, col_a] = ca[slabs : slabs + HALO]
    ends[middle, col_b] = yb[0:rows]
    ends[row_a, col_b] = da[0:HALO]
    ends[row_b, col_b] = db[0:HALO]


def give_edges(own, outs):
    xa, xb, ya, yb, da, db = outs
    rows, tiles = own.shape[0], own.shape[1]
    px, py = parities()
    row_a, row_b = pl.ds((1 - px) * (rows - HALO), HALO), pl.ds(px * (rows - HALO), HALO)
    col_a, col_b = pl.ds((1 - py) * (tiles - HT), HT), pl.ds(py * (tiles - HT), HT)
    xa[0:HALO] = own[row_a]
    xb[0:HALO] = own[row_b]
    ya[0:rows] = own[:, col_a]
    yb[0:rows] = own[:, col_b]
    da[0:HALO] = own[row_a, col_b]
    db[0:HALO] = own[row_b, col_b]


def clear_outside(fields, ranges, ends):
    rows, tiles = fields[0].shape[0], fields[0].shape[1]
    gx, gy = lax.axis_index("gx"), lax.axis_index("gy")

    def zero(first, count, ts):
        def write():
            for f in fields:
                for start, end in ts:
                    f[first : first + count, start:end] = jnp.zeros((count, end - start, K, L), F32)

        return write

    pl.when(gx == 0)(zero(0, 4, ranges))
    pl.when(gx == lax.axis_size("gx") - 1)(zero(rows - 4, 4, ranges))
    if ends:
        pl.when(gy == 0)(zero(0, rows, [(0, 2)]))
        pl.when(gy == lax.axis_size("gy") - 1)(zero(0, rows, [(tiles - 2, tiles)]))


def parts(tiles, inner):
    if inner:
        starts, outs, last = range(HT, tiles + HT, 4), [(HT, tiles)], [(HT, tiles - HT)]
        again = range(HT, tiles, 4)
        return [(t, t - HT) for t in starts], outs, [(t, t) for t in again], last
    outs, last = [(0, HT), (tiles, tiles + HT)], [(0, HT), (tiles - HT, tiles)]
    return [(0, 0), (tiles + HT, HT)], outs, [(0, 0), (tiles, tiles)], last


def inside(at, count):
    total = jnp.zeros(at.shape, F32)
    for offset, tap in zip(range(-4, 5), tap_list()):
        total = total + jnp.where((at + offset >= 0) & (at + offset < count), F32(tap), F32(0.0))
    return total


def in_lanes(*columns):
    lane = lax.broadcasted_iota(jnp.int32, (K, L), 1)
    out = jnp.zeros((K, L), F32)
    for i, c in enumerate(columns):
        out = jnp.where(lane == i, c, out)
    return out


def over_lanes(value):
    return jnp.sum(value, axis=1, keepdims=True)


def centre(field):
    return jnp.log(over_lanes(field[field.shape[0] // 2, field.shape[1] // 2]) * (1.0 / L))


def start_kernel(theta, log_ref, dens_out, e, mass, wb, *rest):
    edges, (turn, across, dens, sem) = rest[:6], rest[6:]
    rows, tiles = dens.shape[0], dens.shape[1]
    loads = [pltpu.make_async_copy(log_ref.at[:, pl.ds(t * L, L)], turn.at[t], sem.at[t]) for t in range(tiles)]
    for c in loads:
        c.start()
    density = lax.broadcasted_iota(jnp.int32, (K, L), 0)
    lane = lax.broadcasted_iota(jnp.int32, (K, L), 1)
    logits = jnp.zeros((K, L), F32)
    for k in range(K):
        logits = jnp.where(density == k, theta[k], logits)
    powers = jnp.exp(logits - jnp.max(logits, axis=0, keepdims=True))
    wb[...] = powers / jnp.sum(powers, axis=0, keepdims=True)
    depth = inside(lane % NZ, NZ)
    first = lax.axis_index("gy") * (tiles * L // NZ)

    at = lax.axis_index("gx") * rows + lax.broadcasted_iota(jnp.int32, (rows, K, L), 0)
    across[...] = 1.0 / inside(at, lax.axis_size("gx") * rows)
    mass[...] = jnp.zeros((K, L), F32)
    for t in range(tiles):
        along = inside(first + t * (L // NZ) + lane // NZ, lax.axis_size("gy") * (tiles * L // NZ))
        around = 1.0 / (along * depth)
        loads[t].wait()

        def some(c, acc):
            for i in range(8):
                x = c * 8 + i
                d = jnp.exp(turn[t, pl.ds(x, K, stride=rows), :])
                dens[x, t] = d
                e[x, t] = d * (around * across[x])
                acc = acc + d
            return acc

        mass[...] += lax.fori_loop(0, rows // 8, some, jnp.zeros((K, L), F32))
        pltpu.make_async_copy(dens.at[:, t], dens_out.at[:, t], sem.at[tiles]).start()
    give_edges(e, edges)
    pltpu.make_async_copy(dens, dens_out, sem.at[tiles]).wait()


def first_fields(inner, wb, w_ref, dens, src, tmp, v, inv_a, tmp2, u, inv_s):
    rows, tiles = dens.shape[0], dens.shape[1]
    first, outs, again, last = parts(tiles, inner)
    conv_xz(src, tmp, w_ref, first)

    def ring(c, carry):
        s = pl.ds(c * 8, 8)
        for start, end in outs:
            spread = jnp.log(conv_y(tmp, c * 8, 8, start, end - start))
            log_q = jnp.sum(wb[...] * spread, axis=2, keepdims=True)
            v[s, start:end] = jnp.exp(log_q - spread)
            inv_a[s, start:end] = jnp.exp(-spread)
        return carry

    lax.fori_loop(0, (rows + 8) // 8, ring, 0)
    clear_outside((v, inv_a), outs, not inner)
    conv_xz(v, tmp2, w_ref, again)

    def second(c, carry):
        s = pl.ds(c * 8, 8)
        for start, end in last:
            inv = 1.0 / conv_y(tmp2, c * 8, 8, start, end - start)
            inv_s[s, start:end] = inv
            u[s, start:end] = dens[s, start:end] * inv
        return carry

    lax.fori_loop(0, rows // 8, second, 0)


def first_inner(w_ref, wb, dens, own, xb, xa, tmp, v, inv_a, tmp2, u, inv_s, big):
    join_rows(big, own, xa, xb)
    first_fields(True, wb, w_ref, dens, big, tmp, v, inv_a, tmp2, u, inv_s)


def first_outer(w_ref, wb, cot, dens, e, yb, ya, ca, da, db, *rest):
    fields, mean, edges, ends = rest[6:12], rest[12], rest[13:19], rest[19]
    rows, tiles = dens.shape[0], dens.shape[1]
    mean[...] = jnp.broadcast_to(centre(e), (K, L))
    join_ends(ends, rows, HALO, ya, yb, ca, da, db)
    first_fields(False, wb, w_ref, dens, ends, *fields)
    give_edges(fields[4], edges)
    xa, xb, ya, yb, da, db = edges
    px, py = parities()
    row_a = pl.ds(pl.multiple_of((1 - px) * (rows - 8), 8), 8)
    row_b = pl.ds(pl.multiple_of(px * (rows - 8), 8), 8)
    for t in range(tiles):
        xa[HALO, t] = cot[row_a, t * L : (t + 1) * L]
        xb[HALO, t] = cot[row_b, t * L : (t + 1) * L]
    for out, side in ((ya, 1 - py), (yb, py)):
        for t in range(HT):
            lanes = pl.ds(pl.multiple_of((side * (tiles - HT) + t) * L, L), L)
            for b in range(rows // 8):
                out[rows + b, t] = cot[b * 8 : b * 8 + 8, lanes]
    for t in range(HT):
        lanes = pl.ds(pl.multiple_of((py * (tiles - HT) + t) * L, L), L)
        da[HALO, t] = cot[row_a, lanes]
        db[HALO, t] = cot[row_b, lanes]


def second_fields(inner, wb, w_ref, mean, cots, own, inv_s, src, tmp, r, tmp2, bu, z, q, sums):
    rows, tiles = own.shape[0], own.shape[1]
    first, outs, again, last = parts(tiles, inner)
    conv_xz(src, tmp, w_ref, first)

    def ring(x, count, mine):
        acc_k = jnp.zeros((K, L), F32)
        acc_s = jnp.zeros((1, L), F32)
        for start, end in outs:
            spread = jnp.log(conv_y(tmp, x, count, start, end - start))
            log_q = jnp.sum(wb[...] * spread, axis=2, keepdims=True)
            ratio = wb[...] * jnp.exp(log_q - spread)
            for i in range(count):
                for t in range(start, end):
                    cell = cots[t + 2, pl.ds(x + i + 4, 1), :]
                    r[x + i, t] = ratio[i, t - start] * cell
                    if mine and 2 <= t < tiles + 2:
                        row_q = jnp.exp(log_q[i, t - start])
                        q[t - 2, pl.ds(x + i - 4, 1), :] = row_q[0:1]
                        combined = cell * row_q[0:1]
                        acc_s = acc_s + combined
                        acc_k = acc_k + combined * (spread[i, t - start] - mean)
        if mine:
            sums[0] += acc_k
            sums[1, 0:1] += acc_s

    ring(0, 4, False)
    ring(rows + 4, 4, False)

    def middle(c, carry):
        ring(c * 8 + 4, 8, True)
        return carry

    lax.fori_loop(0, rows // 8, middle, 0)
    clear_outside((r,), outs, not inner)
    conv_xz(r, tmp2, w_ref, again)

    def second(c, carry):
        s = pl.ds(c * 8, 8)
        for start, end in last:
            back = own[s, start:end] * conv_y(tmp2, c * 8, 8, start, end - start)
            bu[s, start:end] = back
            z[s, start:end] = back * inv_s[s, start:end]
        return carry

    lax.fori_loop(0, rows // 8, second, 0)


def second_inner(w_ref, wb, cot, inv_s, own, xb, xa, tmp, r, tmp2, bu, z, q, sums, big, cots):
    rows, tiles = own.shape[0], own.shape[1]
    join_rows(big, own, xa, xb)
    (row_a, row_b), _ = sides(rows, tiles)
    for t in range(tiles):
        cots[HT + t, HALO : HALO + rows] = cot[:, t * L : (t + 1) * L]
        cots[HT + t, pl.ds(pl.multiple_of(row_a, 8), 8)] = xa[HALO, t]
        cots[HT + t, pl.ds(pl.multiple_of(row_b, 8), 8)] = xb[HALO, t]
    sums[...] = jnp.zeros_like(sums)
    second_fields(True, wb, w_ref, centre(own), cots, own, inv_s, big, tmp, r, tmp2, bu, z, q, sums)


def second_outer(w_ref, wb, mass, cot, inv_s, own, xb, xa, yb, ya, ca, da, db, *rest):
    tmp, r, tmp2, bu, z, q, sums = rest[7:14]
    told, edges, (ends, cots) = rest[14], rest[15:21], rest[21:]
    rows, tiles = own.shape[0], own.shape[1]
    slabs = xa.shape[0]
    join_ends(ends, rows, slabs, ya, yb, ca, da, db)
    (row_a, row_b), (col_a, col_b) = sides(rows, tiles)
    row_a, row_b = pl.ds(pl.multiple_of(row_a, 8), 8), pl.ds(pl.multiple_of(row_b, 8), 8)
    for t in (0, 1, tiles - 2, tiles - 1):
        cots[HT + t, HALO : HALO + rows] = cot[:, t * L : (t + 1) * L]
        cots[HT + t, row_a] = xa[HALO, t]
        cots[HT + t, row_b] = xb[HALO, t]
    for t in range(HT):
        for b in range(rows // 8):
            some_rows = pl.ds(HALO + b * 8, 8)
            cots[col_a + t, some_rows] = ya[rows + b, t]
            cots[col_b + t, some_rows] = yb[rows + b, t]
        cots[col_a + t, row_b] = ca[HALO, t]
        cots[col_a + t, row_a] = ca[slabs + HALO, t]
        cots[col_b + t, row_a] = da[HALO, t]
        cots[col_b + t, row_b] = db[HALO, t]
    mean = centre(own)
    second_fields(False, wb, w_ref, mean, cots, own, inv_s, ends, tmp, r, tmp2, bu, z, q, sums)
    told[...] = in_lanes(over_lanes(mass[...]), over_lanes(sums[0]), over_lanes(sums[1, 0:1]), mean)
    give_edges(z, edges)


def third_fields(inner, wb, w_ref, mean, inv_a, v, e, bu, src, tmp, r, tmp2, gp, sums):
    rows, tiles = e.shape[0], e.shape[1]
    first, outs, again, last = parts(tiles, inner)
    conv_xz(src, tmp, w_ref, first)

    def ring(x, count, mine):
        s = pl.ds(x, count)
        for start, end in outs:
            back_v = -(v[s, start:end] * conv_y(tmp, x, count, start, end - start))
            combined = jnp.sum(back_v, axis=2, keepdims=True)
            inv = inv_a[s, start:end]
            r[s, start:end] = (wb[...] * combined - back_v) * inv
            if mine:
                low, high = max(start, 2) - start, min(end, tiles + 2) - start
                part = combined[:, low:high]
                sums[0] += jnp.sum(part * (-jnp.log(inv[:, low:high]) - mean), axis=(0, 1))
                sums[1, 0:1] += jnp.sum(part, axis=(0, 1))

    ring(0, 4, False)
    ring(rows + 4, 4, False)

    def middle(c, carry):
        ring(c * 8 + 4, 8, True)
        return carry

    lax.fori_loop(0, rows // 8, middle, 0)
    conv_xz(r, tmp2, w_ref, again)

    def second(c, carry):
        s = pl.ds(c * 8, 8)
        for start, end in last:
            gp[s, start:end] = bu[s, start:end] + e[s, start:end] * conv_y(tmp2, c * 8, 8, start, end - start)
        return carry

    lax.fori_loop(0, rows // 8, second, 0)


def third_inner(w_ref, wb, mean, inv_a, v, e, bu, own, xb, xa, tmp, r, tmp2, gp, sums, big):
    join_rows(big, own, xa, xb)
    sums[...] = jnp.zeros_like(sums)
    third_fields(True, wb, w_ref, mean[...], inv_a, v, e, bu, big, tmp, r, tmp2, gp, sums)


def third_outer(w_ref, wb, mean, before, inv_a, v, e, bu, q, yb, ya, ca, da, db, *rest):
    tmp, r, tmp2, gp, sums = rest[5:10]
    gp_out, q_out, told, ends, sem = rest[10:]
    rows, tiles = e.shape[0], e.shape[1]
    middle = pl.ds(HT, tiles - 2 * HT)
    copies = [pltpu.make_async_copy(q, q_out, sem.at[0]), pltpu.make_async_copy(gp.at[:, middle], gp_out.at[:, middle], sem.at[1])]
    for c in copies:
        c.start()
    join_ends(ends, rows, HALO, ya, yb, ca, da, db)
    third_fields(False, wb, w_ref, mean[...], inv_a, v, e, bu, ends, tmp, r, tmp2, gp, sums)
    for i, first in enumerate((0, tiles - HT)):
        lanes = pl.ds(first, HT)
        copies.append(pltpu.make_async_copy(gp.at[:, lanes], gp_out.at[:, lanes], sem.at[i + 2]))
        copies[-1].start()
    early = before[...]
    told[...] = in_lanes(
        *[early[:, i : i + 1] for i in range(4)], over_lanes(sums[0]), over_lanes(sums[1, 0:1]), mean[:, 0:1]
    )
    for c in copies:
        c.wait()


def last_kernel(cells, wb, heard, q_far, gp_far, dens_far, out, bary, theta_out, turn, gp, dens, q, sem):
    rows, tiles = gp.shape[0], gp.shape[1]
    loads = []
    for i, first in enumerate(range(0, tiles, 4)):
        lanes = pl.ds(first, 4)
        for j, (src, dst) in enumerate(((gp_far, gp), (dens_far, dens))):
            loads.append(pltpu.make_async_copy(src.at[:, lanes], dst.at[:, lanes], sem.at[tiles + 2 * i + j]))
            loads[-1].start()
    loads.append(pltpu.make_async_copy(q_far, q, sem.at[tiles + tiles // 2]))
    loads[-1].start()
    weights = wb[:, 0:1]
    everyone = heard[...]
    total = jnp.sum(everyone, axis=0)
    mass, late = total[:, 0:1], total[:, 2:3]
    shift_k = jnp.log(F32(cells)) - jnp.log(mass)
    shift = jnp.sum(weights * shift_k, axis=0, keepdims=True)
    scale = jnp.exp(shift)
    last = weights * (scale * late)
    grad_sums = last + (last - weights * jnp.sum(last, axis=0, keepdims=True))
    coef = jnp.broadcast_to(grad_sums / mass, (K, L))
    scale_all = jnp.broadcast_to(scale, (K, L))
    copies = []
    for t in range(tiles):

        def rows_of(c, carry):
            for i in range(8):
                x = c * 8 + i
                turn[t, pl.ds(x, K, stride=rows), :] = gp[x, t] * scale_all - dens[x, t] * coef
            return carry

        if t % 4 == 0:
            loads[t // 2].wait()
            loads[t // 2 + 1].wait()
        if t == 0:
            loads[-1].wait()
        lax.fori_loop(0, rows // 8, rows_of, 0)
        copies.append(pltpu.make_async_copy(turn.at[t], out.at[:, pl.ds(t * L, L)], sem.at[t]))
        copies[-1].start()
        bary[:, t * L : (t + 1) * L] = q[t] * scale
    offsets = in_lanes(0.0, 0.0, 0.0, 2.0 * shift_k - shift, 0.0, 0.0, shift_k)
    turned = pltpu.roll(everyone.reshape(-1, L), 1, axis=1).reshape(everyone.shape)
    back = jnp.sum((everyone + offsets) * turned, axis=0)
    weight_grad = scale * (total[:, 1:2] + back[:, 3:4] + total[:, 4:5] + back[:, 6:7])
    grad = weights * (weight_grad - jnp.sum(weights * weight_grad, axis=0, keepdims=True))
    theta_out[...] = jnp.broadcast_to(grad, (K, L))
    for c in copies:
        c.wait()


def call(kernel, outs, scratch, semaphores, args, near_out=(), far_in=0, same=None, numbers=()):
    vmem, far = pl.BlockSpec(memory_space=pltpu.VMEM), pl.BlockSpec(memory_space=pl.ANY)
    near = len(args) - far_in
    args = [pltpu.with_memory_space_constraint(a, pltpu.VMEM if i < near else pltpu.HBM) for i, a in enumerate(args)]
    return pl.pallas_call(
        kernel,
        out_shape=outs,
        in_specs=[pl.BlockSpec(memory_space=pltpu.SMEM)] * len(numbers) + [vmem] * near + [far] * far_in,
        out_specs=[far if i in near_out else vmem for i in range(len(outs))],
        scratch_shapes=[pltpu.VMEM(s, F32) for s in scratch] + [pltpu.SemaphoreType.DMA((n,)) for n in semaphores],
        input_output_aliases=same or {},
        compiler_params=pltpu.CompilerParams(vmem_limit_bytes=VMEM),
    )(*numbers, *args)


def partners(axis, parity):
    count = lax.axis_size(axis)
    found = {}
    for i in range(count):
        j = i + 1 if i % 2 == parity else i - 1
        if 0 <= j < count:
            found[i] = j
    return found


def swap(value, axis, parity):
    return lax.ppermute(value, axis, list(partners(axis, parity).items()))


def swap_diagonal(value, parity_x, parity_y):
    along_x, along_y, width = partners("gx", parity_x), partners("gy", parity_y), lax.axis_size("gy")
    pairs = [(i * width + j, k * width + m) for i, k in along_x.items() for j, m in along_y.items()]
    return lax.ppermute(value, ("gx", "gy"), pairs)


def exchange(xa, xb, ya, yb, da, db, tiles):
    rxb, ryb = swap(xb, "gx", 1), swap(yb, "gy", 1)
    rdb, rda = swap_diagonal(db, 1, 1), swap_diagonal(da, 0, 1)
    rxa, rya = swap(xa, "gx", 0), swap(ya, "gy", 0)
    rxb, rxa, rdb, rda = lax.optimization_barrier((rxb, rxa, rdb, rda))
    first = (1 - lax.rem(lax.axis_index("gy"), 2)) * (tiles - HT)
    corner = jnp.concatenate([lax.dynamic_slice_in_dim(r, first, HT, axis=1) for r in (rxb, rxa)], axis=0)
    rca = swap(corner, "gy", 0)
    return rxa, rxb, ryb, rya, rca, rda, rdb


def over_all(told):
    devices = lax.axis_size("gx") * lax.axis_size("gy")
    return lax.all_to_all(jnp.broadcast_to(told[None], (devices, K, L)), ("gx", "gy"), 0, 0, tiled=True)


def shards(log_dens, theta, cotangent):
    _, rows, merged = log_dens.shape
    tiles = merged // L
    cells = lax.axis_size("gx") * lax.axis_size("gy") * rows * merged
    w = jnp.asarray(depth_weights())

    field, ringed, big = (rows, tiles, K, L), (rows + 8, tiles + 4, K, L), (rows + 16, tiles, K, L)
    tmp, tmp2, ends = (rows + 8, tiles + 8, K, L), (rows, tiles + 4, K, L), (rows + 16, 2 * HT, K, L)
    acc, turn, small, cots, q_shape = (2, K, L), (tiles, K * rows, L), (K, L), (tiles + 8, rows + 16, L), (tiles, rows, L)

    def near(*shapes):
        return [pltpu.VMEM(s, F32) for s in shapes]

    def edges(more, more_y):
        return near(*[(HALO + more, tiles, K, L)] * 2, *[(rows + more_y, HT, K, L)] * 2, *[(HALO + more, HT, K, L)] * 2)

    logs = log_dens.reshape(K * rows, merged)
    dens, e, mass, wb, *sent = call(
        start_kernel, [pltpu.HBM(field, F32)] + near(field, small, small) + edges(0, 0), [turn, (rows, K, L), field], [tiles + 1],
        [logs], (0,), 1, numbers=(theta,),
    )
    xa, xb, *others = exchange(*sent, tiles)
    held = [tmp, ringed, ringed, tmp2, field, field]
    held_now = call(first_inner, near(*held), [big], [], [w, wb, dens, e, xb, xa])
    _, v, inv_a, _, u, inv_s, mean, *sent = call(
        first_outer, near(*held, small) + edges(1, rows // 8), [ends], [],
        [w, wb, cotangent, dens, e, *others, *held_now], same={10 + i: i for i in range(6)},
    )
    xa, xb, *others = exchange(*sent, tiles)
    held = [tmp, ringed, tmp2, field, field, q_shape, acc]
    held_now = call(second_inner, near(*held), [big, cots], [], [w, wb, cotangent, inv_s, u, xb, xa])
    _, _, _, bu, z, q, _, told, *sent = call(
        second_outer, near(*held, small) + edges(0, 0), [ends, cots], [],
        [w, wb, mass, cotangent, inv_s, u, xb, xa, *others, *held_now], same={13 + i: i for i in range(7)},
    )
    xa, xb, *others = exchange(*sent, tiles)
    held = [tmp, ringed, tmp2, field, acc]
    held_now = call(third_inner, near(*held), [big], [], [w, wb, mean, inv_a, v, e, bu, z, xb, xa])
    *_, gp_far, q_far, told = call(
        third_outer, near(*held) + [pltpu.HBM(field, F32), pltpu.HBM(q_shape, F32)] + near(small), [ends], [4],
        [w, wb, mean, told, inv_a, v, e, bu, q, *others, *held_now], (5, 6), same={14 + i: i for i in range(5)},
    )
    plain = [jax.ShapeDtypeStruct(s, F32) for s in ((K * rows, merged), (rows, merged), small)]
    grad, bary, grad_theta = call(
        functools.partial(last_kernel, cells), plain, [turn, field, field, q_shape], [tiles + tiles // 2 + 1],
        [wb, over_all(told), q_far, gp_far, dens], (0,), 3,
    )
    return bary, grad.reshape(K, rows, merged), grad_theta[:, 0]


def solution(mesh):
    placed = (P(None, "gx", "gy"), P(), P("gx", "gy"))
    return jax.shard_map(
        shards,
        mesh=mesh,
        in_specs=placed,
        out_specs=(P("gx", "gy"), P(None, "gx", "gy"), P()),
        check_vma=False,
    )
```

```python
import functools
import math

import jax
import jax.numpy as jnp
import numpy as np
from jax import lax
from jax.experimental import pallas as pl
from jax.experimental.pallas import tpu as pltpu
from jax.sharding import PartitionSpec as P

NZ = 64
K = 8
L = 128
HALO = 8
HT = HALO * NZ // L
VMEM = 14 * 1024 * 1024
F32 = jnp.float32
BF16 = jnp.bfloat16


def tap_list():
    raw_taps = [math.exp(-(offset * offset) / 8.0) for offset in range(-4, 5)]
    tap_total = 0.0
    for value in raw_taps:
        tap_total = tap_total + value
    return [value / tap_total for value in raw_taps]


G4, G3, G2, G1, G0 = tap_list()[:5]


def depth_weights():
    taps = tap_list()
    band = np.zeros((L, L), np.float32)
    for i in range(L):
        for j in range(L):
            if i // NZ == j // NZ and abs(i - j) <= 4:
                band[i, j] = taps[i - j + 4]
    high = band.astype(BF16)
    low = (band - high.astype(np.float32)).astype(BF16)
    half = np.concatenate([high, low], axis=1)
    return np.concatenate([half, half], axis=0)


def nine(at):
    return (G0 * at(4) + G1 * (at(3) + at(5))) + (G2 * (at(2) + at(6)) + G3 * (at(1) + at(7))) + G4 * (at(0) + at(8))


def conv_xz(src, dst, w_ref, pieces):
    rows = dst.shape[0]

    def some(now):
        for t, u in now:
            along = []
            for i in range(4):
                for x in range(0, rows, 8):
                    block = src[x : x + 16, u + i]
                    along.append(nine(lambda j: block[j : j + 8]).reshape(8 * K, L))
            value = jnp.concatenate(along, axis=0)
            high = value.astype(BF16)
            low = (value - high.astype(F32)).astype(BF16)
            both = jnp.dot(jnp.concatenate([high, low], axis=1), w_ref[...], preferred_element_type=F32)
            out = both[:, :L] + both[:, L:]
            for i in range(4):
                dst[:, t + i] = out[i * rows * K : (i + 1) * rows * K].reshape(rows, K, L)

    if len(pieces) < 4:
        some(pieces)
    else:

        def two(i, carry):
            some([(t + 8 * i, u + 8 * i) for t, u in pieces[:2]])
            return carry

        lax.fori_loop(0, len(pieces) // 2, two, 0)


def conv_y(src, first, rows, tile, n):
    value = src[pl.ds(first, rows), tile : tile + n + 4]
    flat = (rows * (n + 3) * K, L)
    lane = lax.broadcasted_iota(jnp.int32, flat, 1)
    mixed = jnp.where(lane < NZ, value[:, 1:].reshape(flat), value[:, :-1].reshape(flat))
    odd = pltpu.roll(mixed, NZ, axis=1).reshape(rows, n + 3, K, L)
    return (G0 * value[:, 2 : n + 2] + G1 * (odd[:, 1 : n + 1] + odd[:, 2 : n + 2])) + (
        G2 * (value[:, 1 : n + 1] + value[:, 3 : n + 3]) + G3 * (odd[:, 0:n] + odd[:, 3 : n + 3])
    ) + G4 * (value[:, 0:n] + value[:, 4 : n + 4])


def parities():
    return lax.rem(lax.axis_index("gx"), 2), lax.rem(lax.axis_index("gy"), 2)


def sides(rows, tiles):
    px, py = parities()
    return ((1 - px) * (rows + HALO), px * (rows + HALO)), ((1 - py) * (tiles + HT), py * (tiles + HT))


def join_rows(big, own, xa, xb):
    rows = own.shape[0]
    (row_a, row_b), _ = sides(rows, own.shape[1])
    big[HALO : HALO + rows] = own[...]
    big[pl.ds(row_a, HALO)] = xa[0:HALO]
    big[pl.ds(row_b, HALO)] = xb[0:HALO]


def join_ends(ends, rows, slabs, ya, yb, ca, da, db):
    (row_a, row_b), _ = sides(rows, 0)
    _, py = parities()
    row_a, row_b, middle = pl.ds(row_a, HALO), pl.ds(row_b, HALO), pl.ds(HALO, rows)
    col_a, col_b = pl.ds((1 - py) * HT, HT), pl.ds(py * HT, HT)
    ends[middle, col_a] = ya[0:rows]
    ends[row_b, col_a] = ca[0:HALO]
    ends[row_a, col_a] = ca[slabs : slabs + HALO]
    ends[middle, col_b] = yb[0:rows]
    ends[row_a, col_b] = da[0:HALO]
    ends[row_b, col_b] = db[0:HALO]


def give_edges(own, outs):
    xa, xb, ya, yb, da, db = outs
    rows, tiles = own.shape[0], own.shape[1]
    px, py = parities()
    row_a, row_b = pl.ds((1 - px) * (rows - HALO), HALO), pl.ds(px * (rows - HALO), HALO)
    col_a, col_b = pl.ds((1 - py) * (tiles - HT), HT), pl.ds(py * (tiles - HT), HT)
    xa[0:HALO] = own[row_a]
    xb[0:HALO] = own[row_b]
    ya[0:rows] = own[:, col_a]
    yb[0:rows] = own[:, col_b]
    da[0:HALO] = own[row_a, col_b]
    db[0:HALO] = own[row_b, col_b]


def clear_outside(fields, ranges, ends):
    rows, tiles = fields[0].shape[0], fields[0].shape[1]
    gx, gy = lax.axis_index("gx"), lax.axis_index("gy")

    def zero(first, count, ts):
        def write():
            for f in fields:
                for start, end in ts:
                    f[first : first + count, start:end] = jnp.zeros((count, end - start, K, L), F32)

        return write

    pl.when(gx == 0)(zero(0, 4, ranges))
    pl.when(gx == lax.axis_size("gx") - 1)(zero(rows - 4, 4, ranges))
    if ends:
        pl.when(gy == 0)(zero(0, rows, [(0, 2)]))
        pl.when(gy == lax.axis_size("gy") - 1)(zero(0, rows, [(tiles - 2, tiles)]))


def parts(tiles, inner):
    if inner:
        starts, outs, last = range(HT, tiles + HT, 4), [(HT, tiles)], [(HT, tiles - HT)]
        again = range(HT, tiles, 4)
        return [(t, t - HT) for t in starts], outs, [(t, t) for t in again], last
    outs, last = [(0, HT), (tiles, tiles + HT)], [(0, HT), (tiles - HT, tiles)]
    return [(0, 0), (tiles + HT, HT)], outs, [(0, 0), (tiles, tiles)], last


def inside(at, count):
    total = jnp.zeros(at.shape, F32)
    for offset, tap in zip(range(-4, 5), tap_list()):
        total = total + jnp.where((at + offset >= 0) & (at + offset < count), F32(tap), F32(0.0))
    return total


def in_lanes(*columns):
    lane = lax.broadcasted_iota(jnp.int32, (K, L), 1)
    out = jnp.zeros((K, L), F32)
    for i, c in enumerate(columns):
        out = jnp.where(lane == i, c, out)
    return out


def over_lanes(value):
    return jnp.sum(value, axis=1, keepdims=True)


def centre(field):
    return jnp.log(over_lanes(field[field.shape[0] // 2, field.shape[1] // 2]) * (1.0 / L))


def start_kernel(theta, log_ref, dens_out, e, mass, wb, *rest):
    edges, (turn, across, dens, sem) = rest[:6], rest[6:]
    rows, tiles = dens.shape[0], dens.shape[1]
    loads = [pltpu.make_async_copy(log_ref.at[:, pl.ds(t * L, L)], turn.at[t], sem.at[t]) for t in range(tiles)]
    for c in loads:
        c.start()
    density = lax.broadcasted_iota(jnp.int32, (K, L), 0)
    lane = lax.broadcasted_iota(jnp.int32, (K, L), 1)
    logits = jnp.zeros((K, L), F32)
    for k in range(K):
        logits = jnp.where(density == k, theta[k], logits)
    powers = jnp.exp(logits - jnp.max(logits, axis=0, keepdims=True))
    wb[...] = powers / jnp.sum(powers, axis=0, keepdims=True)
    depth = inside(lane % NZ, NZ)
    first = lax.axis_index("gy") * (tiles * L // NZ)

    at = lax.axis_index("gx") * rows + lax.broadcasted_iota(jnp.int32, (rows, K, L), 0)
    across[...] = 1.0 / inside(at, lax.axis_size("gx") * rows)
    mass[...] = jnp.zeros((K, L), F32)
    for t in range(tiles):
        along = inside(first + t * (L // NZ) + lane // NZ, lax.axis_size("gy") * (tiles * L // NZ))
        around = 1.0 / (along * depth)
        loads[t].wait()

        def some(c, acc):
            for i in range(8):
                x = c * 8 + i
                d = jnp.exp(turn[t, pl.ds(x, K, stride=rows), :])
                dens[x, t] = d
                e[x, t] = d * (around * across[x])
                acc = acc + d
            return acc

        mass[...] += lax.fori_loop(0, rows // 8, some, jnp.zeros((K, L), F32))
        pltpu.make_async_copy(dens.at[:, t], dens_out.at[:, t], sem.at[tiles]).start()
    give_edges(e, edges)
    pltpu.make_async_copy(dens, dens_out, sem.at[tiles]).wait()


def first_fields(inner, wb, w_ref, dens, src, tmp, v, inv_a, tmp2, u, inv_s):
    rows, tiles = dens.shape[0], dens.shape[1]
    first, outs, again, last = parts(tiles, inner)
    conv_xz(src, tmp, w_ref, first)

    def ring(c, carry):
        s = pl.ds(c * 8, 8)
        for start, end in outs:
            spread = jnp.log(conv_y(tmp, c * 8, 8, start, end - start))
            log_q = jnp.sum(wb[...] * spread, axis=2, keepdims=True)
            v[s, start:end] = jnp.exp(log_q - spread)
            inv_a[s, start:end] = jnp.exp(-spread)
        return carry

    lax.fori_loop(0, (rows + 8) // 8, ring, 0)
    clear_outside((v, inv_a), outs, not inner)
    conv_xz(v, tmp2, w_ref, again)

    def second(c, carry):
        s = pl.ds(c * 8, 8)
        for start, end in last:
            inv = 1.0 / conv_y(tmp2, c * 8, 8, start, end - start)
            inv_s[s, start:end] = inv
            u[s, start:end] = dens[s, start:end] * inv
        return carry

    lax.fori_loop(0, rows // 8, second, 0)


def first_inner(w_ref, wb, dens, own, xb, xa, tmp, v, inv_a, tmp2, u, inv_s, big):
    join_rows(big, own, xa, xb)
    first_fields(True, wb, w_ref, dens, big, tmp, v, inv_a, tmp2, u, inv_s)


def first_outer(w_ref, wb, cot, dens, e, yb, ya, ca, da, db, *rest):
    fields, mean, edges, ends = rest[6:12], rest[12], rest[13:19], rest[19]
    rows, tiles = dens.shape[0], dens.shape[1]
    mean[...] = jnp.broadcast_to(centre(e), (K, L))
    join_ends(ends, rows, HALO, ya, yb, ca, da, db)
    first_fields(False, wb, w_ref, dens, ends, *fields)
    give_edges(fields[4], edges)
    xa, xb, ya, yb, da, db = edges
    px, py = parities()
    row_a = pl.ds(pl.multiple_of((1 - px) * (rows - 8), 8), 8)
    row_b = pl.ds(pl.multiple_of(px * (rows - 8), 8), 8)
    for t in range(tiles):
        xa[HALO, t] = cot[row_a, t * L : (t + 1) * L]
        xb[HALO, t] = cot[row_b, t * L : (t + 1) * L]
    for out, side in ((ya, 1 - py), (yb, py)):
        for t in range(HT):
            lanes = pl.ds(pl.multiple_of((side * (tiles - HT) + t) * L, L), L)
            for b in range(rows // 8):
                out[rows + b, t] = cot[b * 8 : b * 8 + 8, lanes]
    for t in range(HT):
        lanes = pl.ds(pl.multiple_of((py * (tiles - HT) + t) * L, L), L)
        da[HALO, t] = cot[row_a, lanes]
        db[HALO, t] = cot[row_b, lanes]


def second_fields(inner, wb, w_ref, mean, cots, own, inv_s, src, tmp, r, tmp2, bu, z, q, sums):
    rows, tiles = own.shape[0], own.shape[1]
    first, outs, again, last = parts(tiles, inner)
    conv_xz(src, tmp, w_ref, first)

    def ring(x, count, mine):
        acc_k = jnp.zeros((K, L), F32)
        acc_s = jnp.zeros((1, L), F32)
        for start, end in outs:
            spread = jnp.log(conv_y(tmp, x, count, start, end - start))
            log_q = jnp.sum(wb[...] * spread, axis=2, keepdims=True)
            ratio = wb[...] * jnp.exp(log_q - spread)
            for i in range(count):
                for t in range(start, end):
                    cell = cots[t + 2, pl.ds(x + i + 4, 1), :]
                    r[x + i, t] = ratio[i, t - start] * cell
                    if mine and 2 <= t < tiles + 2:
                        row_q = jnp.exp(log_q[i, t - start])
                        q[t - 2, pl.ds(x + i - 4, 1), :] = row_q[0:1]
                        combined = cell * row_q[0:1]
                        acc_s = acc_s + combined
                        acc_k = acc_k + combined * (spread[i, t - start] - mean)
        if mine:
            sums[0] += acc_k
            sums[1, 0:1] += acc_s

    ring(0, 4, False)
    ring(rows + 4, 4, False)

    def middle(c, carry):
        ring(c * 8 + 4, 8, True)
        return carry

    lax.fori_loop(0, rows // 8, middle, 0)
    clear_outside((r,), outs, not inner)
    conv_xz(r, tmp2, w_ref, again)

    def second(c, carry):
        s = pl.ds(c * 8, 8)
        for start, end in last:
            back = own[s, start:end] * conv_y(tmp2, c * 8, 8, start, end - start)
            bu[s, start:end] = back
            z[s, start:end] = back * inv_s[s, start:end]
        return carry

    lax.fori_loop(0, rows // 8, second, 0)


def second_inner(w_ref, wb, cot, inv_s, own, xb, xa, tmp, r, tmp2, bu, z, q, sums, big, cots):
    rows, tiles = own.shape[0], own.shape[1]
    join_rows(big, own, xa, xb)
    (row_a, row_b), _ = sides(rows, tiles)
    for t in range(tiles):
        cots[HT + t, HALO : HALO + rows] = cot[:, t * L : (t + 1) * L]
        cots[HT + t, pl.ds(pl.multiple_of(row_a, 8), 8)] = xa[HALO, t]
        cots[HT + t, pl.ds(pl.multiple_of(row_b, 8), 8)] = xb[HALO, t]
    sums[...] = jnp.zeros_like(sums)
    second_fields(True, wb, w_ref, centre(own), cots, own, inv_s, big, tmp, r, tmp2, bu, z, q, sums)


def second_outer(w_ref, wb, mass, cot, inv_s, own, xb, xa, yb, ya, ca, da, db, *rest):
    tmp, r, tmp2, bu, z, q, sums = rest[7:14]
    told, edges, (ends, cots) = rest[14], rest[15:21], rest[21:]
    rows, tiles = own.shape[0], own.shape[1]
    slabs = xa.shape[0]
    join_ends(ends, rows, slabs, ya, yb, ca, da, db)
    (row_a, row_b), (col_a, col_b) = sides(rows, tiles)
    row_a, row_b = pl.ds(pl.multiple_of(row_a, 8), 8), pl.ds(pl.multiple_of(row_b, 8), 8)
    for t in (0, 1, tiles - 2, tiles - 1):
        cots[HT + t, HALO : HALO + rows] = cot[:, t * L : (t + 1) * L]
        cots[HT + t, row_a] = xa[HALO, t]
        cots[HT + t, row_b] = xb[HALO, t]
    for t in range(HT):
        for b in range(rows // 8):
            some_rows = pl.ds(HALO + b * 8, 8)
            cots[col_a + t, some_rows] = ya[rows + b, t]
            cots[col_b + t, some_rows] = yb[rows + b, t]
        cots[col_a + t, row_b] = ca[HALO, t]
        cots[col_a + t, row_a] = ca[slabs + HALO, t]
        cots[col_b + t, row_a] = da[HALO, t]
        cots[col_b + t, row_b] = db[HALO, t]
    mean = centre(own)
    second_fields(False, wb, w_ref, mean, cots, own, inv_s, ends, tmp, r, tmp2, bu, z, q, sums)
    told[...] = in_lanes(over_lanes(mass[...]), over_lanes(sums[0]), over_lanes(sums[1, 0:1]), mean)
    give_edges(z, edges)


def third_fields(inner, wb, w_ref, mean, inv_a, v, e, bu, src, tmp, r, tmp2, gp, sums):
    rows, tiles = e.shape[0], e.shape[1]
    first, outs, again, last = parts(tiles, inner)
    conv_xz(src, tmp, w_ref, first)

    def ring(x, count, mine):
        s = pl.ds(x, count)
        for start, end in outs:
            back_v = -(v[s, start:end] * conv_y(tmp, x, count, start, end - start))
            combined = jnp.sum(back_v, axis=2, keepdims=True)
            inv = inv_a[s, start:end]
            r[s, start:end] = (wb[...] * combined - back_v) * inv
            if mine:
                low, high = max(start, 2) - start, min(end, tiles + 2) - start
                part = combined[:, low:high]
                sums[0] += jnp.sum(part * (-jnp.log(inv[:, low:high]) - mean), axis=(0, 1))
                sums[1, 0:1] += jnp.sum(part, axis=(0, 1))

    ring(0, 4, False)
    ring(rows + 4, 4, False)

    def middle(c, carry):
        ring(c * 8 + 4, 8, True)
        return carry

    lax.fori_loop(0, rows // 8, middle, 0)
    conv_xz(r, tmp2, w_ref, again)

    def second(c, carry):
        s = pl.ds(c * 8, 8)
        for start, end in last:
            gp[s, start:end] = bu[s, start:end] + e[s, start:end] * conv_y(tmp2, c * 8, 8, start, end - start)
        return carry

    lax.fori_loop(0, rows // 8, second, 0)


def third_inner(w_ref, wb, mean, inv_a, v, e, bu, own, xb, xa, tmp, r, tmp2, gp, sums, big):
    join_rows(big, own, xa, xb)
    sums[...] = jnp.zeros_like(sums)
    third_fields(True, wb, w_ref, mean[...], inv_a, v, e, bu, big, tmp, r, tmp2, gp, sums)


def third_outer(w_ref, wb, mean, before, inv_a, v, e, bu, q, yb, ya, ca, da, db, *rest):
    tmp, r, tmp2, gp, sums = rest[5:10]
    gp_out, q_out, told, ends, sem = rest[10:]
    rows, tiles = e.shape[0], e.shape[1]
    middle = pl.ds(HT, tiles - 2 * HT)
    copies = [pltpu.make_async_copy(q, q_out, sem.at[0]), pltpu.make_async_copy(gp.at[:, middle], gp_out.at[:, middle], sem.at[1])]
    for c in copies:
        c.start()
    join_ends(ends, rows, HALO, ya, yb, ca, da, db)
    third_fields(False, wb, w_ref, mean[...], inv_a, v, e, bu, ends, tmp, r, tmp2, gp, sums)
    for i, first in enumerate((0, tiles - HT)):
        lanes = pl.ds(first, HT)
        copies.append(pltpu.make_async_copy(gp.at[:, lanes], gp_out.at[:, lanes], sem.at[i + 2]))
        copies[-1].start()
    early = before[...]
    told[...] = in_lanes(
        *[early[:, i : i + 1] for i in range(4)], over_lanes(sums[0]), over_lanes(sums[1, 0:1]), mean[:, 0:1]
    )
    for c in copies:
        c.wait()


def last_kernel(cells, wb, heard, q_far, gp_far, dens_far, out, bary, theta_out, turn, gp, dens, q, sem):
    rows, tiles = gp.shape[0], gp.shape[1]
    loads = []
    for i, first in enumerate(range(0, tiles, 4)):
        lanes = pl.ds(first, 4)
        for j, (src, dst) in enumerate(((gp_far, gp), (dens_far, dens))):
            loads.append(pltpu.make_async_copy(src.at[:, lanes], dst.at[:, lanes], sem.at[tiles + 2 * i + j]))
            loads[-1].start()
    loads.append(pltpu.make_async_copy(q_far, q, sem.at[tiles + tiles // 2]))
    loads[-1].start()
    weights = wb[:, 0:1]
    everyone = heard[...]
    total = jnp.sum(everyone, axis=0)
    mass, late = total[:, 0:1], total[:, 2:3]
    shift_k = jnp.log(F32(cells)) - jnp.log(mass)
    shift = jnp.sum(weights * shift_k, axis=0, keepdims=True)
    scale = jnp.exp(shift)
    last = weights * (scale * late)
    grad_sums = last + (last - weights * jnp.sum(last, axis=0, keepdims=True))
    coef = jnp.broadcast_to(grad_sums / mass, (K, L))
    scale_all = jnp.broadcast_to(scale, (K, L))
    copies = []
    for t in range(tiles):

        def rows_of(c, carry):
            for i in range(8):
                x = c * 8 + i
                turn[t, pl.ds(x, K, stride=rows), :] = gp[x, t] * scale_all - dens[x, t] * coef
            return carry

        if t % 4 == 0:
            loads[t // 2].wait()
            loads[t // 2 + 1].wait()
        if t == 0:
            loads[-1].wait()
        lax.fori_loop(0, rows // 8, rows_of, 0)
        copies.append(pltpu.make_async_copy(turn.at[t], out.at[:, pl.ds(t * L, L)], sem.at[t]))
        copies[-1].start()
        bary[:, t * L : (t + 1) * L] = q[t] * scale
    offsets = in_lanes(0.0, 0.0, 0.0, 2.0 * shift_k - shift, 0.0, 0.0, shift_k)
    turned = pltpu.roll(everyone.reshape(-1, L), 1, axis=1).reshape(everyone.shape)
    back = jnp.sum((everyone + offsets) * turned, axis=0)
    weight_grad = scale * (total[:, 1:2] + back[:, 3:4] + total[:, 4:5] + back[:, 6:7])
    grad = weights * (weight_grad - jnp.sum(weights * weight_grad, axis=0, keepdims=True))
    theta_out[...] = jnp.broadcast_to(grad, (K, L))
    for c in copies:
        c.wait()


def call(kernel, outs, scratch, semaphores, args, near_out=(), far_in=0, same=None, numbers=()):
    vmem, far = pl.BlockSpec(memory_space=pltpu.VMEM), pl.BlockSpec(memory_space=pl.ANY)
    near = len(args) - far_in
    args = [pltpu.with_memory_space_constraint(a, pltpu.VMEM if i < near else pltpu.HBM) for i, a in enumerate(args)]
    return pl.pallas_call(
        kernel,
        out_shape=outs,
        in_specs=[pl.BlockSpec(memory_space=pltpu.SMEM)] * len(numbers) + [vmem] * near + [far] * far_in,
        out_specs=[far if i in near_out else vmem for i in range(len(outs))],
        scratch_shapes=[pltpu.VMEM(s, F32) for s in scratch] + [pltpu.SemaphoreType.DMA((n,)) for n in semaphores],
        input_output_aliases=same or {},
        compiler_params=pltpu.CompilerParams(vmem_limit_bytes=VMEM),
    )(*numbers, *args)


def partners(axis, parity):
    count = lax.axis_size(axis)
    found = {}
    for i in range(count):
        j = i + 1 if i % 2 == parity else i - 1
        if 0 <= j < count:
            found[i] = j
    return found


def swap(value, axis, parity):
    return lax.ppermute(value, axis, list(partners(axis, parity).items()))


def swap_diagonal(value, parity_x, parity_y):
    along_x, along_y, width = partners("gx", parity_x), partners("gy", parity_y), lax.axis_size("gy")
    pairs = [(i * width + j, k * width + m) for i, k in along_x.items() for j, m in along_y.items()]
    return lax.ppermute(value, ("gx", "gy"), pairs)


def exchange(xa, xb, ya, yb, da, db, tiles):
    rxb, ryb = swap(xb, "gx", 1), swap(yb, "gy", 1)
    rdb, rda = swap_diagonal(db, 1, 1), swap_diagonal(da, 0, 1)
    rxa, rya = swap(xa, "gx", 0), swap(ya, "gy", 0)
    first = (1 - lax.rem(lax.axis_index("gy"), 2)) * (tiles - HT)
    corner = jnp.concatenate([lax.dynamic_slice_in_dim(r, first, HT, axis=1) for r in (rxb, rxa)], axis=0)
    rca = swap(corner, "gy", 0)
    return rxa, rxb, ryb, rya, rca, rda, rdb


def over_all(told):
    devices = lax.axis_size("gx") * lax.axis_size("gy")
    return lax.all_to_all(jnp.broadcast_to(told[None], (devices, K, L)), ("gx", "gy"), 0, 0, tiled=True)


def shards(log_dens, theta, cotangent):
    _, rows, merged = log_dens.shape
    tiles = merged // L
    cells = lax.axis_size("gx") * lax.axis_size("gy") * rows * merged
    w = jnp.asarray(depth_weights())

    field, ringed, big = (rows, tiles, K, L), (rows + 8, tiles + 4, K, L), (rows + 16, tiles, K, L)
    tmp, tmp2, ends = (rows + 8, tiles + 8, K, L), (rows, tiles + 4, K, L), (rows + 16, 2 * HT, K, L)
    acc, turn, small, cots, q_shape = (2, K, L), (tiles, K * rows, L), (K, L), (tiles + 8, rows + 16, L), (tiles, rows, L)

    def near(*shapes):
        return [pltpu.VMEM(s, F32) for s in shapes]

    def edges(more, more_y):
        return near(*[(HALO + more, tiles, K, L)] * 2, *[(rows + more_y, HT, K, L)] * 2, *[(HALO + more, HT, K, L)] * 2)

    logs = log_dens.reshape(K * rows, merged)
    dens, e, mass, wb, *sent = call(
        start_kernel, [pltpu.HBM(field, F32)] + near(field, small, small) + edges(0, 0), [turn, (rows, K, L), field], [tiles + 1],
        [logs], (0,), 1, numbers=(theta,),
    )
    xa, xb, *others = exchange(*sent, tiles)
    held = [tmp, ringed, ringed, tmp2, field, field]
    held_now = call(first_inner, near(*held), [big], [], [w, wb, dens, e, xb, xa])
    _, v, inv_a, _, u, inv_s, mean, *sent = call(
        first_outer, near(*held, small) + edges(1, rows // 8), [ends], [],
        [w, wb, cotangent, dens, e, *others, *held_now], same={10 + i: i for i in range(6)},
    )
    xa, xb, *others = exchange(*sent, tiles)
    held = [tmp, ringed, tmp2, field, field, q_shape, acc]
    held_now = call(second_inner, near(*held), [big, cots], [], [w, wb, cotangent, inv_s, u, xb, xa])
    _, _, _, bu, z, q, _, told, *sent = call(
        second_outer, near(*held, small) + edges(0, 0), [ends, cots], [],
        [w, wb, mass, cotangent, inv_s, u, xb, xa, *others, *held_now], same={13 + i: i for i in range(7)},
    )
    xa, xb, *others = exchange(*sent, tiles)
    held = [tmp, ringed, tmp2, field, acc]
    held_now = call(third_inner, near(*held), [big], [], [w, wb, mean, inv_a, v, e, bu, z, xb, xa])
    *_, gp_far, q_far, told = call(
        third_outer, near(*held) + [pltpu.HBM(field, F32), pltpu.HBM(q_shape, F32)] + near(small), [ends], [4],
        [w, wb, mean, told, inv_a, v, e, bu, q, *others, *held_now], (5, 6), same={14 + i: i for i in range(5)},
    )
    plain = [jax.ShapeDtypeStruct(s, F32) for s in ((K * rows, merged), (rows, merged), small)]
    grad, bary, grad_theta = call(
        functools.partial(last_kernel, cells), plain, [turn, field, field, q_shape], [tiles + tiles // 2 + 1],
        [wb, over_all(told), q_far, gp_far, dens], (0,), 3,
    )
    return bary, grad.reshape(K, rows, merged), grad_theta[:, 0]


def solution(mesh):
    placed = (P(None, "gx", "gy"), P(), P("gx", "gy"))
    return jax.shard_map(
        shards,
        mesh=mesh,
        in_specs=placed,
        out_specs=(P("gx", "gy"), P(None, "gx", "gy"), P()),
        check_vma=False,
    )
```

```python
import functools
import math

import jax
import jax.numpy as jnp
import numpy as np
from jax import lax
from jax.experimental import pallas as pl
from jax.experimental.pallas import tpu as pltpu
from jax.sharding import PartitionSpec as P

NZ = 64
K = 8
L = 128
HALO = 8
HT = HALO * NZ // L
VMEM = 14 * 1024 * 1024
F32 = jnp.float32
BF16 = jnp.bfloat16


def tap_list():
    raw_taps = [math.exp(-(offset * offset) / 8.0) for offset in range(-4, 5)]
    tap_total = 0.0
    for value in raw_taps:
        tap_total = tap_total + value
    return [value / tap_total for value in raw_taps]


G4, G3, G2, G1, G0 = tap_list()[:5]


def depth_weights():
    taps = tap_list()
    band = np.zeros((L, L), np.float32)
    for i in range(L):
        for j in range(L):
            if i // NZ == j // NZ and abs(i - j) <= 4:
                band[i, j] = taps[i - j + 4]
    high = band.astype(BF16)
    low = (band - high.astype(np.float32)).astype(BF16)
    half = np.concatenate([high, low], axis=1)
    return np.concatenate([half, half], axis=0)


def nine(at):
    return (G0 * at(4) + G1 * (at(3) + at(5))) + (G2 * (at(2) + at(6)) + G3 * (at(1) + at(7))) + G4 * (at(0) + at(8))


def conv_xz(src, dst, w_ref, pieces):
    rows = dst.shape[0]

    def some(now):
        for t, u in now:
            along = []
            for i in range(4):
                for x in range(0, rows, 8):
                    block = src[x : x + 16, u + i]
                    along.append(nine(lambda j: block[j : j + 8]).reshape(8 * K, L))
            value = jnp.concatenate(along, axis=0)
            high = value.astype(BF16)
            low = (value - high.astype(F32)).astype(BF16)
            both = jnp.dot(jnp.concatenate([high, low], axis=1), w_ref[...], preferred_element_type=F32)
            out = both[:, :L] + both[:, L:]
            for i in range(4):
                dst[:, t + i] = out[i * rows * K : (i + 1) * rows * K].reshape(rows, K, L)

    if len(pieces) < 4:
        some(pieces)
    else:

        def two(i, carry):
            some([(t + 8 * i, u + 8 * i) for t, u in pieces[:2]])
            return carry

        lax.fori_loop(0, len(pieces) // 2, two, 0)


def conv_y(src, first, rows, tile, n):
    value = src[pl.ds(first, rows), tile : tile + n + 4]
    flat = (rows * (n + 3) * K, L)
    lane = lax.broadcasted_iota(jnp.int32, flat, 1)
    mixed = jnp.where(lane < NZ, value[:, 1:].reshape(flat), value[:, :-1].reshape(flat))
    odd = pltpu.roll(mixed, NZ, axis=1).reshape(rows, n + 3, K, L)
    return (G0 * value[:, 2 : n + 2] + G1 * (odd[:, 1 : n + 1] + odd[:, 2 : n + 2])) + (
        G2 * (value[:, 1 : n + 1] + value[:, 3 : n + 3]) + G3 * (odd[:, 0:n] + odd[:, 3 : n + 3])
    ) + G4 * (value[:, 0:n] + value[:, 4 : n + 4])


def parities():
    return lax.rem(lax.axis_index("gx"), 2), lax.rem(lax.axis_index("gy"), 2)


def sides(rows, tiles):
    px, py = parities()
    return ((1 - px) * (rows + HALO), px * (rows + HALO)), ((1 - py) * (tiles + HT), py * (tiles + HT))


def join_rows(big, own, xa, xb):
    rows = own.shape[0]
    (row_a, row_b), _ = sides(rows, own.shape[1])
    big[HALO : HALO + rows] = own[...]
    big[pl.ds(row_a, HALO)] = xa[0:HALO]
    big[pl.ds(row_b, HALO)] = xb[0:HALO]


def join_ends(ends, rows, slabs, ya, yb, ca, da, db):
    (row_a, row_b), _ = sides(rows, 0)
    _, py = parities()
    row_a, row_b, middle = pl.ds(row_a, HALO), pl.ds(row_b, HALO), pl.ds(HALO, rows)
    col_a, col_b = pl.ds((1 - py) * HT, HT), pl.ds(py * HT, HT)
    ends[middle, col_a] = ya[0:rows]
    ends[row_b, col_a] = ca[0:HALO]
    ends[row_a, col_a] = ca[slabs : slabs + HALO]
    ends[middle, col_b] = yb[0:rows]
    ends[row_a, col_b] = da[0:HALO]
    ends[row_b, col_b] = db[0:HALO]


def give_edges(own, outs):
    xa, xb, ya, yb, da, db = outs
    rows, tiles = own.shape[0], own.shape[1]
    px, py = parities()
    row_a, row_b = pl.ds((1 - px) * (rows - HALO), HALO), pl.ds(px * (rows - HALO), HALO)
    col_a, col_b = pl.ds((1 - py) * (tiles - HT), HT), pl.ds(py * (tiles - HT), HT)
    xa[0:HALO] = own[row_a]
    xb[0:HALO] = own[row_b]
    ya[0:rows] = own[:, col_a]
    yb[0:rows] = own[:, col_b]
    da[0:HALO] = own[row_a, col_b]
    db[0:HALO] = own[row_b, col_b]


def clear_outside(fields, ranges, ends):
    rows, tiles = fields[0].shape[0], fields[0].shape[1]
    gx, gy = lax.axis_index("gx"), lax.axis_index("gy")

    def zero(first, count, ts):
        def write():
            for f in fields:
                for start, end in ts:
                    f[first : first + count, start:end] = jnp.zeros((count, end - start, K, L), F32)

        return write

    pl.when(gx == 0)(zero(0, 4, ranges))
    pl.when(gx == lax.axis_size("gx") - 1)(zero(rows - 4, 4, ranges))
    if ends:
        pl.when(gy == 0)(zero(0, rows, [(0, 2)]))
        pl.when(gy == lax.axis_size("gy") - 1)(zero(0, rows, [(tiles - 2, tiles)]))


def parts(tiles, inner):
    if inner:
        starts, outs, last = range(HT, tiles + HT, 4), [(HT, tiles)], [(HT, tiles - HT)]
        again = range(HT, tiles, 4)
        return [(t, t - HT) for t in starts], outs, [(t, t) for t in again], last
    outs, last = [(0, HT), (tiles, tiles + HT)], [(0, HT), (tiles - HT, tiles)]
    return [(0, 0), (tiles + HT, HT)], outs, [(0, 0), (tiles, tiles)], last


def inside(at, count):
    total = jnp.zeros(at.shape, F32)
    for offset, tap in zip(range(-4, 5), tap_list()):
        total = total + jnp.where((at + offset >= 0) & (at + offset < count), F32(tap), F32(0.0))
    return total


def in_lanes(*columns):
    lane = lax.broadcasted_iota(jnp.int32, (K, L), 1)
    out = jnp.zeros((K, L), F32)
    for i, c in enumerate(columns):
        out = jnp.where(lane == i, c, out)
    return out


def over_lanes(value):
    return jnp.sum(value, axis=1, keepdims=True)


def centre(field):
    return jnp.log(over_lanes(field[field.shape[0] // 2, field.shape[1] // 2]) * (1.0 / L))


def start_kernel(theta, log_ref, dens_out, e, mass, wb, *rest):
    edges, (turn, across, dens, sem) = rest[:6], rest[6:]
    rows, tiles = dens.shape[0], dens.shape[1]
    loads = [pltpu.make_async_copy(log_ref.at[:, pl.ds(t * L, L)], turn.at[t], sem.at[t]) for t in range(tiles)]
    for c in loads:
        c.start()
    density = lax.broadcasted_iota(jnp.int32, (K, L), 0)
    lane = lax.broadcasted_iota(jnp.int32, (K, L), 1)
    logits = jnp.zeros((K, L), F32)
    for k in range(K):
        logits = jnp.where(density == k, theta[k], logits)
    powers = jnp.exp(logits - jnp.max(logits, axis=0, keepdims=True))
    wb[...] = powers / jnp.sum(powers, axis=0, keepdims=True)
    depth = inside(lane % NZ, NZ)
    first = lax.axis_index("gy") * (tiles * L // NZ)

    at = lax.axis_index("gx") * rows + lax.broadcasted_iota(jnp.int32, (rows, K, L), 0)
    across[...] = 1.0 / inside(at, lax.axis_size("gx") * rows)
    mass[...] = jnp.zeros((K, L), F32)
    for t in range(tiles):
        along = inside(first + t * (L // NZ) + lane // NZ, lax.axis_size("gy") * (tiles * L // NZ))
        around = 1.0 / (along * depth)
        loads[t].wait()

        def some(c, acc):
            for i in range(8):
                x = c * 8 + i
                d = jnp.exp(turn[t, pl.ds(x, K, stride=rows), :])
                dens[x, t] = d
                e[x, t] = d * (around * across[x])
                acc = acc + d
            return acc

        mass[...] += lax.fori_loop(0, rows // 8, some, jnp.zeros((K, L), F32))
        pltpu.make_async_copy(dens.at[:, t], dens_out.at[:, t], sem.at[tiles]).start()
    give_edges(e, edges)
    pltpu.make_async_copy(dens, dens_out, sem.at[tiles]).wait()


def first_fields(inner, wb, w_ref, dens, src, tmp, v, inv_a, tmp2, u, inv_s, load):
    rows, tiles = dens.shape[0], dens.shape[1]
    first, outs, again, last = parts(tiles, inner)
    conv_xz(src, tmp, w_ref, first)

    def ring(c, carry):
        s = pl.ds(c * 8, 8)
        for start, end in outs:
            spread = jnp.log(conv_y(tmp, c * 8, 8, start, end - start))
            log_q = jnp.sum(wb[...] * spread, axis=2, keepdims=True)
            v[s, start:end] = jnp.exp(log_q - spread)
            inv_a[s, start:end] = jnp.exp(-spread)
        return carry

    lax.fori_loop(0, (rows + 8) // 8, ring, 0)
    clear_outside((v, inv_a), outs, not inner)
    conv_xz(v, tmp2, w_ref, again)
    load.wait()

    def second(c, carry):
        s = pl.ds(c * 8, 8)
        for start, end in last:
            inv = 1.0 / conv_y(tmp2, c * 8, 8, start, end - start)
            inv_s[s, start:end] = inv
            u[s, start:end] = dens[s, start:end] * inv
        return carry

    lax.fori_loop(0, rows // 8, second, 0)


def first_inner(w_ref, wb, own, xb, xa, dens_far, tmp, v, inv_a, tmp2, u, inv_s, big, dens, sem):
    load = pltpu.make_async_copy(dens_far, dens, sem.at[0])
    load.start()
    join_rows(big, own, xa, xb)
    first_fields(True, wb, w_ref, dens, big, tmp, v, inv_a, tmp2, u, inv_s, load)


def first_outer(w_ref, wb, cot, e, yb, ya, ca, da, db, *rest):
    dens_far, fields, mean, edges, (ends, dens, sem) = rest[6], rest[7:13], rest[13], rest[14:20], rest[20:]
    rows, tiles = dens.shape[0], dens.shape[1]
    load = pltpu.make_async_copy(dens_far, dens, sem.at[0])
    load.start()
    mean[...] = jnp.broadcast_to(centre(e), (K, L))
    join_ends(ends, rows, HALO, ya, yb, ca, da, db)
    first_fields(False, wb, w_ref, dens, ends, *fields, load)
    give_edges(fields[4], edges)
    xa, xb, ya, yb, da, db = edges
    px, py = parities()
    row_a = pl.ds(pl.multiple_of((1 - px) * (rows - 8), 8), 8)
    row_b = pl.ds(pl.multiple_of(px * (rows - 8), 8), 8)
    for t in range(tiles):
        xa[HALO, t] = cot[row_a, t * L : (t + 1) * L]
        xb[HALO, t] = cot[row_b, t * L : (t + 1) * L]
    for out, side in ((ya, 1 - py), (yb, py)):
        for t in range(HT):
            lanes = pl.ds(pl.multiple_of((side * (tiles - HT) + t) * L, L), L)
            for b in range(rows // 8):
                out[rows + b, t] = cot[b * 8 : b * 8 + 8, lanes]
    for t in range(HT):
        lanes = pl.ds(pl.multiple_of((py * (tiles - HT) + t) * L, L), L)
        da[HALO, t] = cot[row_a, lanes]
        db[HALO, t] = cot[row_b, lanes]


def second_fields(inner, wb, w_ref, mean, cots, own, inv_s, src, tmp, r, tmp2, bu, z, q, sums):
    rows, tiles = own.shape[0], own.shape[1]
    first, outs, again, last = parts(tiles, inner)
    conv_xz(src, tmp, w_ref, first)

    def ring(x, count, mine):
        acc_k = jnp.zeros((K, L), F32)
        acc_s = jnp.zeros((1, L), F32)
        for start, end in outs:
            spread = jnp.log(conv_y(tmp, x, count, start, end - start))
            log_q = jnp.sum(wb[...] * spread, axis=2, keepdims=True)
            ratio = wb[...] * jnp.exp(log_q - spread)
            for i in range(count):
                for t in range(start, end):
                    cell = cots[t + 2, pl.ds(x + i + 4, 1), :]
                    r[x + i, t] = ratio[i, t - start] * cell
                    if mine and 2 <= t < tiles + 2:
                        row_q = jnp.exp(log_q[i, t - start])
                        q[t - 2, pl.ds(x + i - 4, 1), :] = row_q[0:1]
                        combined = cell * row_q[0:1]
                        acc_s = acc_s + combined
                        acc_k = acc_k + combined * (spread[i, t - start] - mean)
        if mine:
            sums[0] += acc_k
            sums[1, 0:1] += acc_s

    ring(0, 4, False)
    ring(rows + 4, 4, False)

    def middle(c, carry):
        ring(c * 8 + 4, 8, True)
        return carry

    lax.fori_loop(0, rows // 8, middle, 0)
    clear_outside((r,), outs, not inner)
    conv_xz(r, tmp2, w_ref, again)

    def second(c, carry):
        s = pl.ds(c * 8, 8)
        for start, end in last:
            back = own[s, start:end] * conv_y(tmp2, c * 8, 8, start, end - start)
            bu[s, start:end] = back
            z[s, start:end] = back * inv_s[s, start:end]
        return carry

    lax.fori_loop(0, rows // 8, second, 0)


def second_inner(w_ref, wb, cot, inv_s, own, xb, xa, tmp, r, tmp2, bu, z, q, sums, big, cots):
    rows, tiles = own.shape[0], own.shape[1]
    join_rows(big, own, xa, xb)
    (row_a, row_b), _ = sides(rows, tiles)
    for t in range(tiles):
        cots[HT + t, HALO : HALO + rows] = cot[:, t * L : (t + 1) * L]
        cots[HT + t, pl.ds(pl.multiple_of(row_a, 8), 8)] = xa[HALO, t]
        cots[HT + t, pl.ds(pl.multiple_of(row_b, 8), 8)] = xb[HALO, t]
    sums[...] = jnp.zeros_like(sums)
    second_fields(True, wb, w_ref, centre(own), cots, own, inv_s, big, tmp, r, tmp2, bu, z, q, sums)


def second_outer(w_ref, wb, mass, cot, inv_s, own, xb, xa, yb, ya, ca, da, db, *rest):
    tmp, r, tmp2, bu, z, q, sums = rest[7:14]
    told, edges, (ends, cots) = rest[14], rest[15:21], rest[21:]
    rows, tiles = own.shape[0], own.shape[1]
    slabs = xa.shape[0]
    join_ends(ends, rows, slabs, ya, yb, ca, da, db)
    (row_a, row_b), (col_a, col_b) = sides(rows, tiles)
    row_a, row_b = pl.ds(pl.multiple_of(row_a, 8), 8), pl.ds(pl.multiple_of(row_b, 8), 8)
    for t in (0, 1, tiles - 2, tiles - 1):
        cots[HT + t, HALO : HALO + rows] = cot[:, t * L : (t + 1) * L]
        cots[HT + t, row_a] = xa[HALO, t]
        cots[HT + t, row_b] = xb[HALO, t]
    for t in range(HT):
        for b in range(rows // 8):
            some_rows = pl.ds(HALO + b * 8, 8)
            cots[col_a + t, some_rows] = ya[rows + b, t]
            cots[col_b + t, some_rows] = yb[rows + b, t]
        cots[col_a + t, row_b] = ca[HALO, t]
        cots[col_a + t, row_a] = ca[slabs + HALO, t]
        cots[col_b + t, row_a] = da[HALO, t]
        cots[col_b + t, row_b] = db[HALO, t]
    mean = centre(own)
    second_fields(False, wb, w_ref, mean, cots, own, inv_s, ends, tmp, r, tmp2, bu, z, q, sums)
    told[...] = in_lanes(over_lanes(mass[...]), over_lanes(sums[0]), over_lanes(sums[1, 0:1]), mean)
    give_edges(z, edges)


def third_fields(inner, wb, w_ref, mean, inv_a, v, e, bu, src, tmp, r, tmp2, gp, sums):
    rows, tiles = e.shape[0], e.shape[1]
    first, outs, again, last = parts(tiles, inner)
    conv_xz(src, tmp, w_ref, first)

    def ring(x, count, mine):
        s = pl.ds(x, count)
        for start, end in outs:
            back_v = -(v[s, start:end] * conv_y(tmp, x, count, start, end - start))
            combined = jnp.sum(back_v, axis=2, keepdims=True)
            inv = inv_a[s, start:end]
            r[s, start:end] = (wb[...] * combined - back_v) * inv
            if mine:
                low, high = max(start, 2) - start, min(end, tiles + 2) - start
                part = combined[:, low:high]
                sums[0] += jnp.sum(part * (-jnp.log(inv[:, low:high]) - mean), axis=(0, 1))
                sums[1, 0:1] += jnp.sum(part, axis=(0, 1))

    ring(0, 4, False)
    ring(rows + 4, 4, False)

    def middle(c, carry):
        ring(c * 8 + 4, 8, True)
        return carry

    lax.fori_loop(0, rows // 8, middle, 0)
    conv_xz(r, tmp2, w_ref, again)

    def second(c, carry):
        s = pl.ds(c * 8, 8)
        for start, end in last:
            gp[s, start:end] = bu[s, start:end] + e[s, start:end] * conv_y(tmp2, c * 8, 8, start, end - start)
        return carry

    lax.fori_loop(0, rows // 8, second, 0)


def third_inner(w_ref, wb, mean, inv_a, v, e, bu, own, xb, xa, tmp, r, tmp2, gp, sums, big):
    join_rows(big, own, xa, xb)
    sums[...] = jnp.zeros_like(sums)
    third_fields(True, wb, w_ref, mean[...], inv_a, v, e, bu, big, tmp, r, tmp2, gp, sums)


def third_outer(w_ref, wb, mean, before, inv_a, v, e, bu, q, yb, ya, ca, da, db, *rest):
    tmp, r, tmp2, gp, sums = rest[5:10]
    gp_out, q_out, told, ends, sem = rest[10:]
    rows, tiles = e.shape[0], e.shape[1]
    middle = pl.ds(HT, tiles - 2 * HT)
    copies = [pltpu.make_async_copy(q, q_out, sem.at[0]), pltpu.make_async_copy(gp.at[:, middle], gp_out.at[:, middle], sem.at[1])]
    for c in copies:
        c.start()
    join_ends(ends, rows, HALO, ya, yb, ca, da, db)
    third_fields(False, wb, w_ref, mean[...], inv_a, v, e, bu, ends, tmp, r, tmp2, gp, sums)
    for i, first in enumerate((0, tiles - HT)):
        lanes = pl.ds(first, HT)
        copies.append(pltpu.make_async_copy(gp.at[:, lanes], gp_out.at[:, lanes], sem.at[i + 2]))
        copies[-1].start()
    early = before[...]
    told[...] = in_lanes(
        *[early[:, i : i + 1] for i in range(4)], over_lanes(sums[0]), over_lanes(sums[1, 0:1]), mean[:, 0:1]
    )
    for c in copies:
        c.wait()


def last_kernel(cells, wb, heard, q_far, gp_far, dens_far, out, bary, theta_out, turn, gp, dens, q, sem):
    rows, tiles = gp.shape[0], gp.shape[1]
    loads = []
    for i, first in enumerate(range(0, tiles, 4)):
        lanes = pl.ds(first, 4)
        for j, (src, dst) in enumerate(((gp_far, gp), (dens_far, dens))):
            loads.append(pltpu.make_async_copy(src.at[:, lanes], dst.at[:, lanes], sem.at[tiles + 2 * i + j]))
            loads[-1].start()
    loads.append(pltpu.make_async_copy(q_far, q, sem.at[tiles + tiles // 2]))
    loads[-1].start()
    weights = wb[:, 0:1]
    everyone = heard[...]
    total = jnp.sum(everyone, axis=0)
    mass, late = total[:, 0:1], total[:, 2:3]
    shift_k = jnp.log(F32(cells)) - jnp.log(mass)
    shift = jnp.sum(weights * shift_k, axis=0, keepdims=True)
    scale = jnp.exp(shift)
    last = weights * (scale * late)
    grad_sums = last + (last - weights * jnp.sum(last, axis=0, keepdims=True))
    coef = jnp.broadcast_to(grad_sums / mass, (K, L))
    scale_all = jnp.broadcast_to(scale, (K, L))
    copies = []
    for t in range(tiles):

        def rows_of(c, carry):
            for i in range(8):
                x = c * 8 + i
                turn[t, pl.ds(x, K, stride=rows), :] = gp[x, t] * scale_all - dens[x, t] * coef
            return carry

        if t % 4 == 0:
            loads[t // 2].wait()
            loads[t // 2 + 1].wait()
        if t == 0:
            loads[-1].wait()
        lax.fori_loop(0, rows // 8, rows_of, 0)
        copies.append(pltpu.make_async_copy(turn.at[t], out.at[:, pl.ds(t * L, L)], sem.at[t]))
        copies[-1].start()
        bary[:, t * L : (t + 1) * L] = q[t] * scale
    offsets = in_lanes(0.0, 0.0, 0.0, 2.0 * shift_k - shift, 0.0, 0.0, shift_k)
    turned = pltpu.roll(everyone.reshape(-1, L), 1, axis=1).reshape(everyone.shape)
    back = jnp.sum((everyone + offsets) * turned, axis=0)
    weight_grad = scale * (total[:, 1:2] + back[:, 3:4] + total[:, 4:5] + back[:, 6:7])
    grad = weights * (weight_grad - jnp.sum(weights * weight_grad, axis=0, keepdims=True))
    theta_out[...] = jnp.broadcast_to(grad, (K, L))
    for c in copies:
        c.wait()


def call(kernel, outs, scratch, semaphores, args, near_out=(), far_in=0, same=None, numbers=()):
    vmem, far = pl.BlockSpec(memory_space=pltpu.VMEM), pl.BlockSpec(memory_space=pl.ANY)
    near = len(args) - far_in
    args = [pltpu.with_memory_space_constraint(a, pltpu.VMEM if i < near else pltpu.HBM) for i, a in enumerate(args)]
    return pl.pallas_call(
        kernel,
        out_shape=outs,
        in_specs=[pl.BlockSpec(memory_space=pltpu.SMEM)] * len(numbers) + [vmem] * near + [far] * far_in,
        out_specs=[far if i in near_out else vmem for i in range(len(outs))],
        scratch_shapes=[pltpu.VMEM(s, F32) for s in scratch] + [pltpu.SemaphoreType.DMA((n,)) for n in semaphores],
        input_output_aliases=same or {},
        compiler_params=pltpu.CompilerParams(vmem_limit_bytes=VMEM),
    )(*numbers, *args)


def partners(axis, parity):
    count = lax.axis_size(axis)
    found = {}
    for i in range(count):
        j = i + 1 if i % 2 == parity else i - 1
        if 0 <= j < count:
            found[i] = j
    return found


def swap(value, axis, parity):
    return lax.ppermute(value, axis, list(partners(axis, parity).items()))


def swap_diagonal(value, parity_x, parity_y):
    along_x, along_y, width = partners("gx", parity_x), partners("gy", parity_y), lax.axis_size("gy")
    pairs = [(i * width + j, k * width + m) for i, k in along_x.items() for j, m in along_y.items()]
    return lax.ppermute(value, ("gx", "gy"), pairs)


def exchange(xa, xb, ya, yb, da, db, tiles):
    rxb, ryb = swap(xb, "gx", 1), swap(yb, "gy", 1)
    rdb, rda = swap_diagonal(db, 1, 1), swap_diagonal(da, 0, 1)
    rxa, rya = swap(xa, "gx", 0), swap(ya, "gy", 0)
    rxb, rxa, rdb, rda = lax.optimization_barrier((rxb, rxa, rdb, rda))
    first = (1 - lax.rem(lax.axis_index("gy"), 2)) * (tiles - HT)
    corner = jnp.concatenate([lax.dynamic_slice_in_dim(r, first, HT, axis=1) for r in (rxb, rxa)], axis=0)
    rca = swap(corner, "gy", 0)
    return rxa, rxb, ryb, rya, rca, rda, rdb


def over_all(told):
    devices = lax.axis_size("gx") * lax.axis_size("gy")
    return lax.all_to_all(jnp.broadcast_to(told[None], (devices, K, L)), ("gx", "gy"), 0, 0, tiled=True)


def shards(log_dens, theta, cotangent):
    _, rows, merged = log_dens.shape
    tiles = merged // L
    cells = lax.axis_size("gx") * lax.axis_size("gy") * rows * merged
    w = jnp.asarray(depth_weights())

    field, ringed, big = (rows, tiles, K, L), (rows + 8, tiles + 4, K, L), (rows + 16, tiles, K, L)
    tmp, tmp2, ends = (rows + 8, tiles + 8, K, L), (rows, tiles + 4, K, L), (rows + 16, 2 * HT, K, L)
    acc, turn, small, cots, q_shape = (2, K, L), (tiles, K * rows, L), (K, L), (tiles + 8, rows + 16, L), (tiles, rows, L)

    def near(*shapes):
        return [pltpu.VMEM(s, F32) for s in shapes]

    def edges(more, more_y):
        return near(*[(HALO + more, tiles, K, L)] * 2, *[(rows + more_y, HT, K, L)] * 2, *[(HALO + more, HT, K, L)] * 2)

    logs = log_dens.reshape(K * rows, merged)
    dens, e, mass, wb, *sent = call(
        start_kernel, [pltpu.HBM(field, F32)] + near(field, small, small) + edges(0, 0), [turn, (rows, K, L), field], [tiles + 1],
        [logs], (0,), 1, numbers=(theta,),
    )
    xa, xb, *others = exchange(*sent, tiles)
    held = [tmp, ringed, ringed, tmp2, field, field]
    held_now = call(first_inner, near(*held), [big, field], [1], [w, wb, e, xb, xa, dens], far_in=1)
    _, v, inv_a, _, u, inv_s, mean, *sent = call(
        first_outer, near(*held, small) + edges(1, rows // 8), [ends, field], [1],
        [w, wb, cotangent, e, *others, *held_now, dens], far_in=1, same={9 + i: i for i in range(6)},
    )
    xa, xb, *others = exchange(*sent, tiles)
    held = [tmp, ringed, tmp2, field, field, q_shape, acc]
    held_now = call(second_inner, near(*held), [big, cots], [], [w, wb, cotangent, inv_s, u, xb, xa])
    _, _, _, bu, z, q, _, told, *sent = call(
        second_outer, near(*held, small) + edges(0, 0), [ends, cots], [],
        [w, wb, mass, cotangent, inv_s, u, xb, xa, *others, *held_now], same={13 + i: i for i in range(7)},
    )
    xa, xb, *others = exchange(*sent, tiles)
    held = [tmp, ringed, tmp2, field, acc]
    held_now = call(third_inner, near(*held), [big], [], [w, wb, mean, inv_a, v, e, bu, z, xb, xa])
    *_, gp_far, q_far, told = call(
        third_outer, near(*held) + [pltpu.HBM(field, F32), pltpu.HBM(q_shape, F32)] + near(small), [ends], [4],
        [w, wb, mean, told, inv_a, v, e, bu, q, *others, *held_now], (5, 6), same={14 + i: i for i in range(5)},
    )
    plain = [jax.ShapeDtypeStruct(s, F32) for s in ((K * rows, merged), (rows, merged), small)]
    grad, bary, grad_theta = call(
        functools.partial(last_kernel, cells), plain, [turn, field, field, q_shape], [tiles + tiles // 2 + 1],
        [wb, over_all(told), q_far, gp_far, dens], (0,), 3,
    )
    return bary, grad.reshape(K, rows, merged), grad_theta[:, 0]


def solution(mesh):
    placed = (P(None, "gx", "gy"), P(), P("gx", "gy"))
    return jax.shard_map(
        shards,
        mesh=mesh,
        in_specs=placed,
        out_specs=(P("gx", "gy"), P(None, "gx", "gy"), P()),
        check_vma=False,
    )
```

```python
import functools
import math

import jax
import jax.numpy as jnp
import numpy as np
from jax import lax
from jax.experimental import pallas as pl
from jax.experimental.pallas import tpu as pltpu
from jax.sharding import PartitionSpec as P

NZ = 64
K = 8
L = 128
HALO = 8
HT = HALO * NZ // L
VMEM = 14 * 1024 * 1024
F32 = jnp.float32
BF16 = jnp.bfloat16


def tap_list():
    raw_taps = [math.exp(-(offset * offset) / 8.0) for offset in range(-4, 5)]
    tap_total = 0.0
    for value in raw_taps:
        tap_total = tap_total + value
    return [value / tap_total for value in raw_taps]


G4, G3, G2, G1, G0 = tap_list()[:5]


def depth_weights():
    taps = tap_list()
    band = np.zeros((L, L), np.float32)
    for i in range(L):
        for j in range(L):
            if i // NZ == j // NZ and abs(i - j) <= 4:
                band[i, j] = taps[i - j + 4]
    high = band.astype(BF16)
    low = (band - high.astype(np.float32)).astype(BF16)
    half = np.concatenate([high, low], axis=1)
    return np.concatenate([half, half], axis=0)


def nine(at):
    return (G0 * at(4) + G1 * (at(3) + at(5))) + (G2 * (at(2) + at(6)) + G3 * (at(1) + at(7))) + G4 * (at(0) + at(8))


def conv_xz(src, dst, w_ref, pieces):
    rows = dst.shape[0]

    def some(now):
        for t, u in now:
            along = []
            for i in range(4):
                for x in range(0, rows, 8):
                    block = src[x : x + 16, u + i]
                    along.append(nine(lambda j: block[j : j + 8]).reshape(8 * K, L))
            value = jnp.concatenate(along, axis=0)
            high = value.astype(BF16)
            low = (value - high.astype(F32)).astype(BF16)
            both = jnp.dot(jnp.concatenate([high, low], axis=1), w_ref[...], preferred_element_type=F32)
            out = both[:, :L] + both[:, L:]
            for i in range(4):
                dst[:, t + i] = out[i * rows * K : (i + 1) * rows * K].reshape(rows, K, L)

    if len(pieces) < 4:
        some(pieces)
    else:

        def two(i, carry):
            some([(t + 8 * i, u + 8 * i) for t, u in pieces[:2]])
            return carry

        lax.fori_loop(0, len(pieces) // 2, two, 0)


def conv_y(src, first, rows, tile, n):
    value = src[pl.ds(first, rows), tile : tile + n + 4]
    flat = (rows * (n + 3) * K, L)
    lane = lax.broadcasted_iota(jnp.int32, flat, 1)
    mixed = jnp.where(lane < NZ, value[:, 1:].reshape(flat), value[:, :-1].reshape(flat))
    odd = pltpu.roll(mixed, NZ, axis=1).reshape(rows, n + 3, K, L)
    return (G0 * value[:, 2 : n + 2] + G1 * (odd[:, 1 : n + 1] + odd[:, 2 : n + 2])) + (
        G2 * (value[:, 1 : n + 1] + value[:, 3 : n + 3]) + G3 * (odd[:, 0:n] + odd[:, 3 : n + 3])
    ) + G4 * (value[:, 0:n] + value[:, 4 : n + 4])


def parities():
    return lax.rem(lax.axis_index("gx"), 2), lax.rem(lax.axis_index("gy"), 2)


def sides(rows, tiles):
    px, py = parities()
    return ((1 - px) * (rows + HALO), px * (rows + HALO)), ((1 - py) * (tiles + HT), py * (tiles + HT))


def join_rows(big, own, xa, xb):
    rows = own.shape[0]
    (row_a, row_b), _ = sides(rows, own.shape[1])
    big[HALO : HALO + rows] = own[...]
    big[pl.ds(row_a, HALO)] = xa[0:HALO]
    big[pl.ds(row_b, HALO)] = xb[0:HALO]


def join_ends(ends, rows, slabs, ya, yb, ca, da, db):
    (row_a, row_b), _ = sides(rows, 0)
    _, py = parities()
    row_a, row_b, middle = pl.ds(row_a, HALO), pl.ds(row_b, HALO), pl.ds(HALO, rows)
    col_a, col_b = pl.ds((1 - py) * HT, HT), pl.ds(py * HT, HT)
    ends[middle, col_a] = ya[0:rows]
    ends[row_b, col_a] = ca[0:HALO]
    ends[row_a, col_a] = ca[slabs : slabs + HALO]
    ends[middle, col_b] = yb[0:rows]
    ends[row_a, col_b] = da[0:HALO]
    ends[row_b, col_b] = db[0:HALO]


def give_edges(own, outs):
    xa, xb, ya, yb, da, db = outs
    rows, tiles = own.shape[0], own.shape[1]
    px, py = parities()
    row_a, row_b = pl.ds((1 - px) * (rows - HALO), HALO), pl.ds(px * (rows - HALO), HALO)
    col_a, col_b = pl.ds((1 - py) * (tiles - HT), HT), pl.ds(py * (tiles - HT), HT)
    xa[0:HALO] = own[row_a]
    xb[0:HALO] = own[row_b]
    ya[0:rows] = own[:, col_a]
    yb[0:rows] = own[:, col_b]
    da[0:HALO] = own[row_a, col_b]
    db[0:HALO] = own[row_b, col_b]


def clear_outside(fields, ranges, ends):
    rows, tiles = fields[0].shape[0], fields[0].shape[1]
    gx, gy = lax.axis_index("gx"), lax.axis_index("gy")

    def zero(first, count, ts):
        def write():
            for f in fields:
                for start, end in ts:
                    f[first : first + count, start:end] = jnp.zeros((count, end - start, K, L), F32)

        return write

    pl.when(gx == 0)(zero(0, 4, ranges))
    pl.when(gx == lax.axis_size("gx") - 1)(zero(rows - 4, 4, ranges))
    if ends:
        pl.when(gy == 0)(zero(0, rows, [(0, 2)]))
        pl.when(gy == lax.axis_size("gy") - 1)(zero(0, rows, [(tiles - 2, tiles)]))


def parts(tiles, inner):
    if inner:
        starts, outs, last = range(HT, tiles + HT, 4), [(HT, tiles)], [(HT, tiles - HT)]
        again = range(HT, tiles, 4)
        return [(t, t - HT) for t in starts], outs, [(t, t) for t in again], last
    outs, last = [(0, HT), (tiles, tiles + HT)], [(0, HT), (tiles - HT, tiles)]
    return [(0, 0), (tiles + HT, HT)], outs, [(0, 0), (tiles, tiles)], last


def inside(at, count):
    total = jnp.zeros(at.shape, F32)
    for offset, tap in zip(range(-4, 5), tap_list()):
        total = total + jnp.where((at + offset >= 0) & (at + offset < count), F32(tap), F32(0.0))
    return total


def in_lanes(*columns):
    lane = lax.broadcasted_iota(jnp.int32, (K, L), 1)
    out = jnp.zeros((K, L), F32)
    for i, c in enumerate(columns):
        out = jnp.where(lane == i, c, out)
    return out


def over_lanes(value):
    return jnp.sum(value, axis=1, keepdims=True)


def centre(field):
    return jnp.log(over_lanes(field[field.shape[0] // 2, field.shape[1] // 2]) * (1.0 / L))


def start_kernel(theta, log_ref, dens_out, e, mass, wb, *rest):
    edges, (turn, across, dens, sem) = rest[:6], rest[6:]
    rows, tiles = dens.shape[0], dens.shape[1]
    loads = [pltpu.make_async_copy(log_ref.at[:, pl.ds(t * L, L)], turn.at[t], sem.at[t]) for t in range(tiles)]
    for c in loads:
        c.start()
    density = lax.broadcasted_iota(jnp.int32, (K, L), 0)
    lane = lax.broadcasted_iota(jnp.int32, (K, L), 1)
    logits = jnp.zeros((K, L), F32)
    for k in range(K):
        logits = jnp.where(density == k, theta[k], logits)
    powers = jnp.exp(logits - jnp.max(logits, axis=0, keepdims=True))
    wb[...] = powers / jnp.sum(powers, axis=0, keepdims=True)
    depth = inside(lane % NZ, NZ)
    first = lax.axis_index("gy") * (tiles * L // NZ)

    at = lax.axis_index("gx") * rows + lax.broadcasted_iota(jnp.int32, (rows, K, L), 0)
    across[...] = 1.0 / inside(at, lax.axis_size("gx") * rows)
    mass[...] = jnp.zeros((K, L), F32)
    for t in range(tiles):
        along = inside(first + t * (L // NZ) + lane // NZ, lax.axis_size("gy") * (tiles * L // NZ))
        around = 1.0 / (along * depth)
        loads[t].wait()

        def some(c, acc):
            for i in range(8):
                x = c * 8 + i
                d = jnp.exp(turn[t, pl.ds(x, K, stride=rows), :])
                dens[x, t] = d
                e[x, t] = d * (around * across[x])
                acc = acc + d
            return acc

        mass[...] += lax.fori_loop(0, rows // 8, some, jnp.zeros((K, L), F32))
        pltpu.make_async_copy(dens.at[:, t], dens_out.at[:, t], sem.at[tiles]).start()
    give_edges(e, edges)
    pltpu.make_async_copy(dens, dens_out, sem.at[tiles]).wait()


def first_fields(inner, wb, w_ref, dens, src, tmp, v, inv_a, tmp2, u, inv_s, load):
    rows, tiles = dens.shape[0], dens.shape[1]
    first, outs, again, last = parts(tiles, inner)
    conv_xz(src, tmp, w_ref, first)

    def ring(c, carry):
        s = pl.ds(c * 8, 8)
        for start, end in outs:
            spread = jnp.log(conv_y(tmp, c * 8, 8, start, end - start))
            log_q = jnp.sum(wb[...] * spread, axis=2, keepdims=True)
            v[s, start:end] = jnp.exp(log_q - spread)
            inv_a[s, start:end] = jnp.exp(-spread)
        return carry

    lax.fori_loop(0, (rows + 8) // 8, ring, 0)
    clear_outside((v, inv_a), outs, not inner)
    conv_xz(v, tmp2, w_ref, again)
    load.wait()

    def second(c, carry):
        s = pl.ds(c * 8, 8)
        for start, end in last:
            inv = 1.0 / conv_y(tmp2, c * 8, 8, start, end - start)
            inv_s[s, start:end] = inv
            u[s, start:end] = dens[s, start:end] * inv
        return carry

    lax.fori_loop(0, rows // 8, second, 0)


def first_inner(w_ref, wb, own, xb, xa, dens_far, tmp, v, inv_a, tmp2, u, inv_s, big, dens, sem):
    load = pltpu.make_async_copy(dens_far, dens, sem.at[0])
    load.start()
    join_rows(big, own, xa, xb)
    first_fields(True, wb, w_ref, dens, big, tmp, v, inv_a, tmp2, u, inv_s, load)


def first_outer(w_ref, wb, cot, e, yb, ya, ca, da, db, *rest):
    dens_far, fields, mean, edges, (ends, dens, sem) = rest[6], rest[7:13], rest[13], rest[14:20], rest[20:]
    rows, tiles = dens.shape[0], dens.shape[1]
    load = pltpu.make_async_copy(dens_far, dens, sem.at[0])
    load.start()
    mean[...] = jnp.broadcast_to(centre(e), (K, L))
    join_ends(ends, rows, HALO, ya, yb, ca, da, db)
    first_fields(False, wb, w_ref, dens, ends, *fields, load)
    give_edges(fields[4], edges)
    xa, xb, ya, yb, da, db = edges
    px, py = parities()
    row_a = pl.ds(pl.multiple_of((1 - px) * (rows - 8), 8), 8)
    row_b = pl.ds(pl.multiple_of(px * (rows - 8), 8), 8)
    for t in range(tiles):
        xa[HALO, t] = cot[row_a, t * L : (t + 1) * L]
        xb[HALO, t] = cot[row_b, t * L : (t + 1) * L]
    for out, side in ((ya, 1 - py), (yb, py)):
        for t in range(HT):
            lanes = pl.ds(pl.multiple_of((side * (tiles - HT) + t) * L, L), L)
            for b in range(rows // 8):
                out[rows + b, t] = cot[b * 8 : b * 8 + 8, lanes]
    for t in range(HT):
        lanes = pl.ds(pl.multiple_of((py * (tiles - HT) + t) * L, L), L)
        da[HALO, t] = cot[row_a, lanes]
        db[HALO, t] = cot[row_b, lanes]


def second_fields(inner, wb, w_ref, mean, cots, own, inv_s, src, tmp, r, tmp2, bu, z, q, sums):
    rows, tiles = own.shape[0], own.shape[1]
    first, outs, again, last = parts(tiles, inner)
    conv_xz(src, tmp, w_ref, first)

    def ring(x, count, mine):
        acc_k = jnp.zeros((K, L), F32)
        acc_s = jnp.zeros((1, L), F32)
        for start, end in outs:
            spread = jnp.log(conv_y(tmp, x, count, start, end - start))
            log_q = jnp.sum(wb[...] * spread, axis=2, keepdims=True)
            ratio = wb[...] * jnp.exp(log_q - spread)
            for i in range(count):
                for t in range(start, end):
                    cell = cots[t + 2, pl.ds(x + i + 4, 1), :]
                    r[x + i, t] = ratio[i, t - start] * cell
                    if mine and 2 <= t < tiles + 2:
                        row_q = jnp.exp(log_q[i, t - start])
                        q[t - 2, pl.ds(x + i - 4, 1), :] = row_q[0:1]
                        combined = cell * row_q[0:1]
                        acc_s = acc_s + combined
                        acc_k = acc_k + combined * (spread[i, t - start] - mean)
        if mine:
            sums[0] += acc_k
            sums[1, 0:1] += acc_s

    ring(0, 4, False)
    ring(rows + 4, 4, False)

    def middle(c, carry):
        ring(c * 8 + 4, 8, True)
        return carry

    lax.fori_loop(0, rows // 8, middle, 0)
    clear_outside((r,), outs, not inner)
    conv_xz(r, tmp2, w_ref, again)

    def second(c, carry):
        s = pl.ds(c * 8, 8)
        for start, end in last:
            back = own[s, start:end] * conv_y(tmp2, c * 8, 8, start, end - start)
            bu[s, start:end] = back
            z[s, start:end] = back * inv_s[s, start:end]
        return carry

    lax.fori_loop(0, rows // 8, second, 0)


def second_inner(w_ref, wb, cot, inv_s, own, xb, xa, tmp, r, tmp2, bu, z, q, sums, big, cots):
    rows, tiles = own.shape[0], own.shape[1]
    join_rows(big, own, xa, xb)
    (row_a, row_b), _ = sides(rows, tiles)
    for t in range(tiles):
        cots[HT + t, HALO : HALO + rows] = cot[:, t * L : (t + 1) * L]
        cots[HT + t, pl.ds(pl.multiple_of(row_a, 8), 8)] = xa[HALO, t]
        cots[HT + t, pl.ds(pl.multiple_of(row_b, 8), 8)] = xb[HALO, t]
    sums[...] = jnp.zeros_like(sums)
    second_fields(True, wb, w_ref, centre(own), cots, own, inv_s, big, tmp, r, tmp2, bu, z, q, sums)


def second_outer(w_ref, wb, mass, cot, inv_s, own, xb, xa, yb, ya, ca, da, db, *rest):
    tmp, r, tmp2, bu, z, q, sums = rest[7:14]
    told, edges, (ends, cots) = rest[14], rest[15:21], rest[21:]
    rows, tiles = own.shape[0], own.shape[1]
    slabs = xa.shape[0]
    join_ends(ends, rows, slabs, ya, yb, ca, da, db)
    (row_a, row_b), (col_a, col_b) = sides(rows, tiles)
    row_a, row_b = pl.ds(pl.multiple_of(row_a, 8), 8), pl.ds(pl.multiple_of(row_b, 8), 8)
    for t in (0, 1, tiles - 2, tiles - 1):
        cots[HT + t, HALO : HALO + rows] = cot[:, t * L : (t + 1) * L]
        cots[HT + t, row_a] = xa[HALO, t]
        cots[HT + t, row_b] = xb[HALO, t]
    for t in range(HT):
        for b in range(rows // 8):
            some_rows = pl.ds(HALO + b * 8, 8)
            cots[col_a + t, some_rows] = ya[rows + b, t]
            cots[col_b + t, some_rows] = yb[rows + b, t]
        cots[col_a + t, row_b] = ca[HALO, t]
        cots[col_a + t, row_a] = ca[slabs + HALO, t]
        cots[col_b + t, row_a] = da[HALO, t]
        cots[col_b + t, row_b] = db[HALO, t]
    mean = centre(own)
    second_fields(False, wb, w_ref, mean, cots, own, inv_s, ends, tmp, r, tmp2, bu, z, q, sums)
    told[...] = in_lanes(over_lanes(mass[...]), over_lanes(sums[0]), over_lanes(sums[1, 0:1]), mean)
    give_edges(z, edges)


def third_fields(inner, wb, w_ref, mean, inv_a, v, e, bu, src, tmp, r, tmp2, gp, sums):
    rows, tiles = e.shape[0], e.shape[1]
    first, outs, again, last = parts(tiles, inner)
    conv_xz(src, tmp, w_ref, first)

    def ring(x, count, mine):
        s = pl.ds(x, count)
        for start, end in outs:
            back_v = -(v[s, start:end] * conv_y(tmp, x, count, start, end - start))
            combined = jnp.sum(back_v, axis=2, keepdims=True)
            inv = inv_a[s, start:end]
            r[s, start:end] = (wb[...] * combined - back_v) * inv
            if mine:
                low, high = max(start, 2) - start, min(end, tiles + 2) - start
                part = combined[:, low:high]
                sums[0] += jnp.sum(part * (-jnp.log(inv[:, low:high]) - mean), axis=(0, 1))
                sums[1, 0:1] += jnp.sum(part, axis=(0, 1))

    ring(0, 4, False)
    ring(rows + 4, 4, False)

    def middle(c, carry):
        ring(c * 8 + 4, 8, True)
        return carry

    lax.fori_loop(0, rows // 8, middle, 0)
    conv_xz(r, tmp2, w_ref, again)

    def second(c, carry):
        s = pl.ds(c * 8, 8)
        for start, end in last:
            gp[s, start:end] = bu[s, start:end] + e[s, start:end] * conv_y(tmp2, c * 8, 8, start, end - start)
        return carry

    lax.fori_loop(0, rows // 8, second, 0)


def third_inner(w_ref, wb, mean, inv_a, v, e, bu, own, xb, xa, tmp, r, tmp2, gp, sums, big):
    join_rows(big, own, xa, xb)
    sums[...] = jnp.zeros_like(sums)
    third_fields(True, wb, w_ref, mean[...], inv_a, v, e, bu, big, tmp, r, tmp2, gp, sums)


def third_outer(w_ref, wb, mean, before, inv_a, v, e, bu, q, yb, ya, ca, da, db, *rest):
    tmp, r, tmp2, gp, sums = rest[5:10]
    gp_out, q_out, told, ends, sem = rest[10:]
    rows, tiles = e.shape[0], e.shape[1]
    middle = pl.ds(HT, tiles - 2 * HT)
    copies = [pltpu.make_async_copy(q, q_out, sem.at[0]), pltpu.make_async_copy(gp.at[:, middle], gp_out.at[:, middle], sem.at[1])]
    for c in copies:
        c.start()
    join_ends(ends, rows, HALO, ya, yb, ca, da, db)
    third_fields(False, wb, w_ref, mean[...], inv_a, v, e, bu, ends, tmp, r, tmp2, gp, sums)
    for i, first in enumerate((0, tiles - HT)):
        lanes = pl.ds(first, HT)
        copies.append(pltpu.make_async_copy(gp.at[:, lanes], gp_out.at[:, lanes], sem.at[i + 2]))
        copies[-1].start()
    early = before[...]
    told[...] = in_lanes(
        *[early[:, i : i + 1] for i in range(4)], over_lanes(sums[0]), over_lanes(sums[1, 0:1]), mean[:, 0:1]
    )
    for c in copies:
        c.wait()


def last_kernel(cells, wb, heard, q_far, gp_far, dens_far, out, bary, theta_out, turn, gp, dens, q, sem):
    rows, tiles = gp.shape[0], gp.shape[1]
    loads = []
    for i, first in enumerate(range(0, tiles, 4)):
        lanes = pl.ds(first, 4)
        for j, (src, dst) in enumerate(((gp_far, gp), (dens_far, dens))):
            loads.append(pltpu.make_async_copy(src.at[:, lanes], dst.at[:, lanes], sem.at[tiles + 2 * i + j]))
            loads[-1].start()
    loads.append(pltpu.make_async_copy(q_far, q, sem.at[tiles + tiles // 2]))
    loads[-1].start()
    weights = wb[:, 0:1]
    everyone = heard[...]
    total = jnp.sum(everyone, axis=0)
    mass, late = total[:, 0:1], total[:, 2:3]
    shift_k = jnp.log(F32(cells)) - jnp.log(mass)
    shift = jnp.sum(weights * shift_k, axis=0, keepdims=True)
    scale = jnp.exp(shift)
    last = weights * (scale * late)
    grad_sums = last + (last - weights * jnp.sum(last, axis=0, keepdims=True))
    coef = jnp.broadcast_to(grad_sums / mass, (K, L))
    scale_all = jnp.broadcast_to(scale, (K, L))
    copies = []
    for t in range(tiles):

        def rows_of(c, carry):
            for i in range(8):
                x = c * 8 + i
                turn[t, pl.ds(x, K, stride=rows), :] = gp[x, t] * scale_all - dens[x, t] * coef
            return carry

        if t % 4 == 0:
            loads[t // 2].wait()
            loads[t // 2 + 1].wait()
        if t == 0:
            loads[-1].wait()
        lax.fori_loop(0, rows // 8, rows_of, 0)
        copies.append(pltpu.make_async_copy(turn.at[t], out.at[:, pl.ds(t * L, L)], sem.at[t]))
        copies[-1].start()
        bary[:, t * L : (t + 1) * L] = q[t] * scale
    offsets = in_lanes(0.0, 0.0, 0.0, 2.0 * shift_k - shift, 0.0, 0.0, shift_k)
    turned = pltpu.roll(everyone.reshape(-1, L), 1, axis=1).reshape(everyone.shape)
    back = jnp.sum((everyone + offsets) * turned, axis=0)
    weight_grad = scale * (total[:, 1:2] + back[:, 3:4] + total[:, 4:5] + back[:, 6:7])
    grad = weights * (weight_grad - jnp.sum(weights * weight_grad, axis=0, keepdims=True))
    theta_out[...] = jnp.broadcast_to(grad, (K, L))
    for c in copies:
        c.wait()


def call(kernel, outs, scratch, semaphores, args, near_out=(), far_in=0, same=None, numbers=()):
    vmem, far = pl.BlockSpec(memory_space=pltpu.VMEM), pl.BlockSpec(memory_space=pl.ANY)
    near = len(args) - far_in
    args = [pltpu.with_memory_space_constraint(a, pltpu.VMEM if i < near else pltpu.HBM) for i, a in enumerate(args)]
    return pl.pallas_call(
        kernel,
        out_shape=outs,
        in_specs=[pl.BlockSpec(memory_space=pltpu.SMEM)] * len(numbers) + [vmem] * near + [far] * far_in,
        out_specs=[far if i in near_out else vmem for i in range(len(outs))],
        scratch_shapes=[pltpu.VMEM(s, F32) for s in scratch] + [pltpu.SemaphoreType.DMA((n,)) for n in semaphores],
        input_output_aliases=same or {},
        compiler_params=pltpu.CompilerParams(vmem_limit_bytes=VMEM),
    )(*numbers, *args)


def partners(axis, parity):
    count = lax.axis_size(axis)
    found = {}
    for i in range(count):
        j = i + 1 if i % 2 == parity else i - 1
        if 0 <= j < count:
            found[i] = j
    return found


def swap(value, axis, parity):
    return lax.ppermute(value, axis, list(partners(axis, parity).items()))


def exchange(xa, xb, ya, yb, da, db, tiles):
    del da, db
    rxb, ryb = swap(xb, "gx", 1), swap(yb, "gy", 1)
    rxa, rya = swap(xa, "gx", 0), swap(ya, "gy", 0)
    px, py = lax.rem(lax.axis_index("gx"), 2), lax.rem(lax.axis_index("gy"), 2)
    first = (1 - py) * (tiles - HT)
    corner = jnp.concatenate([lax.dynamic_slice_in_dim(r, first, HT, axis=1) for r in (rxb, rxa)], axis=0)
    rca = swap(corner, "gy", 0)
    slabs = xa.shape[0] - HALO
    rows = ryb.shape[0] if slabs == 0 else ryb.shape[0] * 8 // 9

    def facing(side):
        taken = [lax.dynamic_slice_in_dim(ryb, side * (rows - HALO), HALO, axis=0)]
        if slabs:
            taken.append(lax.dynamic_slice_in_dim(ryb, rows + side * (rows // 8 - 1), 1, axis=0))
        return jnp.concatenate(taken, axis=0)

    rdb, rda = swap(facing(px), "gx", 1), swap(facing(1 - px), "gx", 0)
    return rxa, rxb, ryb, rya, rca, rda, rdb


def over_all(told):
    devices = lax.axis_size("gx") * lax.axis_size("gy")
    return lax.all_to_all(jnp.broadcast_to(told[None], (devices, K, L)), ("gx", "gy"), 0, 0, tiled=True)


def shards(log_dens, theta, cotangent):
    _, rows, merged = log_dens.shape
    tiles = merged // L
    cells = lax.axis_size("gx") * lax.axis_size("gy") * rows * merged
    w = jnp.asarray(depth_weights())

    field, ringed, big = (rows, tiles, K, L), (rows + 8, tiles + 4, K, L), (rows + 16, tiles, K, L)
    tmp, tmp2, ends = (rows + 8, tiles + 8, K, L), (rows, tiles + 4, K, L), (rows + 16, 2 * HT, K, L)
    acc, turn, small, cots, q_shape = (2, K, L), (tiles, K * rows, L), (K, L), (tiles + 8, rows + 16, L), (tiles, rows, L)

    def near(*shapes):
        return [pltpu.VMEM(s, F32) for s in shapes]

    def edges(more, more_y):
        return near(*[(HALO + more, tiles, K, L)] * 2, *[(rows + more_y, HT, K, L)] * 2, *[(HALO + more, HT, K, L)] * 2)

    logs = log_dens.reshape(K * rows, merged)
    dens, e, mass, wb, *sent = call(
        start_kernel, [pltpu.HBM(field, F32)] + near(field, small, small) + edges(0, 0), [turn, (rows, K, L), field], [tiles + 1],
        [logs], (0,), 1, numbers=(theta,),
    )
    xa, xb, *others = exchange(*sent, tiles)
    held = [tmp, ringed, ringed, tmp2, field, field]
    held_now = call(first_inner, near(*held), [big, field], [1], [w, wb, e, xb, xa, dens], far_in=1)
    _, v, inv_a, _, u, inv_s, mean, *sent = call(
        first_outer, near(*held, small) + edges(1, rows // 8), [ends, field], [1],
        [w, wb, cotangent, e, *others, *held_now, dens], far_in=1, same={9 + i: i for i in range(6)},
    )
    xa, xb, *others = exchange(*sent, tiles)
    held = [tmp, ringed, tmp2, field, field, q_shape, acc]
    held_now = call(second_inner, near(*held), [big, cots], [], [w, wb, cotangent, inv_s, u, xb, xa])
    _, _, _, bu, z, q, _, told, *sent = call(
        second_outer, near(*held, small) + edges(0, 0), [ends, cots], [],
        [w, wb, mass, cotangent, inv_s, u, xb, xa, *others, *held_now], same={13 + i: i for i in range(7)},
    )
    xa, xb, *others = exchange(*sent, tiles)
    held = [tmp, ringed, tmp2, field, acc]
    held_now = call(third_inner, near(*held), [big], [], [w, wb, mean, inv_a, v, e, bu, z, xb, xa])
    *_, gp_far, q_far, told = call(
        third_outer, near(*held) + [pltpu.HBM(field, F32), pltpu.HBM(q_shape, F32)] + near(small), [ends], [4],
        [w, wb, mean, told, inv_a, v, e, bu, q, *others, *held_now], (5, 6), same={14 + i: i for i in range(5)},
    )
    plain = [jax.ShapeDtypeStruct(s, F32) for s in ((K * rows, merged), (rows, merged), small)]
    grad, bary, grad_theta = call(
        functools.partial(last_kernel, cells), plain, [turn, field, field, q_shape], [tiles + tiles // 2 + 1],
        [wb, over_all(told), q_far, gp_far, dens], (0,), 3,
    )
    return bary, grad.reshape(K, rows, merged), grad_theta[:, 0]


def solution(mesh):
    placed = (P(None, "gx", "gy"), P(), P("gx", "gy"))
    return jax.shard_map(
        shards,
        mesh=mesh,
        in_specs=placed,
        out_specs=(P("gx", "gy"), P(None, "gx", "gy"), P()),
        check_vma=False,
    )
```

```python
import functools
import math

import jax
import jax.numpy as jnp
import numpy as np
from jax import lax
from jax.experimental import pallas as pl
from jax.experimental.pallas import tpu as pltpu
from jax.sharding import PartitionSpec as P

NZ = 64
K = 8
L = 128
HALO = 8
HT = HALO * NZ // L
VMEM = 14 * 1024 * 1024
F32 = jnp.float32
BF16 = jnp.bfloat16


def tap_list():
    raw_taps = [math.exp(-(offset * offset) / 8.0) for offset in range(-4, 5)]
    tap_total = 0.0
    for value in raw_taps:
        tap_total = tap_total + value
    return [value / tap_total for value in raw_taps]


G4, G3, G2, G1, G0 = tap_list()[:5]


def depth_weights():
    taps = tap_list()
    band = np.zeros((L, L), np.float32)
    for i in range(L):
        for j in range(L):
            if i // NZ == j // NZ and abs(i - j) <= 4:
                band[i, j] = taps[i - j + 4]
    high = band.astype(BF16)
    low = (band - high.astype(np.float32)).astype(BF16)
    half = np.concatenate([high, low], axis=1)
    return np.concatenate([half, half], axis=0)


def nine(at):
    return (G0 * at(4) + G1 * (at(3) + at(5))) + (G2 * (at(2) + at(6)) + G3 * (at(1) + at(7))) + G4 * (at(0) + at(8))


def conv_xz(src, dst, w_ref, pieces):
    rows = dst.shape[0]

    def some(now):
        for t, u in now:
            along = []
            for i in range(4):
                for x in range(0, rows, 8):
                    block = src[x : x + 16, u + i]
                    along.append(nine(lambda j: block[j : j + 8]).reshape(8 * K, L))
            value = jnp.concatenate(along, axis=0)
            high = value.astype(BF16)
            low = (value - high.astype(F32)).astype(BF16)
            both = jnp.dot(jnp.concatenate([high, low], axis=1), w_ref[...], preferred_element_type=F32)
            out = both[:, :L] + both[:, L:]
            for i in range(4):
                dst[:, t + i] = out[i * rows * K : (i + 1) * rows * K].reshape(rows, K, L)

    if len(pieces) < 4:
        some(pieces)
    else:

        def two(i, carry):
            some([(t + 8 * i, u + 8 * i) for t, u in pieces[:2]])
            return carry

        lax.fori_loop(0, len(pieces) // 2, two, 0)


def conv_y(src, first, rows, tile, n):
    value = src[pl.ds(first, rows), tile : tile + n + 4]
    flat = (rows * (n + 3) * K, L)
    lane = lax.broadcasted_iota(jnp.int32, flat, 1)
    mixed = jnp.where(lane < NZ, value[:, 1:].reshape(flat), value[:, :-1].reshape(flat))
    odd = pltpu.roll(mixed, NZ, axis=1).reshape(rows, n + 3, K, L)
    return (G0 * value[:, 2 : n + 2] + G1 * (odd[:, 1 : n + 1] + odd[:, 2 : n + 2])) + (
        G2 * (value[:, 1 : n + 1] + value[:, 3 : n + 3]) + G3 * (odd[:, 0:n] + odd[:, 3 : n + 3])
    ) + G4 * (value[:, 0:n] + value[:, 4 : n + 4])


def parities():
    return lax.rem(lax.axis_index("gx"), 2), lax.rem(lax.axis_index("gy"), 2)


def sides(rows, tiles):
    px, py = parities()
    return ((1 - px) * (rows + HALO), px * (rows + HALO)), ((1 - py) * (tiles + HT), py * (tiles + HT))


def join_rows(big, own, xa, xb):
    rows = own.shape[0]
    (row_a, row_b), _ = sides(rows, own.shape[1])
    big[HALO : HALO + rows] = own[...]
    big[pl.ds(row_a, HALO)] = xa[0:HALO]
    big[pl.ds(row_b, HALO)] = xb[0:HALO]


def join_ends(ends, rows, slabs, ya, yb, ca, da, db):
    (row_a, row_b), _ = sides(rows, 0)
    _, py = parities()
    row_a, row_b, middle = pl.ds(row_a, HALO), pl.ds(row_b, HALO), pl.ds(HALO, rows)
    col_a, col_b = pl.ds((1 - py) * HT, HT), pl.ds(py * HT, HT)
    ends[middle, col_a] = ya[0:rows]
    ends[row_b, col_a] = ca[0:HALO]
    ends[row_a, col_a] = ca[slabs : slabs + HALO]
    ends[middle, col_b] = yb[0:rows]
    ends[row_a, col_b] = da[0:HALO]
    ends[row_b, col_b] = db[0:HALO]


def give_edges(own, outs):
    xa, xb, ya, yb, da, db = outs
    rows, tiles = own.shape[0], own.shape[1]
    px, py = parities()
    row_a, row_b = pl.ds((1 - px) * (rows - HALO), HALO), pl.ds(px * (rows - HALO), HALO)
    col_a, col_b = pl.ds((1 - py) * (tiles - HT), HT), pl.ds(py * (tiles - HT), HT)
    xa[0:HALO] = own[row_a]
    xb[0:HALO] = own[row_b]
    ya[0:rows] = own[:, col_a]
    yb[0:rows] = own[:, col_b]
    da[0:HALO] = own[row_a, col_b]
    db[0:HALO] = own[row_b, col_b]


def clear_outside(fields, ranges, ends):
    rows, tiles = fields[0].shape[0], fields[0].shape[1]
    gx, gy = lax.axis_index("gx"), lax.axis_index("gy")

    def zero(first, count, ts):
        def write():
            for f in fields:
                for start, end in ts:
                    f[first : first + count, start:end] = jnp.zeros((count, end - start, K, L), F32)

        return write

    pl.when(gx == 0)(zero(0, 4, ranges))
    pl.when(gx == lax.axis_size("gx") - 1)(zero(rows - 4, 4, ranges))
    if ends:
        pl.when(gy == 0)(zero(0, rows, [(0, 2)]))
        pl.when(gy == lax.axis_size("gy") - 1)(zero(0, rows, [(tiles - 2, tiles)]))


def parts(tiles, inner):
    if inner:
        starts, outs, last = range(HT, tiles + HT, 4), [(HT, tiles)], [(HT, tiles - HT)]
        again = range(HT, tiles, 4)
        return [(t, t - HT) for t in starts], outs, [(t, t) for t in again], last
    outs, last = [(0, HT), (tiles, tiles + HT)], [(0, HT), (tiles - HT, tiles)]
    return [(0, 0), (tiles + HT, HT)], outs, [(0, 0), (tiles, tiles)], last


def inside(at, count):
    total = jnp.zeros(at.shape, F32)
    for offset, tap in zip(range(-4, 5), tap_list()):
        total = total + jnp.where((at + offset >= 0) & (at + offset < count), F32(tap), F32(0.0))
    return total


def in_lanes(*columns):
    lane = lax.broadcasted_iota(jnp.int32, (K, L), 1)
    out = jnp.zeros((K, L), F32)
    for i, c in enumerate(columns):
        out = jnp.where(lane == i, c, out)
    return out


def over_lanes(value):
    return jnp.sum(value, axis=1, keepdims=True)


def centre(field):
    return jnp.log(over_lanes(field[field.shape[0] // 2, field.shape[1] // 2]) * (1.0 / L))


def start_kernel(theta, log_ref, dens_out, e, mass, wb, *rest):
    edges, (turn, across, dens, sem) = rest[:6], rest[6:]
    rows, tiles = dens.shape[0], dens.shape[1]
    loads = [pltpu.make_async_copy(log_ref.at[:, pl.ds(t * L, L)], turn.at[t], sem.at[t]) for t in range(tiles)]
    for c in loads:
        c.start()
    density = lax.broadcasted_iota(jnp.int32, (K, L), 0)
    lane = lax.broadcasted_iota(jnp.int32, (K, L), 1)
    logits = jnp.zeros((K, L), F32)
    for k in range(K):
        logits = jnp.where(density == k, theta[k], logits)
    powers = jnp.exp(logits - jnp.max(logits, axis=0, keepdims=True))
    wb[...] = powers / jnp.sum(powers, axis=0, keepdims=True)
    depth = inside(lane % NZ, NZ)
    first = lax.axis_index("gy") * (tiles * L // NZ)

    at = lax.axis_index("gx") * rows + lax.broadcasted_iota(jnp.int32, (rows, K, L), 0)
    across[...] = 1.0 / inside(at, lax.axis_size("gx") * rows)
    mass[...] = jnp.zeros((K, L), F32)
    for t in range(tiles):
        along = inside(first + t * (L // NZ) + lane // NZ, lax.axis_size("gy") * (tiles * L // NZ))
        around = 1.0 / (along * depth)
        loads[t].wait()

        def some(c, acc):
            for i in range(8):
                x = c * 8 + i
                d = jnp.exp(turn[t, pl.ds(x, K, stride=rows), :])
                dens[x, t] = d
                e[x, t] = d * (around * across[x])
                acc = acc + d
            return acc

        mass[...] += lax.fori_loop(0, rows // 8, some, jnp.zeros((K, L), F32))
        pltpu.make_async_copy(dens.at[:, t], dens_out.at[:, t], sem.at[tiles]).start()
    give_edges(e, edges)
    pltpu.make_async_copy(dens, dens_out, sem.at[tiles]).wait()


def first_fields(inner, wb, w_ref, dens, src, tmp, v, inv_a, tmp2, u, inv_s, load):
    rows, tiles = dens.shape[0], dens.shape[1]
    first, outs, again, last = parts(tiles, inner)
    conv_xz(src, tmp, w_ref, first)

    def ring(c, carry):
        s = pl.ds(c * 8, 8)
        for start, end in outs:
            spread = jnp.log(conv_y(tmp, c * 8, 8, start, end - start))
            log_q = jnp.sum(wb[...] * spread, axis=2, keepdims=True)
            v[s, start:end] = jnp.exp(log_q - spread)
            inv_a[s, start:end] = jnp.exp(-spread)
        return carry

    lax.fori_loop(0, (rows + 8) // 8, ring, 0)
    clear_outside((v, inv_a), outs, not inner)
    conv_xz(v, tmp2, w_ref, again)
    load.wait()

    def second(c, carry):
        s = pl.ds(c * 8, 8)
        for start, end in last:
            inv = 1.0 / conv_y(tmp2, c * 8, 8, start, end - start)
            inv_s[s, start:end] = inv
            u[s, start:end] = dens[s, start:end] * inv
        return carry

    lax.fori_loop(0, rows // 8, second, 0)


def first_inner(w_ref, wb, own, xb, xa, dens_far, tmp, v, inv_a, tmp2, u, inv_s, big, dens, sem):
    load = pltpu.make_async_copy(dens_far, dens, sem.at[0])
    load.start()
    join_rows(big, own, xa, xb)
    first_fields(True, wb, w_ref, dens, big, tmp, v, inv_a, tmp2, u, inv_s, load)


def first_outer(w_ref, wb, cot, e, yb, ya, ca, da, db, *rest):
    dens_far, fields, mean, edges, (ends, dens, sem) = rest[6], rest[7:13], rest[13], rest[14:20], rest[20:]
    rows, tiles = dens.shape[0], dens.shape[1]
    load = pltpu.make_async_copy(dens_far, dens, sem.at[0])
    load.start()
    mean[...] = jnp.broadcast_to(centre(e), (K, L))
    join_ends(ends, rows, HALO, ya, yb, ca, da, db)
    first_fields(False, wb, w_ref, dens, ends, *fields, load)
    give_edges(fields[4], edges)
    xa, xb, ya, yb, da, db = edges
    px, py = parities()
    row_a = pl.ds(pl.multiple_of((1 - px) * (rows - 8), 8), 8)
    row_b = pl.ds(pl.multiple_of(px * (rows - 8), 8), 8)
    for t in range(tiles):
        xa[HALO, t] = cot[row_a, t * L : (t + 1) * L]
        xb[HALO, t] = cot[row_b, t * L : (t + 1) * L]
    for out, side in ((ya, 1 - py), (yb, py)):
        for t in range(HT):
            lanes = pl.ds(pl.multiple_of((side * (tiles - HT) + t) * L, L), L)
            for b in range(rows // 8):
                out[rows + b, t] = cot[b * 8 : b * 8 + 8, lanes]
    for t in range(HT):
        lanes = pl.ds(pl.multiple_of((py * (tiles - HT) + t) * L, L), L)
        da[HALO, t] = cot[row_a, lanes]
        db[HALO, t] = cot[row_b, lanes]


def second_fields(inner, wb, w_ref, mean, cots, own, inv_s, src, tmp, r, tmp2, bu, z, q, sums):
    rows, tiles = own.shape[0], own.shape[1]
    first, outs, again, last = parts(tiles, inner)
    conv_xz(src, tmp, w_ref, first)

    def ring(x, count, mine):
        acc_k = jnp.zeros((K, L), F32)
        acc_s = jnp.zeros((1, L), F32)
        for start, end in outs:
            spread = jnp.log(conv_y(tmp, x, count, start, end - start))
            log_q = jnp.sum(wb[...] * spread, axis=2, keepdims=True)
            ratio = wb[...] * jnp.exp(log_q - spread)
            for i in range(count):
                for t in range(start, end):
                    cell = cots[t + 2, pl.ds(x + i + 4, 1), :]
                    r[x + i, t] = ratio[i, t - start] * cell
                    if mine and 2 <= t < tiles + 2:
                        row_q = jnp.exp(log_q[i, t - start])
                        q[t - 2, pl.ds(x + i - 4, 1), :] = row_q[0:1]
                        combined = cell * row_q[0:1]
                        acc_s = acc_s + combined
                        acc_k = acc_k + combined * (spread[i, t - start] - mean)
        if mine:
            sums[0] += acc_k
            sums[1, 0:1] += acc_s

    ring(0, 4, False)
    ring(rows + 4, 4, False)

    def middle(c, carry):
        ring(c * 8 + 4, 8, True)
        return carry

    lax.fori_loop(0, rows // 8, middle, 0)
    clear_outside((r,), outs, not inner)
    conv_xz(r, tmp2, w_ref, again)

    def second(c, carry):
        s = pl.ds(c * 8, 8)
        for start, end in last:
            back = own[s, start:end] * conv_y(tmp2, c * 8, 8, start, end - start)
            bu[s, start:end] = back
            z[s, start:end] = back * inv_s[s, start:end]
        return carry

    lax.fori_loop(0, rows // 8, second, 0)


def second_inner(w_ref, wb, cot, inv_s, own, xb, xa, tmp, r, tmp2, bu, z, q, sums, big, cots):
    rows, tiles = own.shape[0], own.shape[1]
    join_rows(big, own, xa, xb)
    (row_a, row_b), _ = sides(rows, tiles)
    for t in range(tiles):
        cots[HT + t, HALO : HALO + rows] = cot[:, t * L : (t + 1) * L]
        cots[HT + t, pl.ds(pl.multiple_of(row_a, 8), 8)] = xa[HALO, t]
        cots[HT + t, pl.ds(pl.multiple_of(row_b, 8), 8)] = xb[HALO, t]
    sums[...] = jnp.zeros_like(sums)
    second_fields(True, wb, w_ref, centre(own), cots, own, inv_s, big, tmp, r, tmp2, bu, z, q, sums)


def second_outer(w_ref, wb, mass, cot, inv_s, own, xb, xa, yb, ya, ca, da, db, *rest):
    tmp, r, tmp2, bu, z, q, sums = rest[7:14]
    told, edges, (ends, cots) = rest[14], rest[15:21], rest[21:]
    rows, tiles = own.shape[0], own.shape[1]
    slabs = xa.shape[0]
    join_ends(ends, rows, slabs, ya, yb, ca, da, db)
    (row_a, row_b), (col_a, col_b) = sides(rows, tiles)
    row_a, row_b = pl.ds(pl.multiple_of(row_a, 8), 8), pl.ds(pl.multiple_of(row_b, 8), 8)
    for t in (0, 1, tiles - 2, tiles - 1):
        cots[HT + t, HALO : HALO + rows] = cot[:, t * L : (t + 1) * L]
        cots[HT + t, row_a] = xa[HALO, t]
        cots[HT + t, row_b] = xb[HALO, t]
    for t in range(HT):
        for b in range(rows // 8):
            some_rows = pl.ds(HALO + b * 8, 8)
            cots[col_a + t, some_rows] = ya[rows + b, t]
            cots[col_b + t, some_rows] = yb[rows + b, t]
        cots[col_a + t, row_b] = ca[HALO, t]
        cots[col_a + t, row_a] = ca[slabs + HALO, t]
        cots[col_b + t, row_a] = da[HALO, t]
        cots[col_b + t, row_b] = db[HALO, t]
    mean = centre(own)
    second_fields(False, wb, w_ref, mean, cots, own, inv_s, ends, tmp, r, tmp2, bu, z, q, sums)
    told[...] = in_lanes(over_lanes(mass[...]), over_lanes(sums[0]), over_lanes(sums[1, 0:1]), mean)
    give_edges(z, edges)


def third_fields(inner, wb, w_ref, mean, inv_a, v, e, bu, src, tmp, r, tmp2, gp, sums):
    rows, tiles = e.shape[0], e.shape[1]
    first, outs, again, last = parts(tiles, inner)
    conv_xz(src, tmp, w_ref, first)

    def ring(x, count, mine):
        s = pl.ds(x, count)
        for start, end in outs:
            back_v = -(v[s, start:end] * conv_y(tmp, x, count, start, end - start))
            combined = jnp.sum(back_v, axis=2, keepdims=True)
            inv = inv_a[s, start:end]
            r[s, start:end] = (wb[...] * combined - back_v) * inv
            if mine:
                low, high = max(start, 2) - start, min(end, tiles + 2) - start
                part = combined[:, low:high]
                sums[0] += jnp.sum(part * (-jnp.log(inv[:, low:high]) - mean), axis=(0, 1))
                sums[1, 0:1] += jnp.sum(part, axis=(0, 1))

    ring(0, 4, False)
    ring(rows + 4, 4, False)

    def middle(c, carry):
        ring(c * 8 + 4, 8, True)
        return carry

    lax.fori_loop(0, rows // 8, middle, 0)
    conv_xz(r, tmp2, w_ref, again)

    def second(c, carry):
        s = pl.ds(c * 8, 8)
        for start, end in last:
            gp[s, start:end] = bu[s, start:end] + e[s, start:end] * conv_y(tmp2, c * 8, 8, start, end - start)
        return carry

    lax.fori_loop(0, rows // 8, second, 0)


def third_inner(w_ref, wb, mean, inv_a, v, e, bu, own, xb, xa, tmp, r, tmp2, gp, sums, big):
    join_rows(big, own, xa, xb)
    sums[...] = jnp.zeros_like(sums)
    third_fields(True, wb, w_ref, mean[...], inv_a, v, e, bu, big, tmp, r, tmp2, gp, sums)


def third_outer(w_ref, wb, mean, before, inv_a, v, e, bu, q, yb, ya, ca, da, db, *rest):
    tmp, r, tmp2, gp, sums = rest[5:10]
    gp_out, q_out, told, ends, sem = rest[10:]
    rows, tiles = e.shape[0], e.shape[1]
    middle = pl.ds(HT, tiles - 2 * HT)
    copies = [pltpu.make_async_copy(q, q_out, sem.at[0]), pltpu.make_async_copy(gp.at[:, middle], gp_out.at[:, middle], sem.at[1])]
    for c in copies:
        c.start()
    join_ends(ends, rows, HALO, ya, yb, ca, da, db)
    third_fields(False, wb, w_ref, mean[...], inv_a, v, e, bu, ends, tmp, r, tmp2, gp, sums)
    for i, first in enumerate((0, tiles - HT)):
        lanes = pl.ds(first, HT)
        copies.append(pltpu.make_async_copy(gp.at[:, lanes], gp_out.at[:, lanes], sem.at[i + 2]))
        copies[-1].start()
    early = before[...]
    told[...] = in_lanes(
        *[early[:, i : i + 1] for i in range(4)], over_lanes(sums[0]), over_lanes(sums[1, 0:1]), mean[:, 0:1]
    )
    for c in copies:
        c.wait()


def last_kernel(cells, wb, heard, q_far, gp_far, dens_far, out, bary, theta_out, turn, gp, dens, q, sem):
    rows, tiles = gp.shape[0], gp.shape[1]
    loads = []
    for i, first in enumerate(range(0, tiles, 4)):
        lanes = pl.ds(first, 4)
        for j, (src, dst) in enumerate(((gp_far, gp), (dens_far, dens))):
            loads.append(pltpu.make_async_copy(src.at[:, lanes], dst.at[:, lanes], sem.at[tiles + 2 * i + j]))
            loads[-1].start()
    loads.append(pltpu.make_async_copy(q_far, q, sem.at[tiles + tiles // 2]))
    loads[-1].start()
    weights = wb[:, 0:1]
    everyone = heard[...]
    total = jnp.sum(everyone, axis=0)
    mass, late = total[:, 0:1], total[:, 2:3]
    shift_k = jnp.log(F32(cells)) - jnp.log(mass)
    shift = jnp.sum(weights * shift_k, axis=0, keepdims=True)
    scale = jnp.exp(shift)
    last = weights * (scale * late)
    grad_sums = last + (last - weights * jnp.sum(last, axis=0, keepdims=True))
    coef = jnp.broadcast_to(grad_sums / mass, (K, L))
    scale_all = jnp.broadcast_to(scale, (K, L))
    copies = []
    for t in range(tiles):

        def rows_of(c, carry):
            for i in range(8):
                x = c * 8 + i
                turn[t, pl.ds(x, K, stride=rows), :] = gp[x, t] * scale_all - dens[x, t] * coef
            return carry

        if t % 4 == 0:
            loads[t // 2].wait()
            loads[t // 2 + 1].wait()
        if t == 0:
            loads[-1].wait()
        lax.fori_loop(0, rows // 8, rows_of, 0)
        copies.append(pltpu.make_async_copy(turn.at[t], out.at[:, pl.ds(t * L, L)], sem.at[t]))
        copies[-1].start()
        bary[:, t * L : (t + 1) * L] = q[t] * scale
    offsets = in_lanes(0.0, 0.0, 0.0, 2.0 * shift_k - shift, 0.0, 0.0, shift_k)
    turned = pltpu.roll(everyone.reshape(-1, L), 1, axis=1).reshape(everyone.shape)
    back = jnp.sum((everyone + offsets) * turned, axis=0)
    weight_grad = scale * (total[:, 1:2] + back[:, 3:4] + total[:, 4:5] + back[:, 6:7])
    grad = weights * (weight_grad - jnp.sum(weights * weight_grad, axis=0, keepdims=True))
    for k in range(K):
        theta_out[k] = grad[k, 0]
    for c in copies:
        c.wait()


def call(kernel, outs, scratch, semaphores, args, near_out=(), far_in=0, same=None, numbers=()):
    vmem, far = pl.BlockSpec(memory_space=pltpu.VMEM), pl.BlockSpec(memory_space=pl.ANY)
    near = len(args) - far_in
    args = [pltpu.with_memory_space_constraint(a, pltpu.VMEM if i < near else pltpu.HBM) for i, a in enumerate(args)]
    return pl.pallas_call(
        kernel,
        out_shape=outs,
        in_specs=[pl.BlockSpec(memory_space=pltpu.SMEM)] * len(numbers) + [vmem] * near + [far] * far_in,
        out_specs=[far if i in near_out else vmem if len(o.shape) > 1 else pl.BlockSpec(memory_space=pltpu.SMEM) for i, o in enumerate(outs)],
        scratch_shapes=[pltpu.VMEM(s, F32) for s in scratch] + [pltpu.SemaphoreType.DMA((n,)) for n in semaphores],
        input_output_aliases=same or {},
        compiler_params=pltpu.CompilerParams(vmem_limit_bytes=VMEM),
    )(*numbers, *args)


def partners(axis, parity):
    count = lax.axis_size(axis)
    found = {}
    for i in range(count):
        j = i + 1 if i % 2 == parity else i - 1
        if 0 <= j < count:
            found[i] = j
    return found


def swap(value, axis, parity):
    return lax.ppermute(value, axis, list(partners(axis, parity).items()))


def swap_diagonal(value, parity_x, parity_y):
    along_x, along_y, width = partners("gx", parity_x), partners("gy", parity_y), lax.axis_size("gy")
    pairs = [(i * width + j, k * width + m) for i, k in along_x.items() for j, m in along_y.items()]
    return lax.ppermute(value, ("gx", "gy"), pairs)


def exchange(xa, xb, ya, yb, da, db, tiles):
    rxb, ryb = swap(xb, "gx", 1), swap(yb, "gy", 1)
    rdb, rda = swap_diagonal(db, 1, 1), swap_diagonal(da, 0, 1)
    rxa, rya = swap(xa, "gx", 0), swap(ya, "gy", 0)
    rxb, rxa, rdb, rda = lax.optimization_barrier((rxb, rxa, rdb, rda))
    first = (1 - lax.rem(lax.axis_index("gy"), 2)) * (tiles - HT)
    corner = jnp.concatenate([lax.dynamic_slice_in_dim(r, first, HT, axis=1) for r in (rxb, rxa)], axis=0)
    rca = swap(corner, "gy", 0)
    return rxa, rxb, ryb, rya, rca, rda, rdb


def over_all(told):
    devices = lax.axis_size("gx") * lax.axis_size("gy")
    return lax.all_to_all(jnp.broadcast_to(told[None], (devices, K, L)), ("gx", "gy"), 0, 0, tiled=True)


def shards(log_dens, theta, cotangent):
    _, rows, merged = log_dens.shape
    tiles = merged // L
    cells = lax.axis_size("gx") * lax.axis_size("gy") * rows * merged
    w = jnp.asarray(depth_weights())

    field, ringed, big = (rows, tiles, K, L), (rows + 8, tiles + 4, K, L), (rows + 16, tiles, K, L)
    tmp, tmp2, ends = (rows + 8, tiles + 8, K, L), (rows, tiles + 4, K, L), (rows + 16, 2 * HT, K, L)
    acc, turn, small, cots, q_shape = (2, K, L), (tiles, K * rows, L), (K, L), (tiles + 8, rows + 16, L), (tiles, rows, L)

    def near(*shapes):
        return [pltpu.VMEM(s, F32) for s in shapes]

    def edges(more, more_y):
        return near(*[(HALO + more, tiles, K, L)] * 2, *[(rows + more_y, HT, K, L)] * 2, *[(HALO + more, HT, K, L)] * 2)

    logs = log_dens.reshape(K * rows, merged)
    dens, e, mass, wb, *sent = call(
        start_kernel, [pltpu.HBM(field, F32)] + near(field, small, small) + edges(0, 0), [turn, (rows, K, L), field], [tiles + 1],
        [logs], (0,), 1, numbers=(theta,),
    )
    xa, xb, *others = exchange(*sent, tiles)
    held = [tmp, ringed, ringed, tmp2, field, field]
    held_now = call(first_inner, near(*held), [big, field], [1], [w, wb, e, xb, xa, dens], far_in=1)
    _, v, inv_a, _, u, inv_s, mean, *sent = call(
        first_outer, near(*held, small) + edges(1, rows // 8), [ends, field], [1],
        [w, wb, cotangent, e, *others, *held_now, dens], far_in=1, same={9 + i: i for i in range(6)},
    )
    xa, xb, *others = exchange(*sent, tiles)
    held = [tmp, ringed, tmp2, field, field, q_shape, acc]
    held_now = call(second_inner, near(*held), [big, cots], [], [w, wb, cotangent, inv_s, u, xb, xa])
    _, _, _, bu, z, q, _, told, *sent = call(
        second_outer, near(*held, small) + edges(0, 0), [ends, cots], [],
        [w, wb, mass, cotangent, inv_s, u, xb, xa, *others, *held_now], same={13 + i: i for i in range(7)},
    )
    xa, xb, *others = exchange(*sent, tiles)
    held = [tmp, ringed, tmp2, field, acc]
    held_now = call(third_inner, near(*held), [big], [], [w, wb, mean, inv_a, v, e, bu, z, xb, xa])
    *_, gp_far, q_far, told = call(
        third_outer, near(*held) + [pltpu.HBM(field, F32), pltpu.HBM(q_shape, F32)] + near(small), [ends], [4],
        [w, wb, mean, told, inv_a, v, e, bu, q, *others, *held_now], (5, 6), same={14 + i: i for i in range(5)},
    )
    plain = [jax.ShapeDtypeStruct(s, F32) for s in ((K * rows, merged), (rows, merged), (K,))]
    grad, bary, grad_theta = call(
        functools.partial(last_kernel, cells), plain, [turn, field, field, q_shape], [tiles + tiles // 2 + 1],
        [wb, over_all(told), q_far, gp_far, dens], (0,), 3,
    )
    return bary, grad.reshape(K, rows, merged), grad_theta


def solution(mesh):
    placed = (P(None, "gx", "gy"), P(), P("gx", "gy"))
    return jax.shard_map(
        shards,
        mesh=mesh,
        in_specs=placed,
        out_specs=(P("gx", "gy"), P(None, "gx", "gy"), P()),
        check_vma=False,
    )
```
